256 devices in a mesh: lon: 16 (over z_lo, x, core), lat: 16 (over y, z_hi).
Axes of the slice: x: 4, y: 4, z: 8 (z_hi: 4, z_lo: 2; z = z_hi * 2 + z_lo), core: 2. Of those that a mesh axis runs over, the one named last changes fastest.
Arguments:
- tracer: float32 [64, 256, 2048], P(None, 'lat', 'lon'), may hold values from -6 to 6
- east_vel: float32 [64, 256, 2048], P(None, 'lat', 'lon'), may hold values from -18 to 18, as said below
- north_vel: float32 [64, 256, 2048], P(None, 'lat', 'lon'), may hold values from -18 to 18, as said below
- viscosity: float32 [64, 256, 2048], P(None, 'lat', 'lon'), may hold values from 0.2 to 1
- land_sea: int32 [64, 256, 2048], P(None, 'lat', 'lon'), may hold values 0 or 1
- thickness: float32 [64], replicated, may hold values from 0.5 to 2
- surface: float32 [256, 2048], P('lat', 'lon'), may hold values from -6 to 6
- surface_diag: float32 [256, 2048], P('lat', 'lon'), may hold values from 0.1 to 2
- precond_kernel: float32 [5, 5], replicated, may hold values from -0.06 to 2, as said below
Outputs:
- tracer_new: float32 [64, 256, 2048], P(None, 'lat', 'lon')
- east_new: float32 [64, 256, 2048], P(None, 'lat', 'lon')
- north_new: float32 [64, 256, 2048], P(None, 'lat', 'lon')
- surface_new: float32 [256, 2048], P('lat', 'lon')
The draws below stay inside these ranges and needn't reach their ends.
Inputs may be any that keep to these rules, and one draw needn't show every extreme that they name: `east_vel`: real-valued; magnitudes differ between latitudes and between longitudes. `north_vel`: real-valued; magnitudes differ between latitudes and between longitudes. `precond_kernel`: point symmetric: entry [a, b] equals entry [4 - a, 4 - b]; the centre entry exceeds the sum of the magnitudes of all other entries.
All inputs are finite; a program needn't handle non-finite values. No bound on the sum of `land_sea` on one device may be relied on, other than what follows from the above.
Results may differ from the reference program's by a relative error of at most 0.00017.
Values sent between devices are 32-bit elements; how exact they have to be, the bound alone decides.
No kernel may reach another device: no remote copies, remote signals or barrier semaphores. Data moves between devices by JAX's collectives and lax.ppermute only.
A program may use at most 64 MiB of HBM per device.

```python
import math
import jax
import jax.numpy as jnp
from jax import lax

NZ = 64
ITERS = 3
NX = 2048
NY = 256


def place_scales(key):
    lat_key, lon_key = jax.random.split(key)
    lat_scale = jnp.exp(jax.random.uniform(lat_key, (1, NY, 1), jnp.float32, 0.0, jnp.log(10.0)))
    lon_scale = jnp.exp(jax.random.uniform(lon_key, (1, 1, NX), jnp.float32, 0.0, jnp.log(10.0)))
    return 0.3 * jnp.sqrt(lat_scale * lon_scale)


def draw_east_vel(key, part):
    key = jax.random.fold_in(key, 11)
    base_key, scale_key = jax.random.split(key)
    base = jax.random.truncated_normal(base_key, -6.0, 6.0, (NZ, NY, NX), jnp.float32)
    return base * place_scales(scale_key)


def draw_north_vel(key, part):
    key = jax.random.fold_in(key, 12)
    base_key, scale_key = jax.random.split(key)
    base = jax.random.truncated_normal(base_key, -6.0, 6.0, (NZ, NY, NX), jnp.float32)
    return base * place_scales(scale_key)


def draw_precond_kernel(key, part):
    key = jax.random.fold_in(key, 13)
    taps_key, centre_key = jax.random.split(key)
    raw_taps = jax.random.uniform(taps_key, (5, 5), jnp.float32, -0.06, 0.06)
    symmetric = 0.5 * (raw_taps + raw_taps[::-1, ::-1])
    centre = jax.random.uniform(centre_key, (), jnp.float32, 1.5, 2.0)
    return symmetric.at[2, 2].set(centre)


def set_ends(array, stream_key, low, largest):
    extent = array.shape
    spot = [jax.random.randint(jax.random.fold_in(stream_key, axis), (), 0, extent[axis]) for axis in range(len(extent))]
    array = array.at[tuple(spot)].set(low)
    longest = extent.index(max(extent))
    spot[longest] = (spot[longest] + 1) % extent[longest]
    return array.at[tuple(spot)].set(largest)


def levels(stream_key, extent, shards, least, high):
    gain = 1.0
    for dim, parts in shards:
        heights = jax.random.uniform(jax.random.fold_in(jax.random.fold_in(stream_key, 6), dim), (parts,), jnp.float32, least / len(shards), high / len(shards))
        gain = gain * jnp.repeat(jnp.exp(heights), extent[dim] // parts).reshape((-1,) + (1,) * (len(extent) - 1 - dim))
    return gain


def bell_draw(own_key, shape, spread, bound, shards=(), held_as=jnp.bfloat16):
    values = jax.random.normal(own_key, shape, jnp.float32) * spread
    if len(shards) > 0:
        values = levels(own_key, shape, shards, -0.22, 0.18) * values
    return jnp.clip(values, min=-bound, max=bound).astype(held_as)


def setup_inputs(seed: int = 0) -> dict:
    key_list = jax.random.split(jax.random.key(seed), 10)
    tracer = bell_draw(key_list[0], (NZ, NY, NX), 1.0, 6.0, ((1, 16), (2, 16)), jnp.float32)
    east_vel = draw_east_vel(jax.random.fold_in(key_list[9], 71), 0)
    north_vel = draw_north_vel(jax.random.fold_in(key_list[9], 71), 0)
    viscosity = jnp.clip(jnp.exp(math.log(1.0) - 1.609438 * jax.random.uniform(key_list[3], (NZ, NY, NX), jnp.float32) ** levels(key_list[3], (NZ, NY, NX), ((1, 16), (2, 16)), -0.2, 0.2)), 0.2, 1.0)
    land_sea = set_ends((jax.random.randint(key_list[4], (NZ, NY, NX), 0, 10) < 9).astype(jnp.int32), jax.random.fold_in(key_list[4], 1), 0, 1)
    thickness = jnp.clip(jnp.exp(jax.random.uniform(key_list[5], (NZ,), jnp.float32, math.log(0.5), math.log(2.0))), 0.5, 2.0)
    surface = bell_draw(key_list[6], (NY, NX), 1.0, 6.0, ((0, 16), (1, 16)), jnp.float32)
    surface_diag = jnp.clip(jnp.exp(math.log(2.0) - 2.9957323 * jax.random.uniform(key_list[7], (NY, NX), jnp.float32) ** levels(key_list[7], (NY, NX), ((0, 16), (1, 16)), -0.2, 0.2)), 0.1, 2.0)
    precond_kernel = draw_precond_kernel(jax.random.fold_in(key_list[9], 71), 0)
    return {"tracer": tracer, "east_vel": east_vel, "north_vel": north_vel, "viscosity": viscosity, "land_sea": land_sea, "thickness": thickness, "surface": surface, "surface_diag": surface_diag, "precond_kernel": precond_kernel}


DT_ADV = 0.25
DT_VISC = 0.2
TAU = 0.05


def east(values, offset=1):
    return jnp.roll(values, -offset, axis=-1)


def west(values):
    return jnp.roll(values, 1, axis=-1)


def lat_shift(values, offset):
    if offset == 0:
        return values
    zeros = jnp.zeros(values.shape[:-2] + (abs(offset),) + values.shape[-1:], values.dtype)
    if offset > 0:
        return jnp.concatenate([values[..., offset:, :], zeros], axis=-2)
    return jnp.concatenate([zeros, values[..., :offset, :]], axis=-2)


def level_step(items):
    tracer, east_vel, north_vel, viscosity, land_sea = items
    wet_cells = land_sea.astype(jnp.float32)
    wet_tracer = tracer * wet_cells
    wet_east = east(wet_cells)
    wet_north = lat_shift(wet_cells, 1)
    flux_east = east_vel * (7.0 * (wet_tracer + east(wet_tracer)) - (west(wet_tracer) + east(wet_tracer, 2))) / 12.0 * wet_cells * wet_east
    flux_north = north_vel * (7.0 * (wet_tracer + lat_shift(wet_tracer, 1)) - (lat_shift(wet_tracer, -1) + lat_shift(wet_tracer, 2))) / 12.0 * wet_cells * wet_north
    tracer_new = wet_cells * (tracer - DT_ADV * (flux_east - west(flux_east) + flux_north - lat_shift(flux_north, -1)))
    face_east = 0.5 * (viscosity + east(viscosity)) * wet_cells * wet_east
    face_north = 0.5 * (viscosity + lat_shift(viscosity, 1)) * wet_cells * wet_north

    def diffuse(source):
        grad_east = face_east * (east(source) - source)
        grad_north = face_north * (lat_shift(source, 1) - source)
        return wet_cells * (source + DT_VISC * (grad_east - west(grad_east) + grad_north - lat_shift(grad_north, -1)))

    return tracer_new, diffuse(east_vel), diffuse(north_vel)


def reference(tracer, east_vel, north_vel, viscosity, land_sea, thickness, surface, surface_diag, precond_kernel):
    tracer_new, east_new, north_new = lax.map(level_step, (tracer, east_vel, north_vel, viscosity, land_sea))
    east_transport = jnp.sum(thickness[:, None, None] * east_new, axis=0)
    north_transport = jnp.sum(thickness[:, None, None] * north_new, axis=0)
    right_side = surface - TAU * (east_transport - west(east_transport) + north_transport - lat_shift(north_transport, -1))

    def operate(source):
        return (4.0 + surface_diag) * source - (east(source) + west(source) + lat_shift(source, 1) + lat_shift(source, -1))

    def precondition(source):
        summed = jnp.zeros_like(source)
        for lat_off in range(-2, 3):
            moved = lat_shift(source, lat_off)
            for lon_off in range(-2, 3):
                summed = summed + precond_kernel[lat_off + 2, lon_off + 2] * east(moved, lon_off)
        return summed

    iterate = surface
    residual = right_side - operate(iterate)
    smoothed = precondition(residual)
    direction = smoothed
    norm_now = jnp.sum(residual * smoothed)
    for iteration in range(ITERS):
        image = operate(direction)
        step_size = norm_now / jnp.sum(direction * image)
        iterate = iterate + step_size * direction
        residual = residual - step_size * image
        if iteration + 1 < ITERS:
            smoothed = precondition(residual)
            norm_next = jnp.sum(residual * smoothed)
            direction = smoothed + (norm_next / norm_now) * direction
            norm_now = norm_next
    return tracer_new, east_new, north_new, iterate
```

```python
import jax
import jax.numpy as jnp
from jax import lax
from jax.experimental import pallas as pl
from jax.experimental.pallas import tpu as pltpu
from jax.sharding import Mesh
from jax.sharding import PartitionSpec as P

DT_ADV = 0.25
DT_VISC = 0.2
TAU = 0.05
SHIFTS = (0.3, 1.3)

LON = ("zl", "x", "c")
LAT = ("y", "zh")
NZ, NR, NC = 64, 16, 128
SWAP_A = [(i, i ^ 1) for i in range(16)]
SWAP_B = [(i, (i + 1) % 16 if i % 2 else (i - 1) % 16) for i in range(16)]

VM = pl.BlockSpec(memory_space=pltpu.VMEM)
SM = pl.BlockSpec(memory_space=pltpu.SMEM)


def call(kernel, outs, specs, flops, nbytes, scratch=()):
    return pl.pallas_call(
        kernel,
        out_shape=[jax.ShapeDtypeStruct(s, jnp.float32) for s in outs],
        in_specs=specs,
        out_specs=[VM] * len(outs),
        scratch_shapes=list(scratch),
        compiler_params=pltpu.CompilerParams(vmem_limit_bytes=32 * 1024 * 1024),
        cost_estimate=pl.CostEstimate(flops=flops, bytes_accessed=nbytes, transcendentals=0),
    )


def lane_of(shape):
    return lax.broadcasted_iota(jnp.int32, shape, len(shape) - 1)


def row_of(shape):
    return lax.broadcasted_iota(jnp.int32, shape, len(shape) - 2)


def even_lon():
    return lax.axis_index("c") == 0


def even_lat():
    return lax.axis_index("zh") % 2 == 0


def lat_index():
    return lax.axis_index("y") * 4 + lax.axis_index("zh")


def b_exists():
    lat = lat_index()
    return jnp.where(jnp.logical_or(lat == 0, lat == 15), 0.0, 1.0).astype(jnp.float32)


def pack_kernel(t, u, v, vi, land, sf, dg, lon_out, a_out, b_out):
    even = even_lat()

    def edge_rows(north, out):
        def pick(ref, offset):
            high = ref[pl.ds(NR - 1 - offset, NZ, stride=NR), :]
            low = ref[pl.ds(offset, NZ, stride=NR), :]
            return jnp.where(north, high, low)

        wet = pick(land, 0).astype(jnp.float32)
        first = pick(t, 0) * wet
        second = pick(t, 1) * pick(land, 1).astype(jnp.float32)
        out[0] = pick(u, 0)
        out[1] = pick(v, 0)
        out[2] = pick(vi, 0)
        out[3] = wet
        out[4] = first
        out[5] = 7.0 * first - second

    edge_rows(even, a_out)
    edge_rows(jnp.logical_not(even), b_out)
    lane = lane_of((NR, NC))
    half = lane < NC // 2
    pair = lane // 2

    def body(k, acc):
        at = pl.ds(pl.multiple_of(k * NR, NR), NR)
        wet = land[at, :].astype(jnp.float32)
        first = t[at, :] * wet
        inner = jnp.where(half, pltpu.roll(first, NC - 1, 1), pltpu.roll(first, 1, 1))
        values = (u[at, :], v[at, :], vi[at, :], wet, first, 7.0 * first - inner)
        mine = pair == k
        return tuple(
            jnp.where(mine, pltpu.roll(x, 2 * k + 1, 1), old) for x, old in zip(values, acc)
        )

    zero = jnp.zeros((NR, NC), jnp.float32)
    acc = lax.fori_loop(0, NZ, body, (zero,) * 6, unroll=4)
    for i in range(6):
        lon_out[i] = acc[i]
    lon_out[6] = sf[...]
    lon_out[7] = dg[...]


def inner_kernel(thick, u, v, vi, land, out):
    def body(k, acc):
        at = pl.ds(pl.multiple_of(k * NR, NR), NR)
        th = thick[k]
        wet = land[at, :].astype(jnp.float32)
        uu, vv, visc = u[at, :], v[at, :], vi[at, :]
        half = 0.5 * th
        own = wet * th
        east = (visc + pltpu.roll(visc, NC - 1, 1)) * (wet * pltpu.roll(wet, NC - 1, 1)) * half
        north = (visc + pltpu.roll(visc, NR - 1, 0)) * (wet * pltpu.roll(wet, NR - 1, 0)) * half
        return (
            acc[0] + own * uu,
            acc[1] + east * (pltpu.roll(uu, NC - 1, 1) - uu),
            acc[2] + north * (pltpu.roll(uu, NR - 1, 0) - uu),
            acc[3] + own * vv,
            acc[4] + east * (pltpu.roll(vv, NC - 1, 1) - vv),
            acc[5] + north * (pltpu.roll(vv, NR - 1, 0) - vv),
        )

    zero = jnp.zeros((NR, NC), jnp.float32)
    acc = lax.fori_loop(0, NZ, body, (zero,) * 6, unroll=4)
    lane, row = lane_of((NR, NC)), row_of((NR, NC))
    for i in range(2):
        east = jnp.where(lane == NC - 1, 0.0, acc[3 * i + 1])
        north = jnp.where(row == NR - 1, 0.0, acc[3 * i + 2])
        out[i] = acc[3 * i] + DT_VISC * (
            east - pltpu.roll(east, 1, 1) + north - pltpu.roll(north, 1, 0)
        )


def lon_sides(first, second):
    even = even_lon()
    return jnp.where(even, first, second), jnp.where(even, second, first)


def beyond(from_a, from_b):
    east, west = lon_sides(from_a, from_b)
    is_east = lane_of((NR, NC)) % 2 == 0
    return jnp.where(is_east, pltpu.roll(east, NC - 1, 1), pltpu.roll(west, 1, 1))


def face_in(own, other):
    face = 0.5 * (own[2] + other[2]) * (own[3] * other[3])
    return face * (other[0] - own[0]), face * (other[1] - own[1])


def join_kernel(inner, lon, lon_a, lon_b, a, from_a, b, from_b, th_lane, th_row, out):
    lane, row = lane_of((NR, NC)), row_of((NR, NC))
    own = [lon[i] for i in range(4)]
    other = [beyond(lon_a[i], lon_b[i]) for i in range(4)]
    thl = th_lane[...]
    is_east = lane % 2 == 0
    even = even_lat()
    row_a = jnp.where(even, NR - 1, 0)
    row_b = jnp.where(even, 0, NR - 1)
    thr = th_row[...]
    lat_a = face_in([a[i] for i in range(4)], [from_a[i] for i in range(4)])
    lat_b = face_in([b[i] for i in range(4)], [from_b[i] for i in range(4)])
    exists = b_exists()
    for i, grad in enumerate(face_in(own, other)):
        grad = grad * thl
        east = jnp.sum(jnp.where(is_east, grad, 0.0), axis=1, keepdims=True)
        west = jnp.sum(jnp.where(is_east, 0.0, grad), axis=1, keepdims=True)
        add = jnp.where(lane == NC - 1, east, 0.0) + jnp.where(lane == 0, west, 0.0)
        ga = jnp.sum(lat_a[i] * thr, axis=0, keepdims=True)
        gb = jnp.sum(lat_b[i] * thr, axis=0, keepdims=True) * exists
        add = add + jnp.where(row == row_a, ga, 0.0) + jnp.where(row == row_b, gb, 0.0)
        out[i] = inner[i] + DT_VISC * add


def side_kernel(tr, tr_a, tr_b, lon, lon_a, lon_b, rest_out, diag_out, edge_out, a_out, b_out):
    lane = lane_of((NR, NC))

    def widen(own, first, second):
        east, west = lon_sides(first, second)
        return jnp.concatenate([own, jnp.where(lane < NC // 2, east, west)], axis=1)

    te, tn = (widen(tr[i], tr_a[i], tr_b[i]) for i in range(2))
    sf, dg = (widen(lon[i], lon_a[i], lon_b[i]) for i in (6, 7))
    row = row_of((NR, 2 * NC))
    east = lambda x: pltpu.roll(x, 2 * NC - 1, 1)
    west = lambda x: pltpu.roll(x, 1, 1)
    north = lambda x: jnp.where(row == NR - 1, 0.0, pltpu.roll(x, NR - 1, 0))
    south = lambda x: jnp.where(row == 0, 0.0, pltpu.roll(x, 1, 0))
    rest = sf - TAU * (te - west(te) + tn - south(tn))
    rest = rest - ((4.0 + dg) * sf - (east(sf) + west(sf) + north(sf) + south(sf)))
    rest_out[...] = rest
    diag_out[...] = dg
    to_north = TAU * tn[NR - 1 :] + sf[NR - 1 :]
    to_south = sf[:1]
    edge_out[...] = jnp.concatenate([to_north, to_south] + [jnp.zeros((6, 2 * NC), jnp.float32)], axis=0)
    msg_north = jnp.concatenate([rest[7:], dg[10:], to_north], axis=0)
    msg_south = jnp.concatenate([rest[:9], dg[:6], to_south], axis=0)
    even = even_lat()
    a_out[...] = jnp.where(even, msg_north, msg_south)
    b_out[...] = jnp.where(even, msg_south, msg_north)


def solve_kernel(pc, rest, dg, edge, from_a, from_b, v_out, dots_out):
    rows, wide = 3 * NR, 2 * NC
    even = even_lat()
    exists = b_exists()
    msg_a = from_a[...]
    msg_b = from_b[...] * exists
    north = jnp.where(even, msg_a, msg_b)
    south = jnp.where(even, msg_b, msg_a)
    zeros = lambda n: jnp.zeros((n, wide), jnp.float32)
    res = jnp.concatenate([zeros(7), south[:9], rest[...], north[:9], zeros(7)], axis=0)
    diag = 4.0 + jnp.concatenate([zeros(10), south[9:15], dg[...], north[9:15], zeros(10)], axis=0)
    row = row_of((rows, wide))
    lat = lat_index()
    low = jnp.where(lat == 0, NR, 0)
    high = jnp.where(lat == 15, 2 * NR, 3 * NR)
    inside = jnp.where(jnp.logical_and(row >= low, row < high), 1.0, 0.0).astype(jnp.float32)
    res = res + jnp.where(row == NR, south[15:], 0.0) + jnp.where(row == NR - 1, edge[1:2], 0.0)
    res = res + jnp.where(row == 2 * NR - 1, north[15:], 0.0) + jnp.where(row == 2 * NR, edge[0:1], 0.0)
    res = res * inside

    def lon_shift(x, n):
        return x if n == 0 else pltpu.roll(x, (-n) % wide, 1)

    def lat_shift(x, n):
        return x if n == 0 else pltpu.roll(x, (-n) % rows, 0)

    def operate(x):
        near = lon_shift(x, 1) + lon_shift(x, -1) + lat_shift(x, 1) + lat_shift(x, -1)
        return diag * x - near

    def precondition(x):
        moved = [lon_shift(x, b) for b in range(-2, 3)]
        total = None
        for a in range(-2, 3):
            line = pc[a + 2, 0] * moved[0]
            for b in range(1, 5):
                line = line + pc[a + 2, b] * moved[b]
            line = lat_shift(line, a)
            total = line if total is None else total + line
        return total * inside

    scale = 1.0 / (5.0 * jnp.full((1, wide), pc[2, 2], jnp.float32))
    p = [res]
    v, av = [], []
    for j in range(3):
        v.append(precondition(p[j]))
        av.append(operate(v[j]))
        if j < 2:
            p.append((av[j] * scale - SHIFTS[j] * p[j]) * inside)
    mine = lambda x: x[NR : 2 * NR, :NC]
    v = [mine(x) for x in v]
    av = [mine(x) for x in av]
    r = mine(res)
    for j in range(3):
        v_out[j] = v[j]
    pairs = [(v[0], av[0]), (v[0], av[1]), (v[0], av[2]), (v[1], av[1]), (v[1], av[2])]
    pairs += [(v[2], av[2]), (v[0], r), (v[1], r), (v[2], r)]
    lines = []
    for x, y in pairs:
        line = jnp.sum(x * y, axis=0, keepdims=True)
        lines.append(line + pltpu.roll(line, NC // 2, 1))
    left = lane_of((1, NC)) < NC // 2
    lines.append(lines[-1])
    out = [jnp.where(left, lines[2 * i], lines[2 * i + 1]) for i in range(5)]
    dots_out[...] = jnp.concatenate(out + [jnp.zeros((3, NC), jnp.float32)], axis=0)


def step_kernel(dots, v, sf, out):
    d = dots[...]
    left = lane_of((8, NC)) < NC // 2
    first = jnp.sum(jnp.where(left, d, 0.0), axis=1, keepdims=True)
    second = jnp.sum(jnp.where(left, 0.0, d), axis=1, keepdims=True)
    h = []
    for i in range(5):
        h += [first[i : i + 1], second[i : i + 1]]
    h00, h01, h02, h11, h12, h22, g0, g1, g2 = h[:9]
    l1 = h01 / h00
    l2 = h02 / h00
    d1 = h11 - l1 * h01
    e12 = h12 - l1 * h02
    l3 = e12 / d1
    d2 = h22 - l2 * h02 - l3 * e12
    y1 = g1 - l1 * g0
    y2 = g2 - l2 * g0 - l3 * y1
    c2 = y2 / d2
    c1 = y1 / d1 - l3 * c2
    c0 = g0 / h00 - l1 * c1 - l2 * c2
    out[...] = sf[...] + c0 * v[0] + c1 * v[1] + c2 * v[2]


def field_kernel(
    t, u, v, vi, land, lon, lon_a, lon_b, a, from_a, b, from_b, t_out, u_out, v_out, packed, lines
):
    lane, row = lane_of((NR, NC)), row_of((NR, NC))
    is_east = lane % 2 == 0
    own = [lon[i] for i in range(6)]
    other = [beyond(lon_a[i], lon_b[i]) for i in range(6)]
    grad_u, grad_v = face_in(own, other)
    packed[0] = other[4]
    packed[1] = (
        jnp.where(is_east, own[0], other[0]) * (own[5] + other[5]) / 12.0 * (own[3] * other[3])
    )
    packed[2] = jnp.where(is_east, grad_u, -grad_u)
    packed[3] = jnp.where(is_east, grad_v, -grad_v)
    even = even_lat()
    exists = b_exists()
    for side in range(2):
        use_a = even if side == 0 else jnp.logical_not(even)
        here = [jnp.where(use_a, a[i], b[i]) for i in range(6)]
        there = [jnp.where(use_a, from_a[i], from_b[i] * exists) for i in range(6)]
        grad_u, grad_v = face_in(here, there)
        speed = here[1] if side == 0 else there[1]
        lines[4 * side] = there[4]
        lines[4 * side + 1] = speed * (here[5] + there[5]) / 12.0 * (here[3] * there[3])
        lines[4 * side + 2] = grad_u if side == 0 else -grad_u
        lines[4 * side + 3] = grad_v if side == 0 else -grad_v

    at_east, at_west = lane == NC - 1, lane == 0
    at_north, at_south = row == NR - 1, row == 0
    lon_up = lambda x: pltpu.roll(x, NC - 1, 1)
    lon_down = lambda x: pltpu.roll(x, 1, 1)
    lat_up = lambda x: pltpu.roll(x, NR - 1, 0)
    lat_down = lambda x: pltpu.roll(x, 1, 0)

    def body(k, carry):
        at = pl.ds(pl.multiple_of(k * NR, NR), NR)
        wet = land[at, :].astype(jnp.float32)
        tt, uu, vv, visc = t[at, :], u[at, :], v[at, :], vi[at, :]
        wt = tt * wet
        side = [pltpu.roll(packed[i], NC - 1 - 2 * k, 1) for i in range(4)]
        line = [jnp.broadcast_to(lines[i, pl.ds(k, 1), :], (NR, NC)) for i in range(8)]
        wet_e = wet * lon_up(wet)
        wet_n = wet * lat_up(wet)
        face_e = 0.5 * (visc + lon_up(visc)) * wet_e
        face_n = 0.5 * (visc + lat_up(visc)) * wet_n

        def spread(flux_e, flux_n, i):
            flux_e = jnp.where(at_east, side[i], flux_e)
            flux_n = jnp.where(at_north, line[i], flux_n)
            back_e = jnp.where(at_west, side[i], lon_down(flux_e))
            back_n = jnp.where(at_south, line[4 + i], lat_down(flux_n))
            return flux_e - back_e + flux_n - back_n

        t_e = jnp.where(at_east, side[0], lon_up(wt))
        t_w = jnp.where(at_west, side[0], lon_down(wt))
        t_n = jnp.where(at_north, line[0], lat_up(wt))
        t_s = jnp.where(at_south, line[4], lat_down(wt))
        flux_e = uu * (7.0 * (wt + t_e) - (t_w + lon_up(t_e))) / 12.0 * wet_e
        flux_n = vv * (7.0 * (wt + t_n) - (t_s + lat_up(t_n))) / 12.0 * wet_n
        t_out[at, :] = wet * (tt - DT_ADV * spread(flux_e, flux_n, 1))
        u_out[at, :] = wet * (
            uu + DT_VISC * spread(face_e * (lon_up(uu) - uu), face_n * (lat_up(uu) - uu), 2)
        )
        v_out[at, :] = wet * (
            vv + DT_VISC * spread(face_e * (lon_up(vv) - vv), face_n * (lat_up(vv) - vv), 3)
        )
        return carry

    lax.fori_loop(0, NZ, body, 0, unroll=2)


def shared_sum(values, axes, count):
    spread = jnp.broadcast_to(values[None], (count,) + values.shape)
    return jnp.sum(lax.all_to_all(spread, axes, 0, 0), axis=0)


def local(tracer, east_vel, north_vel, viscosity, land_sea, thickness, surface, surface_diag, precond_kernel):
    flat = (NZ * NR, NC)
    t, u, v, vi, land = (
        x.reshape(flat) for x in (tracer, east_vel, north_vel, viscosity, land_sea)
    )
    block = NZ * NR * NC * 4
    lon, a, b = call(
        pack_kernel,
        [(8, NR, NC), (6, NZ, NC), (6, NZ, NC)],
        [VM] * 7,
        20 * NZ * NR * NC,
        5 * block,
    )(t, u, v, vi, land, surface, surface_diag)
    from_b = lax.ppermute(b, LAT, SWAP_B)
    from_a = lax.ppermute(a, LAT, SWAP_A)
    lon_b = lax.ppermute(lon, LON, SWAP_B)
    lon_a = lax.ppermute(lon, LON, SWAP_A)
    (inner,) = call(
        inner_kernel, [(2, NR, NC)], [SM] + [VM] * 4, 40 * NZ * NR * NC, 4 * block
    )(thickness, u, v, vi, land)
    th_lane = jnp.repeat(thickness, 2)[None]
    th_row = jnp.broadcast_to(thickness[:, None], (NZ, NC))
    (tr,) = call(join_kernel, [(2, NR, NC)], [VM] * 10, 10**6, 10**6)(
        inner, lon, lon_a, lon_b, a, from_a, b, from_b, th_lane, th_row
    )
    tr_b = lax.ppermute(tr, LON, SWAP_B)
    tr_a = lax.ppermute(tr, LON, SWAP_A)
    t_new, u_new, v_new = call(
        field_kernel,
        [flat] * 3,
        [VM] * 12,
        120 * NZ * NR * NC,
        8 * block,
        [pltpu.VMEM((4, NR, NC), jnp.float32), pltpu.VMEM((8, NZ, NC), jnp.float32)],
    )(t, u, v, vi, land, lon, lon_a, lon_b, a, from_a, b, from_b)
    wide = (NR, 2 * NC)
    rest, dg, edge, side_a, side_b = call(
        side_kernel, [wide, wide, (8, 2 * NC), wide, wide], [VM] * 6, 10**6, 10**5
    )(tr, tr_a, tr_b, lon, lon_a, lon_b)
    got_b = lax.ppermute(side_b, LAT, SWAP_B)
    got_a = lax.ppermute(side_a, LAT, SWAP_A)
    vecs, dots = call(
        solve_kernel, [(3, NR, NC), (8, NC)], [SM] + [VM] * 5, 10**6, 10**5
    )(precond_kernel, rest, dg, edge, got_a, got_b)
    dots = shared_sum(dots, ("x", "y", "c"), 32)
    dots = shared_sum(dots, ("zl", "zh"), 8)
    (surface_new,) = call(step_kernel, [(NR, NC)], [VM] * 3, 10**5, 10**4)(dots, vecs, surface)
    shape = (NZ, NR, NC)
    return t_new.reshape(shape), u_new.reshape(shape), v_new.reshape(shape), surface_new


def solution(mesh):
    sizes = dict(mesh.shape)
    assert sizes == {"lon": 16, "lat": 16} and tuple(mesh.axis_names) == ("lon", "lat")
    fine = Mesh(mesh.devices.reshape(2, 4, 2, 4, 4), ("zl", "x", "c", "y", "zh"))
    deep = P(None, LAT, LON)
    flat = P(LAT, LON)
    return jax.shard_map(
        local,
        mesh=fine,
        in_specs=(deep,) * 5 + (P(), flat, flat, P()),
        out_specs=(deep, deep, deep, flat),
        check_vma=False,
    )
```

```python
import jax
import jax.numpy as jnp
from jax import lax
from jax.experimental import pallas as pl
from jax.experimental.pallas import tpu as pltpu
from jax.sharding import Mesh
from jax.sharding import PartitionSpec as P

DT_ADV = 0.25
DT_VISC = 0.2
TAU = 0.05
SHIFTS = (0.3, 1.3)

LON = ("zl", "x", "c")
LAT = ("y", "zh")
NZ, NR, NC = 64, 16, 128
SWAP_A = [(i, i ^ 1) for i in range(16)]
SWAP_B = [(i, (i + 1) % 16 if i % 2 else (i - 1) % 16) for i in range(16)]

VM = pl.BlockSpec(memory_space=pltpu.VMEM)
SM = pl.BlockSpec(memory_space=pltpu.SMEM)
HBM = pl.BlockSpec(memory_space=pltpu.HBM)
FIELD_UNROLL = 4
FETCH_VMEM = 56


def call(kernel, outs, specs, flops, nbytes, scratch=(), place=VM, vmem=4):
    return pl.pallas_call(
        kernel,
        out_shape=[jax.ShapeDtypeStruct(s, jnp.float32) for s in outs],
        in_specs=specs,
        out_specs=[place] * len(outs),
        scratch_shapes=list(scratch),
        compiler_params=pltpu.CompilerParams(vmem_limit_bytes=vmem * 1024 * 1024),
        cost_estimate=pl.CostEstimate(flops=flops, bytes_accessed=nbytes, transcendentals=0),
    )


def lane_of(shape):
    return lax.broadcasted_iota(jnp.int32, shape, len(shape) - 1)


def row_of(shape):
    return lax.broadcasted_iota(jnp.int32, shape, len(shape) - 2)


def even_lon():
    return lax.axis_index("c") == 0


def even_lat():
    return lax.axis_index("zh") % 2 == 0


def lat_index():
    return lax.axis_index("y") * 4 + lax.axis_index("zh")


def b_exists():
    lat = lat_index()
    return jnp.where(jnp.logical_or(lat == 0, lat == 15), 0.0, 1.0).astype(jnp.float32)


HALF = NZ // 2
CHUNKS = 4


def halves():
    mine = jnp.where(even_lat(), 0, HALF)
    return pl.multiple_of(mine, HALF), pl.multiple_of(HALF - mine, HALF)


def edge_row(ref, north, inwards, first, count):
    if isinstance(north, bool):
        row = NR - 1 - inwards if north else inwards
    else:
        row = jnp.where(north, NR - 1 - inwards, inwards)
    return ref[pl.ds(first * NR + row, count, stride=NR), :].astype(jnp.float32)


def fetch_kernel(u, v, vi, land, sf, dg, lon_out, a_out, b_out, uo, vo, vio, lo, sems):
    span = NZ * NR // CHUNKS
    copies = []
    for c in range(CHUNKS):
        at = pl.ds(c * span, span)
        line = []
        for i, (src, dst) in enumerate(((u, uo), (v, vo), (vi, vio), (land, lo))):
            copy = pltpu.make_async_copy(src.at[at], dst.at[at], sems.at[c, i])
            copy.start()
            line.append(copy)
        copies.append(line)
    pair = lane_of((NR, NC)) // 2

    def body(k, acc):
        at = pl.ds(pl.multiple_of(k * NR, NR), NR)
        wet = lo[at, :].astype(jnp.float32)
        values = (uo[at, :], vo[at, :], vio[at, :], wet)
        mine = pair == k
        return tuple(
            jnp.where(mine, pltpu.roll(x, 2 * k + 1, 1), old) for x, old in zip(values, acc)
        )

    acc = (jnp.zeros((NR, NC), jnp.float32),) * 4
    per = NZ // CHUNKS
    for c in range(CHUNKS):
        for copy in copies[c]:
            copy.wait()
        acc = lax.fori_loop(c * per, (c + 1) * per, body, acc, unroll=8)
    for i in range(4):
        lon_out[i] = acc[i]
    lon_out[4] = sf[...]
    lon_out[5] = dg[...]
    even = even_lat()
    mine, _ = halves()
    for north, out in ((even, a_out), (jnp.logical_not(even), b_out)):
        for i, ref in enumerate((uo, vo, vio, lo)):
            out[i] = edge_row(ref, north, 0, mine, HALF)


def inner_kernel(thick, t, u, v, vi, w, out, lon_out, a_out, b_out):
    lane, row = lane_of((NR, NC)), row_of((NR, NC))
    pair = lane // 2
    half_lane = lane < NC // 2

    def body(k, acc):
        at = pl.ds(pl.multiple_of(k * NR, NR), NR)
        th = thick[k]
        wet, uu, vv, visc = w[at, :].astype(jnp.float32), u[at, :], v[at, :], vi[at, :]
        half = 0.5 * th
        own = wet * th
        east = (visc + pltpu.roll(visc, NC - 1, 1)) * (wet * pltpu.roll(wet, NC - 1, 1)) * half
        north = (visc + pltpu.roll(visc, NR - 1, 0)) * (wet * pltpu.roll(wet, NR - 1, 0)) * half
        first = t[at, :] * wet
        inner = jnp.where(half_lane, pltpu.roll(first, NC - 1, 1), pltpu.roll(first, 1, 1))
        mine = pair == k
        return (
            acc[0] + own * uu,
            acc[1] + east * (pltpu.roll(uu, NC - 1, 1) - uu),
            acc[2] + north * (pltpu.roll(uu, NR - 1, 0) - uu),
            acc[3] + own * vv,
            acc[4] + east * (pltpu.roll(vv, NC - 1, 1) - vv),
            acc[5] + north * (pltpu.roll(vv, NR - 1, 0) - vv),
            jnp.where(mine, pltpu.roll(first, 2 * k + 1, 1), acc[6]),
            jnp.where(mine, pltpu.roll(7.0 * first - inner, 2 * k + 1, 1), acc[7]),
        )

    zero = jnp.zeros((NR, NC), jnp.float32)
    acc = lax.fori_loop(0, NZ, body, (zero,) * 8, unroll=4)
    for i in range(2):
        east = jnp.where(lane == NC - 1, 0.0, acc[3 * i + 1])
        north = jnp.where(row == NR - 1, 0.0, acc[3 * i + 2])
        out[i] = acc[3 * i] + DT_VISC * (
            east - pltpu.roll(east, 1, 1) + north - pltpu.roll(north, 1, 0)
        )
        lon_out[i] = acc[6 + i]
    even = even_lat()
    _, theirs = halves()
    for north, dst in ((even, a_out), (jnp.logical_not(even), b_out)):
        for i, ref in enumerate((u, v, vi, w)):
            dst[i] = edge_row(ref, north, 0, theirs, HALF)
        for i in range(2):
            first = edge_row(t, north, 0, i * HALF, HALF) * edge_row(w, north, 0, i * HALF, HALF)
            second = edge_row(t, north, 1, i * HALF, HALF) * edge_row(w, north, 1, i * HALF, HALF)
            dst[4 + i] = first
            dst[6 + i] = 7.0 * first - second


def lon_sides(first, second):
    even = even_lon()
    return jnp.where(even, first, second), jnp.where(even, second, first)


def beyond(from_a, from_b):
    east, west = lon_sides(from_a, from_b)
    is_east = lane_of((NR, NC)) % 2 == 0
    return jnp.where(is_east, pltpu.roll(east, NC - 1, 1), pltpu.roll(west, 1, 1))


def face_in(own, other):
    face = 0.5 * (own[2] + other[2]) * (own[3] * other[3])
    return face * (other[0] - own[0]), face * (other[1] - own[1])


MSG = 72


def join_kernel(inner, lon, lon_a, lon_b, lon2, a2, from_a, b2, from_b, th_lane, th_row, out):
    lane = lane_of((NR, NC))
    own = [lon[i] for i in range(4)]
    other = [beyond(lon_a[i], lon_b[i]) for i in range(4)]
    is_east = lane % 2 == 0
    for i, grad in enumerate(face_in(own, other)):
        grad = grad * th_lane[...]
        east = jnp.sum(jnp.where(is_east, grad, 0.0), axis=1, keepdims=True)
        west = jnp.sum(jnp.where(is_east, 0.0, grad), axis=1, keepdims=True)
        add = jnp.where(lane == NC - 1, east, 0.0) + jnp.where(lane == 0, west, 0.0)
        out[NR * i : NR * (i + 1), :] = inner[i] + DT_VISC * add
    _, theirs = halves()
    weight = DT_VISC * th_row[pl.ds(theirs, HALF), :]
    lat_a = face_in([a2[i] for i in range(4)], [from_a[i] for i in range(4)])
    weight_b = weight * b_exists()
    lat_b = face_in([b2[i] for i in range(4)], [from_b[i] for i in range(4)])
    sums = [jnp.sum(x * weight, axis=0, keepdims=True) for x in lat_a]
    sums += [jnp.sum(x * weight_b, axis=0, keepdims=True) for x in lat_b]
    out[2 * NR : 2 * NR + 8, :] = jnp.concatenate(sums + [jnp.zeros((4, NC), jnp.float32)], axis=0)
    out[40:56, :] = lon2[0]
    out[56:72, :] = lon2[1]


def side_kernel(msg, msg_a, msg_b, lon, lon_a, lon_b, rest_out, diag_out, edge_out, a_out, b_out):
    def widen(own, first, second):
        east, west = lon_sides(first, second)
        halo = jnp.where(lane_of(own.shape) < NC // 2, east, west)
        return jnp.concatenate([own, halo], axis=1)

    part = lambda lo, hi: widen(msg[lo:hi, :], msg_a[lo:hi, :], msg_b[lo:hi, :])
    te, tn, faces = part(0, NR), part(NR, 2 * NR), part(2 * NR, 2 * NR + 8)
    sf, dg = (widen(lon[i], lon_a[i], lon_b[i]) for i in (4, 5))
    row = row_of((NR, 2 * NC))
    even = even_lat()
    north_u, north_v = (jnp.where(even, faces[i : i + 1], faces[i + 2 : i + 3]) for i in range(2))
    south_u, south_v = (jnp.where(even, faces[i + 2 : i + 3], faces[i : i + 1]) for i in range(2))
    at_north, at_south = row == NR - 1, row == 0
    te = te + jnp.where(at_north, north_u, 0.0) + jnp.where(at_south, south_u, 0.0)
    tn = tn + jnp.where(at_north, north_v, 0.0) + jnp.where(at_south, south_v, 0.0)
    east = lambda x: pltpu.roll(x, 2 * NC - 1, 1)
    west = lambda x: pltpu.roll(x, 1, 1)
    north = lambda x: jnp.where(at_north, 0.0, pltpu.roll(x, NR - 1, 0))
    south = lambda x: jnp.where(at_south, 0.0, pltpu.roll(x, 1, 0))
    across = lambda fu, fv: TAU * (fu - west(fu) + fv)
    rest = sf - TAU * (te - west(te) + tn - south(tn))
    rest = rest - ((4.0 + dg) * sf - (east(sf) + west(sf) + north(sf) + south(sf)))
    rest = rest - jnp.where(at_south, TAU * south_v, 0.0)
    rest_out[...] = rest
    diag_out[...] = dg
    first = TAU * tn[NR - 1 :] + sf[NR - 1 :] + across(north_u, north_v)
    second = -TAU * north_v
    to_south = sf[:1] + across(south_u, south_v)
    zero = jnp.zeros((5, 2 * NC), jnp.float32)
    edge_out[...] = jnp.concatenate([first, second, to_south, zero], axis=0)
    msg_north = jnp.concatenate([rest[8:], dg[11:], first, second, zero[:1]], axis=0)
    msg_south = jnp.concatenate([rest[:9], dg[:6], to_south], axis=0)
    a_out[...] = jnp.where(even, msg_north, msg_south)
    b_out[...] = jnp.where(even, msg_south, msg_north)


def solve_kernel(pc, rest, dg, edge, from_a, from_b, v_out, dots_out):
    rows, wide = 3 * NR, 2 * NC
    even = even_lat()
    exists = b_exists()
    msg_a = from_a[...]
    msg_b = from_b[...] * exists
    north = jnp.where(even, msg_a, msg_b)
    south = jnp.where(even, msg_b, msg_a)
    zeros = lambda n: jnp.zeros((n, wide), jnp.float32)
    row = row_of((rows, wide))
    lat = lat_index()
    low = jnp.where(lat == 0, NR, 0)
    high = jnp.where(lat == 15, 2 * NR, 3 * NR)
    inside = jnp.where(jnp.logical_and(row >= low, row < high), 1.0, 0.0).astype(jnp.float32)
    below = jnp.concatenate([zeros(8), south[:7], south[7:8] + edge[2:3]], axis=0)
    above = jnp.concatenate(
        [north[:1] + edge[0:1], north[1:2] + edge[1:2], north[2:9], zeros(7)], axis=0
    )
    own = rest[...] + jnp.concatenate([south[13:15], zeros(13), north[15:]], axis=0)
    res = jnp.concatenate([below, own, above], axis=0) * inside
    diag = 4.0 + jnp.concatenate([zeros(11), south[8:13], dg[...], north[9:15], zeros(10)], axis=0)

    def lon_shift(x, n):
        return x if n == 0 else pltpu.roll(x, (-n) % wide, 1)

    def lat_shift(x, n):
        return x if n == 0 else pltpu.roll(x, (-n) % rows, 0)

    def operate(x):
        near = lon_shift(x, 1) + lon_shift(x, -1) + lat_shift(x, 1) + lat_shift(x, -1)
        return diag * x - near

    def precondition(x):
        moved = [lon_shift(x, b) for b in range(-2, 3)]
        total = None
        for a in range(-2, 3):
            line = pc[a + 2, 0] * moved[0]
            for b in range(1, 5):
                line = line + pc[a + 2, b] * moved[b]
            line = lat_shift(line, a)
            total = line if total is None else total + line
        return total * inside

    scale = 1.0 / (5.0 * jnp.full((1, wide), pc[2, 2], jnp.float32))
    p0 = res
    v0 = precondition(p0)
    a0 = operate(v0)
    p1 = (a0 * scale - SHIFTS[0] * p0) * inside
    v1 = precondition(p1)
    a1 = operate(v1)
    p2 = (a1 * scale - SHIFTS[1] * p1) * inside
    v2 = precondition(p2)
    mine = lambda x: x[NR : 2 * NR, :NC]
    half_a2 = mine(diag * v2 - 2.0 * (lon_shift(v2, 1) + lat_shift(v2, 1)))
    v0, v1, v2, a0, a1, r = (mine(x) for x in (v0, v1, v2, a0, a1, p0))
    v_out[0] = v0
    v_out[1] = v1
    v_out[2] = v2
    pairs = ((v0, a0), (v0, a1), (v2, a0), (v1, a1), (v2, a1), (v2, half_a2), (v0, r), (v1, r), (v2, r))
    lines = []
    for x, y in pairs:
        line = jnp.sum(x * y, axis=0, keepdims=True)
        lines.append(line + pltpu.roll(line, NC // 2, 1))
    left = lane_of((1, NC)) < NC // 2
    lines.append(lines[-1])
    out = [jnp.where(left, lines[2 * i], lines[2 * i + 1]) for i in range(5)]
    dots_out[...] = jnp.concatenate(out + [jnp.zeros((3, NC), jnp.float32)], axis=0)


def step_kernel(dots, v, sf, out):
    d = dots[...]
    left = lane_of((8, NC)) < NC // 2
    first = jnp.sum(jnp.where(left, d, 0.0), axis=1, keepdims=True)
    second = jnp.sum(jnp.where(left, 0.0, d), axis=1, keepdims=True)
    h = []
    for i in range(5):
        h += [first[i : i + 1], second[i : i + 1]]
    h00, h01, h02, h11, h12, h22, g0, g1, g2 = h[:9]
    l1 = h01 / h00
    l2 = h02 / h00
    d1 = h11 - l1 * h01
    e12 = h12 - l1 * h02
    l3 = e12 / d1
    d2 = h22 - l2 * h02 - l3 * e12
    y1 = g1 - l1 * g0
    y2 = g2 - l2 * g0 - l3 * y1
    c2 = y2 / d2
    c1 = y1 / d1 - l3 * c2
    c0 = g0 / h00 - l1 * c1 - l2 * c2
    out[...] = sf[...] + c0 * v[0] + c1 * v[1] + c2 * v[2]


def field_kernel(
    t, u, v, vi, w,
    lon, lon_a, lon_b, msg, msg_a, msg_b,
    from_a, from_a2, from_b, from_b2,
    t_hbm, u_hbm, v_hbm, t_out, u_out, v_out, packed, lines, sems,
):
    lane, row = lane_of((NR, NC)), row_of((NR, NC))
    is_east = lane % 2 == 0
    own = [lon[i] for i in range(4)]
    other = [beyond(lon_a[i], lon_b[i]) for i in range(4)]
    grad_u, grad_v = face_in(own, other)
    packed[0] = beyond(msg_a[40:56, :], msg_b[40:56, :])
    far = msg[56:72, :] + beyond(msg_a[56:72, :], msg_b[56:72, :])
    packed[1] = jnp.where(is_east, own[0], other[0]) * far * (1.0 / 12.0) * (own[3] * other[3])
    packed[2] = jnp.where(is_east, grad_u, -grad_u)
    packed[3] = jnp.where(is_east, grad_v, -grad_v)
    even = even_lat()
    exists = b_exists()
    mine, theirs = halves()
    for first, there_a, there_b in ((mine, from_a2, from_b2), (theirs, from_a, from_b)):
        at = pl.ds(first, HALF)
        part = first // HALF
        for side in range(2):
            use_a = even if side == 0 else jnp.logical_not(even)
            here = [edge_row(ref, side == 0, 0, first, HALF) for ref in (u, v, vi, w)]
            there = [jnp.where(use_a, there_a[i], there_b[i] * exists) for i in range(4)]
            near = jnp.where(use_a, from_a2[4 + part], from_b2[4 + part] * exists)
            far = jnp.where(use_a, from_a2[6 + part], from_b2[6 + part])
            near_own = edge_row(t, side == 0, 0, first, HALF) * here[3]
            next_own = edge_row(t, side == 0, 1, first, HALF) * edge_row(w, side == 0, 1, first, HALF)
            far = far + (7.0 * near_own - next_own)
            grad_u, grad_v = face_in(here, there)
            speed = here[1] if side == 0 else there[1]
            lines[4 * side, at, :] = near
            lines[4 * side + 1, at, :] = speed * far * (1.0 / 12.0) * (here[3] * there[3])
            lines[4 * side + 2, at, :] = grad_u if side == 0 else -grad_u
            lines[4 * side + 3, at, :] = grad_v if side == 0 else -grad_v

    at_east, at_west = lane == NC - 1, lane == 0
    at_north, at_south = row == NR - 1, row == 0
    lon_up = lambda x: pltpu.roll(x, NC - 1, 1)
    lon_down = lambda x: pltpu.roll(x, 1, 1)
    lat_up = lambda x: pltpu.roll(x, NR - 1, 0)
    lat_down = lambda x: pltpu.roll(x, 1, 0)

    def body(k, carry):
        at = pl.ds(pl.multiple_of(k * NR, NR), NR)
        tt, uu, vv, visc = t[at, :], u[at, :], v[at, :], vi[at, :]
        wet = w[at, :].astype(jnp.float32)
        wt = tt * wet
        side = [pltpu.roll(packed[i], NC - 1 - 2 * k, 1) for i in range(4)]
        line = [jnp.broadcast_to(lines[i, pl.ds(k, 1), :], (NR, NC)) for i in range(8)]
        wet_e = wet * lon_up(wet)
        wet_n = wet * lat_up(wet)
        face_e = (0.5 * DT_VISC) * (visc + lon_up(visc)) * wet_e
        face_n = (0.5 * DT_VISC) * (visc + lat_up(visc)) * wet_n

        def spread(flux_e, flux_n, i, by):
            flux_e = jnp.where(at_east, by * side[i], flux_e)
            flux_n = jnp.where(at_north, by * line[i], flux_n)
            back_e = jnp.where(at_west, by * side[i], lon_down(flux_e))
            back_n = jnp.where(at_south, by * line[4 + i], lat_down(flux_n))
            return flux_e - back_e + flux_n - back_n

        t_e = jnp.where(at_east, side[0], lon_up(wt))
        t_w = jnp.where(at_west, side[0], lon_down(wt))
        t_n = jnp.where(at_north, line[0], lat_up(wt))
        t_s = jnp.where(at_south, line[4], lat_down(wt))
        by = DT_ADV / 12.0
        flux_e = uu * (7.0 * (wt + t_e) - (t_w + lon_up(t_e))) * (by * wet_e)
        flux_n = vv * (7.0 * (wt + t_n) - (t_s + lat_up(t_n))) * (by * wet_n)
        t_out[at, :] = wet * (tt - spread(flux_e, flux_n, 1, DT_ADV))
        u_out[at, :] = wet * (uu + spread(face_e * (lon_up(uu) - uu), face_n * (lat_up(uu) - uu), 2, DT_VISC))
        v_out[at, :] = wet * (vv + spread(face_e * (lon_up(vv) - vv), face_n * (lat_up(vv) - vv), 3, DT_VISC))
        return carry

    per = NZ // CHUNKS
    copies = []
    for c in range(CHUNKS):
        lax.fori_loop(c * per, (c + 1) * per, body, 0, unroll=FIELD_UNROLL)
        at = pl.ds(c * per * NR, per * NR)
        for i, (src, dst) in enumerate(((t_out, t_hbm), (u_out, u_hbm), (v_out, v_hbm))):
            copy = pltpu.make_async_copy(src.at[at], dst.at[at], sems.at[c, i])
            copy.start()
            copies.append(copy)
    for copy in copies:
        copy.wait()


def shared_sum(values, axes, count):
    spread = jnp.broadcast_to(values[None], (count,) + values.shape)
    return jnp.sum(lax.all_to_all(spread, axes, 0, 0), axis=0)


def local(tracer, east_vel, north_vel, viscosity, land_sea, thickness, surface, surface_diag, precond_kernel):
    flat = (NZ * NR, NC)
    u, v, vi, w, t = (x.reshape(flat) for x in (east_vel, north_vel, viscosity, land_sea, tracer))
    block = NZ * NR * NC * 4
    lon, a, b = call(
        fetch_kernel,
        [(6, NR, NC), (4, HALF, NC), (4, HALF, NC)],
        [HBM] * 4 + [VM] * 2,
        20 * NZ * NR * NC,
        5 * block,
        [pltpu.VMEM(flat, jnp.float32)] * 3
        + [pltpu.VMEM(flat, jnp.int32), pltpu.SemaphoreType.DMA((CHUNKS, 4))],
        vmem=FETCH_VMEM,
    )(u, v, vi, w, surface, surface_diag)
    from_b = lax.ppermute(b, LAT, SWAP_B)
    from_a = lax.ppermute(a, LAT, SWAP_A)
    lon_b = lax.ppermute(lon, LON, SWAP_B)
    lon_a = lax.ppermute(lon, LON, SWAP_A)
    inner, lon2, a2, b2 = call(
        inner_kernel,
        [(2, NR, NC), (2, NR, NC), (8, HALF, NC), (8, HALF, NC)],
        [SM] + [VM] * 5,
        40 * NZ * NR * NC,
        4 * block,
    )(thickness, t, u, v, vi, w)
    th_lane = jnp.repeat(thickness, 2)[None]
    th_row = jnp.broadcast_to(thickness[:, None], (NZ, NC))
    (msg,) = call(join_kernel, [(MSG, NC)], [VM] * 11, 10**6, 10**6)(
        inner, lon, lon_a, lon_b, lon2, a2, from_a, b2, from_b, th_lane, th_row
    )
    msg_b = lax.ppermute(msg, LON, SWAP_B)
    msg_a = lax.ppermute(msg, LON, SWAP_A)
    from_b2 = lax.ppermute(b2, LAT, SWAP_B)
    from_a2 = lax.ppermute(a2, LAT, SWAP_A)
    wide = (NR, 2 * NC)
    rest, dg, edge, side_a, side_b = call(
        side_kernel, [wide, wide, (8, 2 * NC), wide, wide], [VM] * 6, 10**6, 10**5
    )(msg, msg_a, msg_b, lon, lon_a, lon_b)
    got_b = lax.ppermute(side_b, LAT, SWAP_B)
    got_a = lax.ppermute(side_a, LAT, SWAP_A)
    t_new, u_new, v_new = call(
        field_kernel,
        [flat] * 3,
        [VM] * 15,
        120 * NZ * NR * NC,
        8 * block,
        [pltpu.VMEM(flat, jnp.float32)] * 3
        + [
            pltpu.VMEM((4, NR, NC), jnp.float32),
            pltpu.VMEM((8, NZ, NC), jnp.float32),
            pltpu.SemaphoreType.DMA((CHUNKS, 3)),
        ],
        HBM,
    )(t, u, v, vi, w, lon, lon_a, lon_b, msg, msg_a, msg_b, from_a, from_a2, from_b, from_b2)
    vecs, dots = call(
        solve_kernel, [(3, NR, NC), (8, NC)], [SM] + [VM] * 5, 10**6, 10**5
    )(precond_kernel, rest, dg, edge, got_a, got_b)
    dots = shared_sum(dots, ("x", "y", "c"), 32)
    dots = shared_sum(dots, ("zl", "zh"), 8)
    (surface_new,) = call(step_kernel, [(NR, NC)], [VM] * 3, 10**5, 10**4)(dots, vecs, surface)
    shape = (NZ, NR, NC)
    return t_new.reshape(shape), u_new.reshape(shape), v_new.reshape(shape), surface_new


def solution(mesh):
    sizes = dict(mesh.shape)
    assert sizes == {"lon": 16, "lat": 16} and tuple(mesh.axis_names) == ("lon", "lat")
    fine = Mesh(mesh.devices.reshape(2, 4, 2, 4, 4), ("zl", "x", "c", "y", "zh"))
    deep = P(None, LAT, LON)
    flat = P(LAT, LON)
    return jax.shard_map(
        local,
        mesh=fine,
        in_specs=(deep,) * 5 + (P(), flat, flat, P()),
        out_specs=(deep, deep, deep, flat),
        check_vma=False,
    )
```

```python
import jax
import jax.numpy as jnp
from jax import lax
from jax.experimental import pallas as pl
from jax.experimental.pallas import tpu as pltpu
from jax.sharding import Mesh
from jax.sharding import PartitionSpec as P

DT_ADV = 0.25
DT_VISC = 0.2
TAU = 0.05
SHIFTS = (0.3, 1.3)

LON = ("zl", "x", "c")
LAT = ("y", "zh")
NZ, NR, NC = 64, 16, 128
SWAP_A = [(i, i ^ 1) for i in range(16)]
SWAP_B = [(i, (i + 1) % 16 if i % 2 else (i - 1) % 16) for i in range(16)]

VM = pl.BlockSpec(memory_space=pltpu.VMEM)
SM = pl.BlockSpec(memory_space=pltpu.SMEM)
HBM = pl.BlockSpec(memory_space=pltpu.HBM)
FETCH_VMEM = 53.5
FETCH_UNROLL = 4


def call(kernel, outs, specs, flops, nbytes, scratch=(), place=VM, vmem=4):
    return pl.pallas_call(
        kernel,
        out_shape=[jax.ShapeDtypeStruct(s, jnp.float32) for s in outs],
        in_specs=specs,
        out_specs=place if isinstance(place, list) else [place] * len(outs),
        scratch_shapes=list(scratch),
        compiler_params=pltpu.CompilerParams(vmem_limit_bytes=int(vmem * 1024 * 1024)),
        cost_estimate=pl.CostEstimate(flops=flops, bytes_accessed=nbytes, transcendentals=0),
    )


def lane_of(shape):
    return lax.broadcasted_iota(jnp.int32, shape, len(shape) - 1)


def row_of(shape):
    return lax.broadcasted_iota(jnp.int32, shape, len(shape) - 2)


def even_lon():
    return lax.axis_index("c") == 0


def even_lat():
    return lax.axis_index("zh") % 2 == 0


def lat_index():
    return lax.axis_index("y") * 4 + lax.axis_index("zh")


def b_exists():
    lat = lat_index()
    return jnp.where(jnp.logical_or(lat == 0, lat == 15), 0.0, 1.0).astype(jnp.float32)


HALF = NZ // 2
CHUNKS = 4


def halves():
    mine = jnp.where(even_lat(), 0, HALF)
    return pl.multiple_of(mine, HALF), pl.multiple_of(HALF - mine, HALF)


def edge_row(ref, north, inwards, first, count):
    if isinstance(north, bool):
        row = NR - 1 - inwards if north else inwards
    else:
        row = jnp.where(north, NR - 1 - inwards, inwards)
    return ref[pl.ds(first * NR + row, count, stride=NR), :].astype(jnp.float32)


def pipeline(copies, body, acc, unroll):
    per = NZ // CHUNKS

    def start(c, carry):
        for copy in copies(c):
            copy.start()
        return carry

    def chunk(c, carry):
        for copy in copies(c):
            copy.wait()
        return lax.fori_loop(0, per, lambda i, x: body(c * per + i, x), carry, unroll=unroll)

    lax.fori_loop(0, CHUNKS, start, 0)
    return lax.fori_loop(0, CHUNKS, chunk, acc)


def chunk_copies(pairs, sems):
    span = NZ * NR // CHUNKS

    def copies(c):
        at = pl.ds(pl.multiple_of(c * span, span), span)
        return [
            pltpu.make_async_copy(src.at[at], dst.at[at], sems.at[c, i])
            for i, (src, dst) in enumerate(pairs)
        ]

    return copies


def level(k):
    return pl.ds(pl.multiple_of(k * NR, NR), NR)


def fetch_kernel(
    thick_hbm, u, v, vi, land, lon_out, a_out, b_out, late_a, late_b, out, th_out, uo, vo, vio, lo, thick, sems, th_sem
):
    lane, row = lane_of((NR, NC)), row_of((NR, NC))
    pair = lane // 2
    up = lambda x: pltpu.roll(x, NC - 1, 1)
    north_of = lambda x: pltpu.roll(x, NR - 1, 0)

    def body(k, acc):
        at = level(k)
        wet, uu, vv, visc = lo[at, :].astype(jnp.float32), uo[at, :], vo[at, :], vio[at, :]
        mine = pair == k
        packed = tuple(
            jnp.where(mine, pltpu.roll(x, 2 * k + 1, 1), old)
            for x, old in zip((uu, vv, visc, wet), acc[:4])
        )
        th = jnp.full((1, NC), thick[k], jnp.float32)
        th_out[pl.ds(k, 1), :] = th
        own = wet * th
        half = 0.5 * own
        east = (visc + up(visc)) * (half * up(wet))
        north = (visc + north_of(visc)) * (half * north_of(wet))
        return packed + (
            acc[4] + own * uu,
            acc[5] + east * (up(uu) - uu),
            acc[6] + north * (north_of(uu) - uu),
            acc[7] + own * vv,
            acc[8] + east * (up(vv) - vv),
            acc[9] + north * (north_of(vv) - vv),
            jnp.where(mine[:1], th, acc[10]),
        )

    thick_copy = pltpu.make_async_copy(thick_hbm, thick, th_sem)
    thick_copy.start()
    copies = chunk_copies(((u, uo), (v, vo), (vi, vio), (land, lo)), sems)
    thick_copy.wait()
    zero = jnp.zeros((NR, NC), jnp.float32)
    acc = pipeline(copies, body, (zero,) * 10 + (zero[:1],), FETCH_UNROLL)
    for i in range(4):
        lon_out[i] = acc[i]
    th_out[NZ:, :] = jnp.broadcast_to(acc[10], (8, NC))
    for i in range(2):
        east = jnp.where(lane == NC - 1, 0.0, acc[3 * i + 5])
        north = jnp.where(row == NR - 1, 0.0, acc[3 * i + 6])
        out[i] = acc[3 * i + 4] + DT_VISC * (
            east - pltpu.roll(east, 1, 1) + north - pltpu.roll(north, 1, 0)
        )
    even = even_lat()
    mine, theirs = halves()
    for north, first, rest in ((even, a_out, late_a), (jnp.logical_not(even), b_out, late_b)):
        for i, ref in enumerate((uo, vo, vio, lo)):
            first[i] = edge_row(ref, north, 0, mine, HALF)
            rest[i] = edge_row(ref, north, 0, theirs, HALF)


def late_kernel(pc, t, land, late_a, late_b, lon_out, a_out, b_out, pc_out, to, lo, sems):
    lane = lane_of((NR, NC))
    pair = lane // 2
    half_lane = lane < NC // 2

    def body(k, acc):
        at = level(k)
        first = to[at, :] * lo[at, :].astype(jnp.float32)
        inner = jnp.where(half_lane, pltpu.roll(first, NC - 1, 1), pltpu.roll(first, 1, 1))
        mine = pair == k
        return tuple(
            jnp.where(mine, pltpu.roll(x, 2 * k + 1, 1), old)
            for x, old in zip((first, 7.0 * first - inner), acc)
        )

    copies = chunk_copies(((t, to), (land, lo)), sems)
    acc = pipeline(copies, body, (jnp.zeros((NR, NC), jnp.float32),) * 2, 8)
    lon_out[0] = acc[0]
    lon_out[1] = acc[1]
    for i in range(25):
        pc_out[i : i + 1, :] = jnp.full((1, 2 * NC), pc[i // 5, i % 5], jnp.float32)
    even = even_lat()
    for north, src, dst in ((even, late_a, a_out), (jnp.logical_not(even), late_b, b_out)):
        dst[:4] = src[...]
        for i in range(2):
            first, second = (
                edge_row(to, north, n, i * HALF, HALF) * edge_row(lo, north, n, i * HALF, HALF)
                for n in range(2)
            )
            dst[4 + i] = first
            dst[6 + i] = 7.0 * first - second


def lon_sides(first, second):
    even = even_lon()
    return jnp.where(even, first, second), jnp.where(even, second, first)


def beyond(from_a, from_b):
    east, west = lon_sides(from_a, from_b)
    is_east = lane_of((NR, NC)) % 2 == 0
    return jnp.where(is_east, pltpu.roll(east, NC - 1, 1), pltpu.roll(west, 1, 1))


def face_in(own, other):
    face = 0.5 * (own[2] + other[2]) * (own[3] * other[3])
    return face * (other[0] - own[0]), face * (other[1] - own[1])


MSG = 104


def join_kernel(inner, lon, lon_a, lon_b, lon2, a2, from_a, b2, from_b, th, sf, dg, out):
    lane = lane_of((NR, NC))
    own = [lon[i] for i in range(4)]
    other = [beyond(lon_a[i], lon_b[i]) for i in range(4)]
    is_east = lane % 2 == 0
    for i, grad in enumerate(face_in(own, other)):
        grad = grad * th[NZ : NZ + 1, :]
        east = jnp.sum(jnp.where(is_east, grad, 0.0), axis=1, keepdims=True)
        west = jnp.sum(jnp.where(is_east, 0.0, grad), axis=1, keepdims=True)
        add = jnp.where(lane == NC - 1, east, 0.0) + jnp.where(lane == 0, west, 0.0)
        out[NR * i : NR * (i + 1), :] = inner[i] + DT_VISC * add
    _, theirs = halves()
    weight = DT_VISC * th[pl.ds(theirs, HALF), :]
    lat_a = face_in([a2[i] for i in range(4)], [from_a[i] for i in range(4)])
    weight_b = weight * b_exists()
    lat_b = face_in([b2[i] for i in range(4)], [from_b[i] for i in range(4)])
    sums = [jnp.sum(x * weight, axis=0, keepdims=True) for x in lat_a]
    sums += [jnp.sum(x * weight_b, axis=0, keepdims=True) for x in lat_b]
    out[2 * NR : 2 * NR + 8, :] = jnp.concatenate(sums + [jnp.zeros((4, NC), jnp.float32)], axis=0)
    out[40:56, :] = lon2[0]
    out[56:72, :] = lon2[1]
    out[72:88, :] = sf[...]
    out[88:104, :] = dg[...]


def side_kernel(msg, msg_a, msg_b, rest_out, diag_out, edge_out, a_out, b_out):
    def widen(own, first, second):
        east, west = lon_sides(first, second)
        halo = jnp.where(lane_of(own.shape) < NC // 2, east, west)
        return jnp.concatenate([own, halo], axis=1)

    part = lambda lo, hi: widen(msg[lo:hi, :], msg_a[lo:hi, :], msg_b[lo:hi, :])
    te, tn, faces = part(0, NR), part(NR, 2 * NR), part(2 * NR, 2 * NR + 8)
    sf, dg = part(72, 88), part(88, 104)
    row = row_of((NR, 2 * NC))
    even = even_lat()
    north_u, north_v = (jnp.where(even, faces[i : i + 1], faces[i + 2 : i + 3]) for i in range(2))
    south_u, south_v = (jnp.where(even, faces[i + 2 : i + 3], faces[i : i + 1]) for i in range(2))
    at_north, at_south = row == NR - 1, row == 0
    te = te + jnp.where(at_north, north_u, 0.0) + jnp.where(at_south, south_u, 0.0)
    tn = tn + jnp.where(at_north, north_v, 0.0) + jnp.where(at_south, south_v, 0.0)
    east = lambda x: pltpu.roll(x, 2 * NC - 1, 1)
    west = lambda x: pltpu.roll(x, 1, 1)
    north = lambda x: jnp.where(at_north, 0.0, pltpu.roll(x, NR - 1, 0))
    south = lambda x: jnp.where(at_south, 0.0, pltpu.roll(x, 1, 0))
    across = lambda fu, fv: TAU * (fu - west(fu) + fv)
    rest = sf - TAU * (te - west(te) + tn - south(tn))
    rest = rest - ((4.0 + dg) * sf - (east(sf) + west(sf) + north(sf) + south(sf)))
    rest = rest - jnp.where(at_south, TAU * south_v, 0.0)
    rest_out[...] = rest
    diag_out[...] = dg
    first = TAU * tn[NR - 1 :] + sf[NR - 1 :] + across(north_u, north_v)
    second = -TAU * north_v
    to_south = sf[:1] + across(south_u, south_v)
    zero = jnp.zeros((5, 2 * NC), jnp.float32)
    edge_out[...] = jnp.concatenate([first, second, to_south, zero], axis=0)
    msg_north = jnp.concatenate([rest[8:], dg[11:], first, second, zero[:1]], axis=0)
    msg_south = jnp.concatenate([rest[:9], dg[:6], to_south], axis=0)
    a_out[...] = jnp.where(even, msg_north, msg_south)
    b_out[...] = jnp.where(even, msg_south, msg_north)


def solve_kernel(pc, rest, dg, edge, from_a, from_b, v_hbm, dots_out, v_out, sem):
    rows, wide = 3 * NR, 2 * NC
    even = even_lat()
    exists = b_exists()
    msg_a = from_a[...]
    msg_b = from_b[...] * exists
    north = jnp.where(even, msg_a, msg_b)
    south = jnp.where(even, msg_b, msg_a)
    zeros = lambda n: jnp.zeros((n, wide), jnp.float32)
    row = row_of((rows, wide))
    lat = lat_index()
    low = jnp.where(lat == 0, NR, 0)
    high = jnp.where(lat == 15, 2 * NR, 3 * NR)
    inside = jnp.where(jnp.logical_and(row >= low, row < high), 1.0, 0.0).astype(jnp.float32)
    below = jnp.concatenate([zeros(8), south[:7], south[7:8] + edge[2:3]], axis=0)
    above = jnp.concatenate(
        [north[:1] + edge[0:1], north[1:2] + edge[1:2], north[2:9], zeros(7)], axis=0
    )
    own = rest[...] + jnp.concatenate([south[13:15], zeros(13), north[15:]], axis=0)
    res = jnp.concatenate([below, own, above], axis=0) * inside
    diag = 4.0 + jnp.concatenate([zeros(11), south[8:13], dg[...], north[9:15], zeros(10)], axis=0)

    def lon_shift(x, n):
        return x if n == 0 else pltpu.roll(x, (-n) % wide, 1)

    def lat_shift(x, n):
        return x if n == 0 else pltpu.roll(x, (-n) % rows, 0)

    def operate(x):
        near = lon_shift(x, 1) + lon_shift(x, -1) + lat_shift(x, 1) + lat_shift(x, -1)
        return diag * x - near

    def tap(a, b):
        at = 5 * (a + 2) + b + 2
        return pc[at : at + 1, :]

    def precondition(x):
        moved = [lon_shift(x, b) for b in range(-2, 3)]
        total = None
        for a in range(-2, 3):
            line = tap(a, -2) * moved[0]
            for b in range(1, 5):
                line = line + tap(a, b - 2) * moved[b]
            line = lat_shift(line, a)
            total = line if total is None else total + line
        return total * inside

    scale = 1.0 / (5.0 * tap(0, 0))
    p0 = res
    v0 = precondition(p0)
    a0 = operate(v0)
    p1 = (a0 * scale - SHIFTS[0] * p0) * inside
    v1 = precondition(p1)
    a1 = operate(v1)
    p2 = (a1 * scale - SHIFTS[1] * p1) * inside
    v2 = precondition(p2)
    mine = lambda x: x[NR : 2 * NR, :NC]
    half_a2 = mine(diag * v2 - 2.0 * (lon_shift(v2, 1) + lat_shift(v2, 1)))
    v0, v1, v2, a0, a1, r = (mine(x) for x in (v0, v1, v2, a0, a1, p0))
    v_out[0] = v0
    v_out[1] = v1
    v_out[2] = v2
    pairs = ((v0, a0), (v0, a1), (v2, a0), (v1, a1), (v2, a1), (v2, half_a2), (v0, r), (v1, r), (v2, r))
    copy = pltpu.make_async_copy(v_out, v_hbm, sem)
    copy.start()
    lane = lane_of((1, NC))
    line = jnp.zeros((1, NC), jnp.float32)
    for i, (x, y) in enumerate(pairs):
        total = jnp.sum(jnp.sum(x * y, axis=0, keepdims=True), axis=1, keepdims=True)
        line = line + jnp.where(lane == i, total, 0.0)
    dots_out[...] = jnp.broadcast_to(line[None], dots_out.shape)
    copy.wait()


def relay_kernel(got, out, held, spread, sems):
    copy = pltpu.make_async_copy(got, held, sems.at[0])
    copy.start()
    copy.wait()
    spread[...] = jnp.broadcast_to(jnp.sum(held[...], axis=0, keepdims=True), spread.shape)
    copy = pltpu.make_async_copy(spread, out, sems.at[1])
    copy.start()
    copy.wait()


def step_kernel(got, v, sf, out, held, sem):
    copy = pltpu.make_async_copy(got, held, sem)
    copy.start()
    copy.wait()
    line = jnp.sum(held[...], axis=0)
    lane = lane_of((1, NC))
    h00, h01, h02, h11, h12, h22, g0, g1, g2 = (
        jnp.sum(jnp.where(lane == i, line, 0.0), axis=1, keepdims=True) for i in range(9)
    )
    l1 = h01 / h00
    l2 = h02 / h00
    d1 = h11 - l1 * h01
    e12 = h12 - l1 * h02
    l3 = e12 / d1
    d2 = h22 - l2 * h02 - l3 * e12
    y1 = g1 - l1 * g0
    y2 = g2 - l2 * g0 - l3 * y1
    c2 = y2 / d2
    c1 = y1 / d1 - l3 * c2
    c0 = g0 / h00 - l1 * c1 - l2 * c2
    out[...] = sf[...] + c0 * v[0] + c1 * v[1] + c2 * v[2]


def row_masks():
    lane, row = lane_of((NR, NC)), row_of((NR, NC))
    return lane == NC - 1, lane == 0, row == NR - 1, row == 0


def spread_of(packed, lines):
    at_east, at_west, at_north, at_south = row_masks()

    def spread(k, flux_e, flux_n, i):
        side = pltpu.roll(packed[i], NC - 1 - 2 * k, 1)
        north = jnp.broadcast_to(lines[2 * i, pl.ds(k, 1), :], (NR, NC))
        south = jnp.broadcast_to(lines[2 * i + 1, pl.ds(k, 1), :], (NR, NC))
        flux_e = jnp.where(at_east, side, flux_e)
        flux_n = jnp.where(at_north, north, flux_n)
        back_e = jnp.where(at_west, side, pltpu.roll(flux_e, 1, 1))
        back_n = jnp.where(at_south, south, pltpu.roll(flux_n, 1, 0))
        return flux_e - back_e + (flux_n - back_n)

    return spread


def write_out(body, pairs, sems, unroll):
    per = NZ // CHUNKS
    copies = chunk_copies(pairs, sems)

    def chunk(c, carry):
        lax.fori_loop(0, per, lambda i, x: body(c * per + i, x), 0, unroll=unroll)
        for copy in copies(c):
            copy.start()
        return carry

    def finish(c, carry):
        for copy in copies(c):
            copy.wait()
        return carry

    lax.fori_loop(0, CHUNKS, chunk, 0)
    lax.fori_loop(0, CHUNKS, finish, 0)


def velocity_kernel(
    u, v, vi, w, lon, lon_a, lon_b, from_a, from_a2, from_b, from_b2,
    u_hbm, v_hbm, u_out, v_out, packed, lines, sems,
):
    is_east = lane_of((NR, NC)) % 2 == 0
    own = [lon[i] for i in range(4)]
    other = [beyond(lon_a[i], lon_b[i]) for i in range(4)]
    for i, grad in enumerate(face_in(own, other)):
        packed[i] = DT_VISC * jnp.where(is_east, grad, -grad)
    even = even_lat()
    exists = b_exists()
    mine, theirs = halves()
    for first, there_a, there_b in ((mine, from_a2, from_b2), (theirs, from_a, from_b)):
        at = pl.ds(first, HALF)
        for side in range(2):
            use_a = even if side == 0 else jnp.logical_not(even)
            here = [edge_row(ref, side == 0, 0, first, HALF) for ref in (u, v, vi, w)]
            there = [jnp.where(use_a, there_a[i], there_b[i] * exists) for i in range(4)]
            sign = DT_VISC if side == 0 else -DT_VISC
            for i, grad in enumerate(face_in(here, there)):
                lines[2 * i + side, at, :] = sign * grad
    spread = spread_of(packed, lines)
    lon_up = lambda x: pltpu.roll(x, NC - 1, 1)
    lat_up = lambda x: pltpu.roll(x, NR - 1, 0)

    def body(k, carry):
        at = level(k)
        uu, vv, visc = u[at, :], v[at, :], vi[at, :]
        wet = w[at, :].astype(jnp.float32)
        half = wet * (0.5 * DT_VISC)
        face_e = (visc + lon_up(visc)) * (half * lon_up(wet))
        face_n = (visc + lat_up(visc)) * (half * lat_up(wet))
        u_out[at, :] = wet * (uu + spread(k, face_e * (lon_up(uu) - uu), face_n * (lat_up(uu) - uu), 0))
        v_out[at, :] = wet * (vv + spread(k, face_e * (lon_up(vv) - vv), face_n * (lat_up(vv) - vv), 1))
        return carry

    write_out(body, ((u_out, u_hbm), (v_out, v_hbm)), sems, 8)


def tracer_kernel(
    t, u, v, w, lon, lon_a, lon_b, msg, msg_a, msg_b, from_a, from_a2, from_b, from_b2,
    t_hbm, t_out, packed, lines, sems,
):
    is_east = lane_of((NR, NC)) % 2 == 0
    by = DT_ADV / 12.0
    packed[1] = beyond(msg_a[40:56, :], msg_b[40:56, :])
    far = msg[56:72, :] + beyond(msg_a[56:72, :], msg_b[56:72, :])
    speed = jnp.where(is_east, lon[0], beyond(lon_a[0], lon_b[0]))
    packed[0] = speed * far * (by * lon[3] * beyond(lon_a[3], lon_b[3]))
    even = even_lat()
    exists = b_exists()
    mine, theirs = halves()
    for first, there_a, there_b in ((mine, from_a2, from_b2), (theirs, from_a, from_b)):
        at = pl.ds(first, HALF)
        part = first // HALF
        for side in range(2):
            north = side == 0
            use_a = even if north else jnp.logical_not(even)
            wet_here = edge_row(w, north, 0, first, HALF)
            wet_there = jnp.where(use_a, there_a[3], there_b[3] * exists)
            near = edge_row(t, north, 0, first, HALF) * wet_here
            inner = edge_row(t, north, 1, first, HALF) * edge_row(w, north, 1, first, HALF)
            far = jnp.where(use_a, from_a2[6 + part], from_b2[6 + part]) + (7.0 * near - inner)
            if north:
                speed = edge_row(v, True, 0, first, HALF)
            else:
                speed = jnp.where(use_a, there_a[1], there_b[1])
            lines[side, at, :] = speed * far * (by * wet_here * wet_there)
            lines[2 + side, at, :] = jnp.where(use_a, from_a2[4 + part], from_b2[4 + part] * exists)
    spread = spread_of(packed, lines)
    at_east, at_west, at_north, at_south = row_masks()
    lon_up = lambda x: pltpu.roll(x, NC - 1, 1)
    lat_up = lambda x: pltpu.roll(x, NR - 1, 0)

    def body(k, carry):
        at = level(k)
        tt = t[at, :]
        wet = w[at, :].astype(jnp.float32)
        wt = tt * wet
        side = pltpu.roll(packed[1], NC - 1 - 2 * k, 1)
        north = jnp.broadcast_to(lines[2, pl.ds(k, 1), :], (NR, NC))
        south = jnp.broadcast_to(lines[3, pl.ds(k, 1), :], (NR, NC))
        t_e = jnp.where(at_east, side, lon_up(wt))
        t_w = jnp.where(at_west, side, pltpu.roll(wt, 1, 1))
        t_n = jnp.where(at_north, north, lat_up(wt))
        t_s = jnp.where(at_south, south, pltpu.roll(wt, 1, 0))
        part = by * wet
        flux_e = u[at, :] * (7.0 * (wt + t_e) - (t_w + lon_up(t_e))) * (part * lon_up(wet))
        flux_n = v[at, :] * (7.0 * (wt + t_n) - (t_s + lat_up(t_n))) * (part * lat_up(wet))
        t_out[at, :] = wet * (tt - spread(k, flux_e, flux_n, 0))
        return carry

    write_out(body, ((t_out, t_hbm),), sems, 8)


def local(tracer, east_vel, north_vel, viscosity, land_sea, thickness, surface, surface_diag, precond_kernel):
    flat = (NZ * NR, NC)
    u, v, vi, w, t = (x.reshape(flat) for x in (east_vel, north_vel, viscosity, land_sea, tracer))
    block = NZ * NR * NC * 4
    field = pltpu.VMEM(flat, jnp.float32)
    wets = pltpu.VMEM(flat, jnp.int32)
    dma = pltpu.SemaphoreType.DMA
    rows = (4, HALF, NC)
    lon, a, b, late_a, late_b, inner, th = call(
        fetch_kernel,
        [(4, NR, NC), rows, rows, rows, rows, (2, NR, NC), (NZ + 8, NC)],
        [HBM] * 5,
        50 * NZ * NR * NC,
        4 * block,
        [field] * 3 + [wets, pltpu.SMEM((NZ,), jnp.float32), dma((CHUNKS, 4)), dma],
        vmem=FETCH_VMEM,
    )(thickness, u, v, vi, w)
    from_b = lax.ppermute(b, LAT, SWAP_B)
    from_a = lax.ppermute(a, LAT, SWAP_A)
    lon_b = lax.ppermute(lon, LON, SWAP_B)
    lon_a = lax.ppermute(lon, LON, SWAP_A)
    lon2, a2, b2, taps = call(
        late_kernel,
        [(2, NR, NC), (8, HALF, NC), (8, HALF, NC), (32, 2 * NC)],
        [SM] + [HBM] * 2 + [VM] * 2,
        20 * NZ * NR * NC,
        2 * block,
        [field, wets, dma((CHUNKS, 2))],
        vmem=FETCH_VMEM,
    )(precond_kernel, t, w, late_a, late_b)
    (msg,) = call(join_kernel, [(MSG, NC)], [VM] * 12, 10**6, 10**6)(
        inner, lon, lon_a, lon_b, lon2, late_a, from_a, late_b, from_b, th, surface, surface_diag
    )
    msg, a2, b2 = lax.optimization_barrier((msg, a2, b2))
    msg_b = lax.ppermute(msg, LON, SWAP_B)
    msg_a = lax.ppermute(msg, LON, SWAP_A)
    from_b2 = lax.ppermute(b2, LAT, SWAP_B)
    from_a2 = lax.ppermute(a2, LAT, SWAP_A)
    wide = (NR, 2 * NC)
    rest, dg, edge, side_a, side_b = call(
        side_kernel, [wide, wide, (8, 2 * NC), wide, wide], [VM] * 3, 10**6, 10**5
    )(msg, msg_a, msg_b)
    got_b = lax.ppermute(side_b, LAT, SWAP_B)
    got_a = lax.ppermute(side_a, LAT, SWAP_A)
    lat = (from_a, from_a2, from_b, from_b2)
    u_new, v_new = call(
        velocity_kernel,
        [flat] * 2,
        [VM] * 11,
        60 * NZ * NR * NC,
        6 * block,
        [field] * 2
        + [pltpu.VMEM((2, NR, NC), jnp.float32), pltpu.VMEM((4, NZ, NC), jnp.float32), dma((CHUNKS, 2))],
        HBM,
    )(u, v, vi, w, lon, lon_a, lon_b, *lat)
    got_a, got_b, u_new, v_new = lax.optimization_barrier((got_a, got_b, u_new, v_new))
    t_new = call(
        tracer_kernel,
        [flat],
        [VM] * 14,
        60 * NZ * NR * NC,
        5 * block,
        [field, pltpu.VMEM((2, NR, NC), jnp.float32), pltpu.VMEM((4, NZ, NC), jnp.float32), dma((CHUNKS, 1))],
        HBM,
    )(t, u, v, w, lon, lon_a, lon_b, msg, msg_a, msg_b, *lat)[0]
    vecs, dots = call(
        solve_kernel,
        [(3, NR, NC), (32, 1, NC)],
        [VM] * 6,
        10**6,
        10**5,
        [pltpu.VMEM((3, NR, NC), jnp.float32), dma],
        [HBM, VM],
    )(taps, rest, dg, edge, got_a, got_b)
    dots = lax.all_to_all(dots, ("x", "y", "c"), 0, 0)
    dots, t_new = lax.optimization_barrier((dots, t_new))
    (dots,) = call(
        relay_kernel,
        [(8, 1, NC)],
        [HBM],
        10**4,
        10**4,
        [pltpu.VMEM((32, 1, NC), jnp.float32), pltpu.VMEM((8, 1, NC), jnp.float32), dma((2,))],
        HBM,
    )(dots)
    dots = lax.all_to_all(dots, ("zl", "zh"), 0, 0)
    (surface_new,) = call(
        step_kernel,
        [(NR, NC)],
        [HBM] + [VM] * 2,
        10**5,
        10**4,
        [pltpu.VMEM((8, 1, NC), jnp.float32), dma],
    )(dots, vecs, surface)
    shape = (NZ, NR, NC)
    return t_new.reshape(shape), u_new.reshape(shape), v_new.reshape(shape), surface_new


def solution(mesh):
    sizes = dict(mesh.shape)
    assert sizes == {"lon": 16, "lat": 16} and tuple(mesh.axis_names) == ("lon", "lat")
    fine = Mesh(mesh.devices.reshape(2, 4, 2, 4, 4), ("zl", "x", "c", "y", "zh"))
    deep = P(None, LAT, LON)
    flat = P(LAT, LON)
    return jax.shard_map(
        local,
        mesh=fine,
        in_specs=(deep,) * 5 + (P(), flat, flat, P()),
        out_specs=(deep, deep, deep, flat),
        check_vma=False,
    )
```

```python
import functools

import jax
import jax.numpy as jnp
from jax import lax
from jax.experimental import pallas as pl
from jax.experimental.pallas import tpu as pltpu
from jax.sharding import Mesh
from jax.sharding import PartitionSpec as P

DT_ADV = 0.25
DT_VISC = 0.2
TAU = 0.05
SHIFTS = (0.3, 1.3)

LON = ("zl", "x", "c")
LAT = ("y", "zh")
NZ, NR, NC = 64, 16, 128
SWAP_A = [(i, i ^ 1) for i in range(16)]
SWAP_B = [(i, (i + 1) % 16 if i % 2 else (i - 1) % 16) for i in range(16)]

VM = pl.BlockSpec(memory_space=pltpu.VMEM)
SM = pl.BlockSpec(memory_space=pltpu.SMEM)
HBM = pl.BlockSpec(memory_space=pltpu.HBM)
FETCH_VMEM = 53.25
FETCH_UNROLL = 4


def call(kernel, outs, specs, flops, nbytes, scratch=(), place=VM, vmem=4, aliases=None):
    return pl.pallas_call(
        kernel,
        out_shape=[jax.ShapeDtypeStruct(s, jnp.float32) for s in outs],
        in_specs=specs,
        out_specs=place if isinstance(place, list) else [place] * len(outs),
        scratch_shapes=list(scratch),
        input_output_aliases=aliases or {},
        compiler_params=pltpu.CompilerParams(vmem_limit_bytes=int(vmem * 1024 * 1024)),
        cost_estimate=pl.CostEstimate(flops=flops, bytes_accessed=nbytes, transcendentals=0),
    )


def lane_of(shape):
    return lax.broadcasted_iota(jnp.int32, shape, len(shape) - 1)


def row_of(shape):
    return lax.broadcasted_iota(jnp.int32, shape, len(shape) - 2)


def even_lon():
    return lax.axis_index("c") == 0


def even_lat():
    return lax.axis_index("zh") % 2 == 0


def lat_index():
    return lax.axis_index("y") * 4 + lax.axis_index("zh")


def b_exists():
    lat = lat_index()
    return jnp.where(jnp.logical_or(lat == 0, lat == 15), 0.0, 1.0).astype(jnp.float32)


HALF = NZ // 2
CHUNKS = 4


def halves():
    mine = jnp.where(even_lat(), 0, HALF)
    return pl.multiple_of(mine, HALF), pl.multiple_of(HALF - mine, HALF)


def edge_row(ref, north, inwards, first, count):
    if isinstance(north, bool):
        row = NR - 1 - inwards if north else inwards
    else:
        row = jnp.where(north, NR - 1 - inwards, inwards)
    return ref[pl.ds(first * NR + row, count, stride=NR), :].astype(jnp.float32)


def pipeline(copies, body, acc, unroll):
    per = NZ // CHUNKS

    def start(c, carry):
        for copy in copies(c):
            copy.start()
        return carry

    def chunk(c, carry):
        for copy in copies(c):
            copy.wait()
        return lax.fori_loop(0, per, lambda i, x: body(c * per + i, x), carry, unroll=unroll)

    lax.fori_loop(0, CHUNKS, start, 0)
    return lax.fori_loop(0, CHUNKS, chunk, acc)


def chunk_copies(pairs, sems):
    span = NZ * NR // CHUNKS

    def copies(c):
        at = pl.ds(pl.multiple_of(c * span, span), span)
        return [
            pltpu.make_async_copy(src.at[at], dst.at[at], sems.at[c, i])
            for i, (src, dst) in enumerate(pairs)
        ]

    return copies


def level(k):
    return pl.ds(pl.multiple_of(k * NR, NR), NR)


def fetch_kernel(
    thick_hbm, u, v, vi, land, t,
    lon_out, a_out, b_out, late_a, late_b, out, th_out, uo, vo, vio, lo, to, thick, sems, th_sem,
):
    lane, row = lane_of((NR, NC)), row_of((NR, NC))
    pair = lane // 2
    half_lane = lane < NC // 2
    up = lambda x: pltpu.roll(x, NC - 1, 1)
    north_of = lambda x: pltpu.roll(x, NR - 1, 0)

    def body(k, acc):
        at = level(k)
        wet, uu, vv, visc = lo[at, :].astype(jnp.float32), uo[at, :], vo[at, :], vio[at, :]
        mine = pair == k
        first = to[at, :] * wet
        inner = jnp.where(half_lane, up(first), pltpu.roll(first, 1, 1))
        packed = tuple(
            jnp.where(mine, pltpu.roll(x, 2 * k + 1, 1), old)
            for x, old in zip((uu, vv, visc, wet, first, 7.0 * first - inner), acc[:6])
        )
        th = jnp.full((1, NC), thick[k], jnp.float32)
        th_out[pl.ds(k, 1), :] = th
        own = wet * th
        half = 0.5 * own
        east = (visc + up(visc)) * (half * up(wet))
        north = (visc + north_of(visc)) * (half * north_of(wet))
        return packed + (
            acc[6] + own * uu,
            acc[7] + east * (up(uu) - uu),
            acc[8] + north * (north_of(uu) - uu),
            acc[9] + own * vv,
            acc[10] + east * (up(vv) - vv),
            acc[11] + north * (north_of(vv) - vv),
            jnp.where(mine[:1], th, acc[12]),
        )

    thick_copy = pltpu.make_async_copy(thick_hbm, thick, th_sem)
    thick_copy.start()
    copies = chunk_copies(((u, uo), (v, vo), (vi, vio), (land, lo), (t, to)), sems)
    thick_copy.wait()
    zero = jnp.zeros((NR, NC), jnp.float32)
    acc = pipeline(copies, body, (zero,) * 12 + (zero[:1],), FETCH_UNROLL)
    for i in range(6):
        lon_out[i] = acc[i]
    th_out[NZ:, :] = jnp.broadcast_to(acc[12], (8, NC))
    for i in range(2):
        east = jnp.where(lane == NC - 1, 0.0, acc[3 * i + 7])
        north = jnp.where(row == NR - 1, 0.0, acc[3 * i + 8])
        out[i] = acc[3 * i + 6] + DT_VISC * (
            east - pltpu.roll(east, 1, 1) + north - pltpu.roll(north, 1, 0)
        )
    even = even_lat()
    mine, theirs = halves()
    for north, first, rest in ((even, a_out, late_a), (jnp.logical_not(even), b_out, late_b)):
        for i, ref in enumerate((uo, vo, vio, lo)):
            first[i] = edge_row(ref, north, 0, mine, HALF)
            rest[i] = edge_row(ref, north, 0, theirs, HALF)
        for i in range(2):
            near, inner = (
                edge_row(to, north, n, i * HALF, HALF) * edge_row(lo, north, n, i * HALF, HALF)
                for n in range(2)
            )
            rest[4 + i] = near
            rest[6 + i] = 7.0 * near - inner


def taps_kernel(pc, out):
    for i in range(25):
        out[i : i + 1, :] = jnp.full((1, 2 * NC), pc[i // 5, i % 5], jnp.float32)


def lon_sides(first, second):
    even = even_lon()
    return jnp.where(even, first, second), jnp.where(even, second, first)


def beyond(from_a, from_b):
    east, west = lon_sides(from_a, from_b)
    is_east = lane_of((NR, NC)) % 2 == 0
    return jnp.where(is_east, pltpu.roll(east, NC - 1, 1), pltpu.roll(west, 1, 1))


def face_in(own, other):
    face = 0.5 * (own[2] + other[2]) * (own[3] * other[3])
    return face * (other[0] - own[0]), face * (other[1] - own[1])


MSG = 72


def join_kernel(inner, lon, lon_a, lon_b, a2, from_a, b2, from_b, th, sf, dg, out):
    lane = lane_of((NR, NC))
    own = [lon[i] for i in range(4)]
    other = [beyond(lon_a[i], lon_b[i]) for i in range(4)]
    is_east = lane % 2 == 0
    for i, grad in enumerate(face_in(own, other)):
        grad = grad * th[NZ : NZ + 1, :]
        east = jnp.sum(jnp.where(is_east, grad, 0.0), axis=1, keepdims=True)
        west = jnp.sum(jnp.where(is_east, 0.0, grad), axis=1, keepdims=True)
        add = jnp.where(lane == NC - 1, east, 0.0) + jnp.where(lane == 0, west, 0.0)
        out[NR * i : NR * (i + 1), :] = inner[i] + DT_VISC * add
    _, theirs = halves()
    weight = DT_VISC * th[pl.ds(theirs, HALF), :]
    lat_a = face_in([a2[i] for i in range(4)], [from_a[i] for i in range(4)])
    weight_b = weight * b_exists()
    lat_b = face_in([b2[i] for i in range(4)], [from_b[i] for i in range(4)])
    sums = [jnp.sum(x * weight, axis=0, keepdims=True) for x in lat_a]
    sums += [jnp.sum(x * weight_b, axis=0, keepdims=True) for x in lat_b]
    out[2 * NR : 2 * NR + 8, :] = jnp.concatenate(sums + [jnp.zeros((4, NC), jnp.float32)], axis=0)
    out[40:56, :] = sf[...]
    out[56:72, :] = dg[...]


def side_kernel(msg, msg_a, msg_b, rest_out, diag_out, edge_out, a_out, b_out):
    def widen(own, first, second):
        east, west = lon_sides(first, second)
        halo = jnp.where(lane_of(own.shape) < NC // 2, east, west)
        return jnp.concatenate([own, halo], axis=1)

    part = lambda lo, hi: widen(msg[lo:hi, :], msg_a[lo:hi, :], msg_b[lo:hi, :])
    te, tn, faces = part(0, NR), part(NR, 2 * NR), part(2 * NR, 2 * NR + 8)
    sf, dg = part(40, 56), part(56, 72)
    row = row_of((NR, 2 * NC))
    even = even_lat()
    north_u, north_v = (jnp.where(even, faces[i : i + 1], faces[i + 2 : i + 3]) for i in range(2))
    south_u, south_v = (jnp.where(even, faces[i + 2 : i + 3], faces[i : i + 1]) for i in range(2))
    at_north, at_south = row == NR - 1, row == 0
    te = te + jnp.where(at_north, north_u, 0.0) + jnp.where(at_south, south_u, 0.0)
    tn = tn + jnp.where(at_north, north_v, 0.0) + jnp.where(at_south, south_v, 0.0)
    east = lambda x: pltpu.roll(x, 2 * NC - 1, 1)
    west = lambda x: pltpu.roll(x, 1, 1)
    north = lambda x: jnp.where(at_north, 0.0, pltpu.roll(x, NR - 1, 0))
    south = lambda x: jnp.where(at_south, 0.0, pltpu.roll(x, 1, 0))
    across = lambda fu, fv: TAU * (fu - west(fu) + fv)
    rest = sf - TAU * (te - west(te) + tn - south(tn))
    rest = rest - ((4.0 + dg) * sf - (east(sf) + west(sf) + north(sf) + south(sf)))
    rest = rest - jnp.where(at_south, TAU * south_v, 0.0)
    rest_out[...] = rest
    diag_out[...] = dg
    first = TAU * tn[NR - 1 :] + sf[NR - 1 :] + across(north_u, north_v)
    second = -TAU * north_v
    to_south = sf[:1] + across(south_u, south_v)
    zero = jnp.zeros((5, 2 * NC), jnp.float32)
    edge_out[...] = jnp.concatenate([first, second, to_south, zero], axis=0)
    msg_north = jnp.concatenate([rest[8:], dg[11:], first, second, zero[:1]], axis=0)
    msg_south = jnp.concatenate([rest[:9], dg[:6], to_south], axis=0)
    a_out[...] = jnp.where(even, msg_north, msg_south)
    b_out[...] = jnp.where(even, msg_south, msg_north)


def solve_kernel(pc, rest, dg, edge, from_a, from_b, v_hbm, dots_out, v_out, sem):
    rows, wide = 3 * NR, 2 * NC
    even = even_lat()
    exists = b_exists()
    msg_a = from_a[...]
    msg_b = from_b[...] * exists
    north = jnp.where(even, msg_a, msg_b)
    south = jnp.where(even, msg_b, msg_a)
    zeros = lambda n: jnp.zeros((n, wide), jnp.float32)
    row = row_of((rows, wide))
    lat = lat_index()
    low = jnp.where(lat == 0, NR, 0)
    high = jnp.where(lat == 15, 2 * NR, 3 * NR)
    inside = jnp.where(jnp.logical_and(row >= low, row < high), 1.0, 0.0).astype(jnp.float32)
    below = jnp.concatenate([zeros(8), south[:7], south[7:8] + edge[2:3]], axis=0)
    above = jnp.concatenate(
        [north[:1] + edge[0:1], north[1:2] + edge[1:2], north[2:9], zeros(7)], axis=0
    )
    own = rest[...] + jnp.concatenate([south[13:15], zeros(13), north[15:]], axis=0)
    res = jnp.concatenate([below, own, above], axis=0) * inside
    diag = 4.0 + jnp.concatenate([zeros(11), south[8:13], dg[...], north[9:15], zeros(10)], axis=0)

    def lon_shift(x, n):
        return x if n == 0 else pltpu.roll(x, (-n) % wide, 1)

    def lat_shift(x, n):
        return x if n == 0 else pltpu.roll(x, (-n) % rows, 0)

    def operate(x):
        near = lon_shift(x, 1) + lon_shift(x, -1) + lat_shift(x, 1) + lat_shift(x, -1)
        return diag * x - near

    def tap(a, b):
        at = 5 * (a + 2) + b + 2
        return pc[at : at + 1, :]

    def precondition(x):
        moved = [lon_shift(x, b) for b in range(-2, 3)]
        total = None
        for a in range(-2, 3):
            line = tap(a, -2) * moved[0]
            for b in range(1, 5):
                line = line + tap(a, b - 2) * moved[b]
            line = lat_shift(line, a)
            total = line if total is None else total + line
        return total * inside

    scale = 1.0 / (5.0 * tap(0, 0))
    p0 = res
    v0 = precondition(p0)
    a0 = operate(v0)
    p1 = (a0 * scale - SHIFTS[0] * p0) * inside
    v1 = precondition(p1)
    a1 = operate(v1)
    p2 = (a1 * scale - SHIFTS[1] * p1) * inside
    v2 = precondition(p2)
    mine = lambda x: x[NR : 2 * NR, :NC]
    half_a2 = mine(diag * v2 - 2.0 * (lon_shift(v2, 1) + lat_shift(v2, 1)))
    v0, v1, v2, a0, a1, r = (mine(x) for x in (v0, v1, v2, a0, a1, p0))
    v_out[0] = v0
    v_out[1] = v1
    v_out[2] = v2
    pairs = ((v0, a0), (v0, a1), (v2, a0), (v1, a1), (v2, a1), (v2, half_a2), (v0, r), (v1, r), (v2, r))
    copy = pltpu.make_async_copy(v_out, v_hbm, sem)
    copy.start()
    lane = lane_of((1, NC))
    line = jnp.zeros((1, NC), jnp.float32)
    for i, (x, y) in enumerate(pairs):
        total = jnp.sum(jnp.sum(x * y, axis=0, keepdims=True), axis=1, keepdims=True)
        line = line + jnp.where(lane == i, total, 0.0)
    dots_out[...] = jnp.broadcast_to(line[None], dots_out.shape)
    copy.wait()


def relay_kernel(got, out, held, spread, sems):
    copy = pltpu.make_async_copy(got, held, sems.at[0])
    copy.start()
    copy.wait()
    spread[...] = jnp.broadcast_to(jnp.sum(held[...], axis=0, keepdims=True), spread.shape)
    copy = pltpu.make_async_copy(spread, out, sems.at[1])
    copy.start()
    copy.wait()


def step_kernel(got, v, sf, out, held, sem):
    copy = pltpu.make_async_copy(got, held, sem)
    copy.start()
    copy.wait()
    line = jnp.sum(held[...], axis=0)
    lane = lane_of((1, NC))
    h00, h01, h02, h11, h12, h22, g0, g1, g2 = (
        jnp.sum(jnp.where(lane == i, line, 0.0), axis=1, keepdims=True) for i in range(9)
    )
    l1 = h01 / h00
    l2 = h02 / h00
    d1 = h11 - l1 * h01
    e12 = h12 - l1 * h02
    l3 = e12 / d1
    d2 = h22 - l2 * h02 - l3 * e12
    y1 = g1 - l1 * g0
    y2 = g2 - l2 * g0 - l3 * y1
    c2 = y2 / d2
    c1 = y1 / d1 - l3 * c2
    c0 = g0 / h00 - l1 * c1 - l2 * c2
    out[...] = sf[...] + c0 * v[0] + c1 * v[1] + c2 * v[2]


def row_masks():
    lane, row = lane_of((NR, NC)), row_of((NR, NC))
    return lane == NC - 1, lane == 0, row == NR - 1, row == 0


def spread_of(packed, lines):
    at_east, at_west, at_north, at_south = row_masks()

    def spread(k, flux_e, flux_n, i):
        side = pltpu.roll(packed[i], NC - 1 - 2 * k, 1)
        north = jnp.broadcast_to(lines[2 * i, pl.ds(k, 1), :], (NR, NC))
        south = jnp.broadcast_to(lines[2 * i + 1, pl.ds(k, 1), :], (NR, NC))
        flux_e = jnp.where(at_east, side, flux_e)
        flux_n = jnp.where(at_north, north, flux_n)
        back_e = jnp.where(at_west, side, pltpu.roll(flux_e, 1, 1))
        back_n = jnp.where(at_south, south, pltpu.roll(flux_n, 1, 0))
        return flux_e - back_e + (flux_n - back_n)

    return spread


def write_out(body, pairs, sems, unroll, first=0, count=NZ):
    per = NZ // CHUNKS
    all_copies = chunk_copies(pairs, sems)
    copies = lambda c: all_copies(first // per + c)

    def chunk(c, carry):
        lax.fori_loop(0, per, lambda i, x: body(first + c * per + i, x), 0, unroll=unroll)
        for copy in copies(c):
            copy.start()
        return carry

    def finish(c, carry):
        for copy in copies(c):
            copy.wait()
        return carry

    lax.fori_loop(0, count // per, chunk, 0)
    lax.fori_loop(0, count // per, finish, 0)


def velocity_kernel(early, u, v, vi, w, lon, lon_a, lon_b, from_a, from_b, *rest):
    u_hbm, v_hbm, u_out, v_out, packed, lines, sems = rest[0 if early else 2 :]
    is_east = lane_of((NR, NC)) % 2 == 0
    own = [lon[i] for i in range(4)]
    other = [beyond(lon_a[i], lon_b[i]) for i in range(4)]
    for i, grad in enumerate(face_in(own, other)):
        packed[i] = DT_VISC * jnp.where(is_east, grad, -grad)
    even = even_lat()
    exists = b_exists()
    mine, theirs = halves()
    first = theirs if early else mine
    at = pl.ds(first, HALF)
    for side in range(2):
        use_a = even if side == 0 else jnp.logical_not(even)
        here = [edge_row(ref, side == 0, 0, first, HALF) for ref in (u, v, vi, w)]
        there = [jnp.where(use_a, from_a[i], from_b[i] * exists) for i in range(4)]
        sign = DT_VISC if side == 0 else -DT_VISC
        for i, grad in enumerate(face_in(here, there)):
            lines[2 * i + side, at, :] = sign * grad
    spread = spread_of(packed, lines)
    lon_up = lambda x: pltpu.roll(x, NC - 1, 1)
    lat_up = lambda x: pltpu.roll(x, NR - 1, 0)

    def body(k, carry):
        at = level(k)
        uu, vv, visc = u[at, :], v[at, :], vi[at, :]
        wet = w[at, :].astype(jnp.float32)
        half = wet * (0.5 * DT_VISC)
        face_e = (visc + lon_up(visc)) * (half * lon_up(wet))
        face_n = (visc + lat_up(visc)) * (half * lat_up(wet))
        u_out[at, :] = wet * (uu + spread(k, face_e * (lon_up(uu) - uu), face_n * (lat_up(uu) - uu), 0))
        v_out[at, :] = wet * (vv + spread(k, face_e * (lon_up(vv) - vv), face_n * (lat_up(vv) - vv), 1))
        return carry

    write_out(body, ((u_out, u_hbm), (v_out, v_hbm)), sems, 8, first, HALF)


def tracer_kernel(
    t, u, v, w, lon, lon_a, lon_b, from_a, from_a2, from_b, from_b2,
    t_hbm, t_out, packed, lines, sems,
):
    is_east = lane_of((NR, NC)) % 2 == 0
    by = DT_ADV / 12.0
    packed[1] = beyond(lon_a[4], lon_b[4])
    far = lon[5] + beyond(lon_a[5], lon_b[5])
    speed = jnp.where(is_east, lon[0], beyond(lon_a[0], lon_b[0]))
    packed[0] = speed * far * (by * lon[3] * beyond(lon_a[3], lon_b[3]))
    even = even_lat()
    exists = b_exists()
    mine, theirs = halves()
    for first, there_a, there_b in ((mine, from_a2, from_b2), (theirs, from_a, from_b)):
        at = pl.ds(first, HALF)
        part = first // HALF
        for side in range(2):
            north = side == 0
            use_a = even if north else jnp.logical_not(even)
            wet_here = edge_row(w, north, 0, first, HALF)
            wet_there = jnp.where(use_a, there_a[3], there_b[3] * exists)
            near = edge_row(t, north, 0, first, HALF) * wet_here
            inner = edge_row(t, north, 1, first, HALF) * edge_row(w, north, 1, first, HALF)
            far = jnp.where(use_a, from_a2[6 + part], from_b2[6 + part]) + (7.0 * near - inner)
            if north:
                speed = edge_row(v, True, 0, first, HALF)
            else:
                speed = jnp.where(use_a, there_a[1], there_b[1])
            lines[side, at, :] = speed * far * (by * wet_here * wet_there)
            lines[2 + side, at, :] = jnp.where(use_a, from_a2[4 + part], from_b2[4 + part] * exists)
    spread = spread_of(packed, lines)
    at_east, at_west, at_north, at_south = row_masks()
    lon_up = lambda x: pltpu.roll(x, NC - 1, 1)
    lat_up = lambda x: pltpu.roll(x, NR - 1, 0)

    def body(k, carry):
        at = level(k)
        tt = t[at, :]
        wet = w[at, :].astype(jnp.float32)
        wt = tt * wet
        side = pltpu.roll(packed[1], NC - 1 - 2 * k, 1)
        north = jnp.broadcast_to(lines[2, pl.ds(k, 1), :], (NR, NC))
        south = jnp.broadcast_to(lines[3, pl.ds(k, 1), :], (NR, NC))
        t_e = jnp.where(at_east, side, lon_up(wt))
        t_w = jnp.where(at_west, side, pltpu.roll(wt, 1, 1))
        t_n = jnp.where(at_north, north, lat_up(wt))
        t_s = jnp.where(at_south, south, pltpu.roll(wt, 1, 0))
        part = by * wet
        flux_e = u[at, :] * (7.0 * (wt + t_e) - (t_w + lon_up(t_e))) * (part * lon_up(wet))
        flux_n = v[at, :] * (7.0 * (wt + t_n) - (t_s + lat_up(t_n))) * (part * lat_up(wet))
        t_out[at, :] = wet * (tt - spread(k, flux_e, flux_n, 0))
        return carry

    write_out(body, ((t_out, t_hbm),), sems, 8)


def local(tracer, east_vel, north_vel, viscosity, land_sea, thickness, surface, surface_diag, precond_kernel):
    flat = (NZ * NR, NC)
    u, v, vi, w, t = (x.reshape(flat) for x in (east_vel, north_vel, viscosity, land_sea, tracer))
    block = NZ * NR * NC * 4
    field = pltpu.VMEM(flat, jnp.float32)
    wets = pltpu.VMEM(flat, jnp.int32)
    dma = pltpu.SemaphoreType.DMA
    rows = (4, HALF, NC)
    late = (8, HALF, NC)
    lon, a, b, a2, b2, inner, th = call(
        fetch_kernel,
        [(6, NR, NC), rows, rows, late, late, (2, NR, NC), (NZ + 8, NC)],
        [HBM] * 6,
        50 * NZ * NR * NC,
        5 * block,
        [field] * 3 + [wets, field, pltpu.SMEM((NZ,), jnp.float32), dma((CHUNKS, 5)), dma],
        vmem=FETCH_VMEM,
    )(thickness, u, v, vi, w, t)
    from_b = lax.ppermute(b, LAT, SWAP_B)
    from_a = lax.ppermute(a, LAT, SWAP_A)
    lon_b = lax.ppermute(lon, LON, SWAP_B)
    lon_a = lax.ppermute(lon, LON, SWAP_A)
    (msg,) = call(join_kernel, [(MSG, NC)], [VM] * 11, 10**6, 10**6)(
        inner, lon, lon_a, lon_b, a2, from_a, b2, from_b, th, surface, surface_diag
    )
    msg_b = lax.ppermute(msg, LON, SWAP_B)
    msg_a = lax.ppermute(msg, LON, SWAP_A)
    wide = (NR, 2 * NC)
    rest, dg, edge, side_a, side_b = call(
        side_kernel, [wide, wide, (8, 2 * NC), wide, wide], [VM] * 3, 10**6, 10**5
    )(msg, msg_a, msg_b)
    got_b = lax.ppermute(side_b, LAT, SWAP_B)
    got_a = lax.ppermute(side_a, LAT, SWAP_A)
    (taps,) = call(taps_kernel, [(32, 2 * NC)], [SM], 10**4, 10**4)(precond_kernel)
    vecs, dots = call(
        solve_kernel,
        [(3, NR, NC), (32, 1, NC)],
        [VM] * 6,
        10**6,
        10**5,
        [pltpu.VMEM((3, NR, NC), jnp.float32), dma],
        [HBM, VM],
    )(taps, rest, dg, edge, got_a, got_b)
    def velocity(early, edges, written):
        return call(
            functools.partial(velocity_kernel, early),
            [flat] * 2,
            [VM] * 9 + [HBM] * len(written),
            30 * NZ * NR * NC,
            3 * block,
            [field] * 2
            + [pltpu.VMEM((2, NR, NC), jnp.float32), pltpu.VMEM((4, NZ, NC), jnp.float32), dma((CHUNKS, 2))],
            HBM,
            aliases={9 + i: i for i in range(len(written))},
        )(u, v, vi, w, lon, lon_a, lon_b, *edges, *written)

    dots, from_a, from_b = lax.optimization_barrier((dots, from_a, from_b))
    u_half, v_half = velocity(True, (from_a, from_b), ())
    dots, a2, b2 = lax.optimization_barrier((dots, a2, b2))
    from_b2 = lax.ppermute(b2, LAT, SWAP_B)
    from_a2 = lax.ppermute(a2, LAT, SWAP_A)
    dots = lax.all_to_all(dots, ("x", "y", "c"), 0, 0)
    dots, u_half, v_half = lax.optimization_barrier((dots, u_half, v_half))
    lat = (from_a, from_a2, from_b, from_b2)
    u_new, v_new = velocity(False, (from_a2, from_b2), (u_half, v_half))
    t_new = call(
        tracer_kernel,
        [flat],
        [VM] * 11,
        60 * NZ * NR * NC,
        5 * block,
        [field, pltpu.VMEM((2, NR, NC), jnp.float32), pltpu.VMEM((4, NZ, NC), jnp.float32), dma((CHUNKS, 1))],
        HBM,
    )(t, u, v, w, lon, lon_a, lon_b, *lat)[0]
    (dots,) = call(
        relay_kernel,
        [(8, 1, NC)],
        [HBM],
        10**4,
        10**4,
        [pltpu.VMEM((32, 1, NC), jnp.float32), pltpu.VMEM((8, 1, NC), jnp.float32), dma((2,))],
        HBM,
    )(dots)
    dots = lax.all_to_all(dots, ("zl", "zh"), 0, 0)
    dots, t_new, u_new, v_new = lax.optimization_barrier((dots, t_new, u_new, v_new))
    (surface_new,) = call(
        step_kernel,
        [(NR, NC)],
        [HBM] + [VM] * 2,
        10**5,
        10**4,
        [pltpu.VMEM((8, 1, NC), jnp.float32), dma],
    )(dots, vecs, surface)
    shape = (NZ, NR, NC)
    return t_new.reshape(shape), u_new.reshape(shape), v_new.reshape(shape), surface_new


def solution(mesh):
    sizes = dict(mesh.shape)
    assert sizes == {"lon": 16, "lat": 16} and tuple(mesh.axis_names) == ("lon", "lat")
    fine = Mesh(mesh.devices.reshape(2, 4, 2, 4, 4), ("zl", "x", "c", "y", "zh"))
    deep = P(None, LAT, LON)
    flat = P(LAT, LON)
    return jax.shard_map(
        local,
        mesh=fine,
        in_specs=(deep,) * 5 + (P(), flat, flat, P()),
        out_specs=(deep, deep, deep, flat),
        check_vma=False,
    )
```

```python
import functools

import jax
import jax.numpy as jnp
from jax import lax
from jax.experimental import pallas as pl
from jax.experimental.pallas import tpu as pltpu
from jax.sharding import Mesh
from jax.sharding import PartitionSpec as P

DT_ADV = 0.25
DT_VISC = 0.2
TAU = 0.05
SHIFTS = (0.3, 1.3)

LON = ("zl", "x", "c")
LAT = ("y", "zh")
NZ, NR, NC = 64, 16, 128
SWAP_A = [(i, i ^ 1) for i in range(16)]
SWAP_B = [(i, (i + 1) % 16 if i % 2 else (i - 1) % 16) for i in range(16)]

VM = pl.BlockSpec(memory_space=pltpu.VMEM)
SM = pl.BlockSpec(memory_space=pltpu.SMEM)
HBM = pl.BlockSpec(memory_space=pltpu.HBM)
FETCH_VMEM = 53.25
FETCH_UNROLL = 4


def call(kernel, outs, specs, flops, nbytes, scratch=(), place=VM, vmem=4, aliases=None):
    return pl.pallas_call(
        kernel,
        out_shape=[jax.ShapeDtypeStruct(s, jnp.float32) for s in outs],
        in_specs=specs,
        out_specs=place if isinstance(place, list) else [place] * len(outs),
        scratch_shapes=list(scratch),
        input_output_aliases=aliases or {},
        compiler_params=pltpu.CompilerParams(vmem_limit_bytes=int(vmem * 1024 * 1024)),
        cost_estimate=pl.CostEstimate(flops=flops, bytes_accessed=nbytes, transcendentals=0),
    )


def lane_of(shape):
    return lax.broadcasted_iota(jnp.int32, shape, len(shape) - 1)


def row_of(shape):
    return lax.broadcasted_iota(jnp.int32, shape, len(shape) - 2)


def even_lon():
    return lax.axis_index("c") == 0


def even_lat():
    return lax.axis_index("zh") % 2 == 0


def lat_index():
    return lax.axis_index("y") * 4 + lax.axis_index("zh")


def b_exists():
    lat = lat_index()
    return jnp.where(jnp.logical_or(lat == 0, lat == 15), 0.0, 1.0).astype(jnp.float32)


HALF = NZ // 2
CHUNKS = 4


def halves():
    mine = jnp.where(even_lat(), 0, HALF)
    return pl.multiple_of(mine, HALF), pl.multiple_of(HALF - mine, HALF)


def edge_row(ref, north, inwards, first, count):
    if isinstance(north, bool):
        row = NR - 1 - inwards if north else inwards
    else:
        row = jnp.where(north, NR - 1 - inwards, inwards)
    return ref[pl.ds(first * NR + row, count, stride=NR), :].astype(jnp.float32)


def pipeline(copies, body, acc, unroll):
    per = NZ // CHUNKS

    def start(c, carry):
        for copy in copies(c):
            copy.start()
        return carry

    def chunk(c, carry):
        for copy in copies(c):
            copy.wait()
        return lax.fori_loop(0, per, lambda i, x: body(c * per + i, x), carry, unroll=unroll)

    lax.fori_loop(0, CHUNKS, start, 0)
    return lax.fori_loop(0, CHUNKS, chunk, acc)


def chunk_copies(pairs, sems):
    span = NZ * NR // CHUNKS

    def copies(c):
        at = pl.ds(pl.multiple_of(c * span, span), span)
        return [
            pltpu.make_async_copy(src.at[at], dst.at[at], sems.at[c, i])
            for i, (src, dst) in enumerate(pairs)
        ]

    return copies


def level(k):
    return pl.ds(pl.multiple_of(k * NR, NR), NR)


def fetch_kernel(
    thick_hbm, u, v, vi, land, t,
    lon_out, a_out, b_out, late_a, late_b, out, th_out, uo, vo, vio, lo, to, thick, sems, th_sem,
):
    lane, row = lane_of((NR, NC)), row_of((NR, NC))
    pair = lane // 2
    half_lane = lane < NC // 2
    up = lambda x: pltpu.roll(x, NC - 1, 1)
    north_of = lambda x: pltpu.roll(x, NR - 1, 0)

    def body(k, acc):
        at = level(k)
        wet, uu, vv, visc = lo[at, :].astype(jnp.float32), uo[at, :], vo[at, :], vio[at, :]
        mine = pair == k
        first = to[at, :] * wet
        inner = jnp.where(half_lane, up(first), pltpu.roll(first, 1, 1))
        packed = tuple(
            jnp.where(mine, pltpu.roll(x, 2 * k + 1, 1), old)
            for x, old in zip((uu, vv, visc, wet, first, 7.0 * first - inner), acc[:6])
        )
        th = jnp.full((1, NC), thick[k], jnp.float32)
        th_out[pl.ds(k, 1), :] = th
        own = wet * th
        half = 0.5 * own
        east = (visc + up(visc)) * (half * up(wet))
        north = (visc + north_of(visc)) * (half * north_of(wet))
        return packed + (
            acc[6] + own * uu,
            acc[7] + east * (up(uu) - uu),
            acc[8] + north * (north_of(uu) - uu),
            acc[9] + own * vv,
            acc[10] + east * (up(vv) - vv),
            acc[11] + north * (north_of(vv) - vv),
            jnp.where(mine[:1], th, acc[12]),
        )

    thick_copy = pltpu.make_async_copy(thick_hbm, thick, th_sem)
    thick_copy.start()
    copies = chunk_copies(((u, uo), (v, vo), (vi, vio), (land, lo), (t, to)), sems)
    thick_copy.wait()
    zero = jnp.zeros((NR, NC), jnp.float32)
    acc = pipeline(copies, body, (zero,) * 12 + (zero[:1],), FETCH_UNROLL)
    for i in range(6):
        lon_out[i] = acc[i]
    th_out[NZ:, :] = jnp.broadcast_to(acc[12], (8, NC))
    for i in range(2):
        east = jnp.where(lane == NC - 1, 0.0, acc[3 * i + 7])
        north = jnp.where(row == NR - 1, 0.0, acc[3 * i + 8])
        out[i] = acc[3 * i + 6] + DT_VISC * (
            east - pltpu.roll(east, 1, 1) + north - pltpu.roll(north, 1, 0)
        )
    even = even_lat()
    mine, theirs = halves()
    for north, first, rest in ((even, a_out, late_a), (jnp.logical_not(even), b_out, late_b)):
        for i, ref in enumerate((uo, vo, vio, lo)):
            first[i] = edge_row(ref, north, 0, mine, HALF)
            rest[i] = edge_row(ref, north, 0, theirs, HALF)
        for i in range(2):
            near, inner = (
                edge_row(to, north, n, i * HALF, HALF) * edge_row(lo, north, n, i * HALF, HALF)
                for n in range(2)
            )
            rest[4 + i] = near
            rest[6 + i] = 7.0 * near - inner


def taps_kernel(pc, out):
    for i in range(25):
        out[i : i + 1, :] = jnp.full((1, 2 * NC), pc[i // 5, i % 5], jnp.float32)


def lon_sides(first, second):
    even = even_lon()
    return jnp.where(even, first, second), jnp.where(even, second, first)


def beyond(from_a, from_b):
    east, west = lon_sides(from_a, from_b)
    is_east = lane_of((NR, NC)) % 2 == 0
    return jnp.where(is_east, pltpu.roll(east, NC - 1, 1), pltpu.roll(west, 1, 1))


def face_in(own, other):
    face = 0.5 * (own[2] + other[2]) * (own[3] * other[3])
    return face * (other[0] - own[0]), face * (other[1] - own[1])


MSG = 72


def join_kernel(inner, lon, lon_a, lon_b, a2, from_a, b2, from_b, th, sf, dg, out):
    lane = lane_of((NR, NC))
    own = [lon[i] for i in range(4)]
    other = [beyond(lon_a[i], lon_b[i]) for i in range(4)]
    is_east = lane % 2 == 0
    for i, grad in enumerate(face_in(own, other)):
        grad = grad * th[NZ : NZ + 1, :]
        east = jnp.sum(jnp.where(is_east, grad, 0.0), axis=1, keepdims=True)
        west = jnp.sum(jnp.where(is_east, 0.0, grad), axis=1, keepdims=True)
        add = jnp.where(lane == NC - 1, east, 0.0) + jnp.where(lane == 0, west, 0.0)
        out[NR * i : NR * (i + 1), :] = inner[i] + DT_VISC * add
    _, theirs = halves()
    weight = DT_VISC * th[pl.ds(theirs, HALF), :]
    lat_a = face_in([a2[i] for i in range(4)], [from_a[i] for i in range(4)])
    weight_b = weight * b_exists()
    lat_b = face_in([b2[i] for i in range(4)], [from_b[i] for i in range(4)])
    sums = [jnp.sum(x * weight, axis=0, keepdims=True) for x in lat_a]
    sums += [jnp.sum(x * weight_b, axis=0, keepdims=True) for x in lat_b]
    out[2 * NR : 2 * NR + 8, :] = jnp.concatenate(sums + [jnp.zeros((4, NC), jnp.float32)], axis=0)
    out[40:56, :] = sf[...]
    out[56:72, :] = dg[...]


def side_kernel(msg, msg_a, msg_b, rest_out, diag_out, edge_out, a_out, b_out):
    def widen(own, first, second):
        east, west = lon_sides(first, second)
        halo = jnp.where(lane_of(own.shape) < NC // 2, east, west)
        return jnp.concatenate([own, halo], axis=1)

    part = lambda lo, hi: widen(msg[lo:hi, :], msg_a[lo:hi, :], msg_b[lo:hi, :])
    te, tn, faces = part(0, NR), part(NR, 2 * NR), part(2 * NR, 2 * NR + 8)
    sf, dg = part(40, 56), part(56, 72)
    row = row_of((NR, 2 * NC))
    even = even_lat()
    north_u, north_v = (jnp.where(even, faces[i : i + 1], faces[i + 2 : i + 3]) for i in range(2))
    south_u, south_v = (jnp.where(even, faces[i + 2 : i + 3], faces[i : i + 1]) for i in range(2))
    at_north, at_south = row == NR - 1, row == 0
    te = te + jnp.where(at_north, north_u, 0.0) + jnp.where(at_south, south_u, 0.0)
    tn = tn + jnp.where(at_north, north_v, 0.0) + jnp.where(at_south, south_v, 0.0)
    east = lambda x: pltpu.roll(x, 2 * NC - 1, 1)
    west = lambda x: pltpu.roll(x, 1, 1)
    north = lambda x: jnp.where(at_north, 0.0, pltpu.roll(x, NR - 1, 0))
    south = lambda x: jnp.where(at_south, 0.0, pltpu.roll(x, 1, 0))
    across = lambda fu, fv: TAU * (fu - west(fu) + fv)
    rest = sf - TAU * (te - west(te) + tn - south(tn))
    rest = rest - ((4.0 + dg) * sf - (east(sf) + west(sf) + north(sf) + south(sf)))
    rest = rest - jnp.where(at_south, TAU * south_v, 0.0)
    rest_out[...] = rest
    diag_out[...] = dg
    first = TAU * tn[NR - 1 :] + sf[NR - 1 :] + across(north_u, north_v)
    second = -TAU * north_v
    to_south = sf[:1] + across(south_u, south_v)
    zero = jnp.zeros((5, 2 * NC), jnp.float32)
    edge_out[...] = jnp.concatenate([first, second, to_south, zero], axis=0)
    msg_north = jnp.concatenate([rest[8:], dg[11:], first, second, zero[:1]], axis=0)
    msg_south = jnp.concatenate([rest[:9], dg[:6], to_south], axis=0)
    a_out[...] = jnp.where(even, msg_north, msg_south)
    b_out[...] = jnp.where(even, msg_south, msg_north)


def solve_kernel(pc, rest, dg, edge, from_a, from_b, v_hbm, dots_out, v_out, sem):
    rows, wide = 3 * NR, 2 * NC
    even = even_lat()
    exists = b_exists()
    msg_a = from_a[...]
    msg_b = from_b[...] * exists
    north = jnp.where(even, msg_a, msg_b)
    south = jnp.where(even, msg_b, msg_a)
    zeros = lambda n: jnp.zeros((n, wide), jnp.float32)
    row = row_of((rows, wide))
    lat = lat_index()
    low = jnp.where(lat == 0, NR, 0)
    high = jnp.where(lat == 15, 2 * NR, 3 * NR)
    inside = jnp.where(jnp.logical_and(row >= low, row < high), 1.0, 0.0).astype(jnp.float32)
    below = jnp.concatenate([zeros(8), south[:7], south[7:8] + edge[2:3]], axis=0)
    above = jnp.concatenate(
        [north[:1] + edge[0:1], north[1:2] + edge[1:2], north[2:9], zeros(7)], axis=0
    )
    own = rest[...] + jnp.concatenate([south[13:15], zeros(13), north[15:]], axis=0)
    res = jnp.concatenate([below, own, above], axis=0) * inside
    diag = 4.0 + jnp.concatenate([zeros(11), south[8:13], dg[...], north[9:15], zeros(10)], axis=0)

    def lon_shift(x, n):
        return x if n == 0 else pltpu.roll(x, (-n) % wide, 1)

    def lat_shift(x, n):
        return x if n == 0 else pltpu.roll(x, (-n) % rows, 0)

    def operate(x):
        near = lon_shift(x, 1) + lon_shift(x, -1) + lat_shift(x, 1) + lat_shift(x, -1)
        return diag * x - near

    def tap(a, b):
        at = 5 * (a + 2) + b + 2
        return pc[at : at + 1, :]

    def precondition(x):
        moved = [lon_shift(x, b) for b in range(-2, 3)]
        total = None
        for a in range(-2, 3):
            line = tap(a, -2) * moved[0]
            for b in range(1, 5):
                line = line + tap(a, b - 2) * moved[b]
            line = lat_shift(line, a)
            total = line if total is None else total + line
        return total * inside

    scale = 1.0 / (5.0 * tap(0, 0))
    p0 = res
    v0 = precondition(p0)
    a0 = operate(v0)
    p1 = (a0 * scale - SHIFTS[0] * p0) * inside
    v1 = precondition(p1)
    a1 = operate(v1)
    p2 = (a1 * scale - SHIFTS[1] * p1) * inside
    v2 = precondition(p2)
    mine = lambda x: x[NR : 2 * NR, :NC]
    half_a2 = mine(diag * v2 - 2.0 * (lon_shift(v2, 1) + lat_shift(v2, 1)))
    v0, v1, v2, a0, a1, r = (mine(x) for x in (v0, v1, v2, a0, a1, p0))
    v_out[0] = v0
    v_out[1] = v1
    v_out[2] = v2
    pairs = ((v0, a0), (v0, a1), (v2, a0), (v1, a1), (v2, a1), (v2, half_a2), (v0, r), (v1, r), (v2, r))
    copy = pltpu.make_async_copy(v_out, v_hbm, sem)
    copy.start()
    lane = lane_of((1, NC))
    line = jnp.zeros((1, NC), jnp.float32)
    for i, (x, y) in enumerate(pairs):
        total = jnp.sum(jnp.sum(x * y, axis=0, keepdims=True), axis=1, keepdims=True)
        line = line + jnp.where(lane == i, total, 0.0)
    dots_out[...] = jnp.broadcast_to(line[None], dots_out.shape)
    copy.wait()


def relay_kernel(got, out, held, spread, sems):
    copy = pltpu.make_async_copy(got, held, sems.at[0])
    copy.start()
    copy.wait()
    spread[...] = jnp.broadcast_to(jnp.sum(held[...], axis=0, keepdims=True)[:, :1], spread.shape)
    copy = pltpu.make_async_copy(spread, out, sems.at[1])
    copy.start()
    copy.wait()


def step_kernel(got, v, sf, out, held, sem):
    copy = pltpu.make_async_copy(got, held, sem)
    copy.start()
    copy.wait()
    line = jnp.sum(held[...], axis=0)
    lane = lane_of((1, NC))
    h00, h01, h02, h11, h12, h22, g0, g1, g2 = (
        jnp.sum(jnp.where(lane == i, line, 0.0), axis=1, keepdims=True) for i in range(9)
    )
    l1 = h01 / h00
    l2 = h02 / h00
    d1 = h11 - l1 * h01
    e12 = h12 - l1 * h02
    l3 = e12 / d1
    d2 = h22 - l2 * h02 - l3 * e12
    y1 = g1 - l1 * g0
    y2 = g2 - l2 * g0 - l3 * y1
    c2 = y2 / d2
    c1 = y1 / d1 - l3 * c2
    c0 = g0 / h00 - l1 * c1 - l2 * c2
    out[...] = sf[...] + c0 * v[0] + c1 * v[1] + c2 * v[2]


def row_masks():
    lane, row = lane_of((NR, NC)), row_of((NR, NC))
    return lane == NC - 1, lane == 0, row == NR - 1, row == 0


def spread_of(packed, lines):
    at_east, at_west, at_north, at_south = row_masks()

    def spread(k, flux_e, flux_n, i):
        side = pltpu.roll(packed[i], NC - 1 - 2 * k, 1)
        north = jnp.broadcast_to(lines[2 * i, pl.ds(k, 1), :], (NR, NC))
        south = jnp.broadcast_to(lines[2 * i + 1, pl.ds(k, 1), :], (NR, NC))
        flux_e = jnp.where(at_east, side, flux_e)
        flux_n = jnp.where(at_north, north, flux_n)
        back_e = jnp.where(at_west, side, pltpu.roll(flux_e, 1, 1))
        back_n = jnp.where(at_south, south, pltpu.roll(flux_n, 1, 0))
        return flux_e - back_e + (flux_n - back_n)

    return spread


def write_out(body, pairs, sems, unroll, first=0, count=NZ):
    per = NZ // CHUNKS
    all_copies = chunk_copies(pairs, sems)
    copies = lambda c: all_copies(first // per + c)

    def chunk(c, carry):
        lax.fori_loop(0, per, lambda i, x: body(first + c * per + i, x), 0, unroll=unroll)
        for copy in copies(c):
            copy.start()
        return carry

    def finish(c, carry):
        for copy in copies(c):
            copy.wait()
        return carry

    lax.fori_loop(0, count // per, chunk, 0)
    lax.fori_loop(0, count // per, finish, 0)


def velocity_kernel(early, u, v, vi, w, lon, lon_a, lon_b, from_a, from_b, *rest):
    u_hbm, v_hbm, u_out, v_out, packed, lines, sems = rest[0 if early else 2 :]
    is_east = lane_of((NR, NC)) % 2 == 0
    own = [lon[i] for i in range(4)]
    other = [beyond(lon_a[i], lon_b[i]) for i in range(4)]
    for i, grad in enumerate(face_in(own, other)):
        packed[i] = DT_VISC * jnp.where(is_east, grad, -grad)
    even = even_lat()
    exists = b_exists()
    mine, theirs = halves()
    first = theirs if early else mine
    at = pl.ds(first, HALF)
    for side in range(2):
        use_a = even if side == 0 else jnp.logical_not(even)
        here = [edge_row(ref, side == 0, 0, first, HALF) for ref in (u, v, vi, w)]
        there = [jnp.where(use_a, from_a[i], from_b[i] * exists) for i in range(4)]
        sign = DT_VISC if side == 0 else -DT_VISC
        for i, grad in enumerate(face_in(here, there)):
            lines[2 * i + side, at, :] = sign * grad
    spread = spread_of(packed, lines)
    lon_up = lambda x: pltpu.roll(x, NC - 1, 1)
    lat_up = lambda x: pltpu.roll(x, NR - 1, 0)

    def body(k, carry):
        at = level(k)
        uu, vv, visc = u[at, :], v[at, :], vi[at, :]
        wet = w[at, :].astype(jnp.float32)
        half = wet * (0.5 * DT_VISC)
        face_e = (visc + lon_up(visc)) * (half * lon_up(wet))
        face_n = (visc + lat_up(visc)) * (half * lat_up(wet))
        u_out[at, :] = wet * (uu + spread(k, face_e * (lon_up(uu) - uu), face_n * (lat_up(uu) - uu), 0))
        v_out[at, :] = wet * (vv + spread(k, face_e * (lon_up(vv) - vv), face_n * (lat_up(vv) - vv), 1))
        return carry

    write_out(body, ((u_out, u_hbm), (v_out, v_hbm)), sems, 8, first, HALF)


def tracer_kernel(
    t, u, v, w, lon, lon_a, lon_b, from_a, from_a2, from_b, from_b2,
    t_hbm, t_out, packed, lines, sems,
):
    is_east = lane_of((NR, NC)) % 2 == 0
    by = DT_ADV / 12.0
    packed[1] = beyond(lon_a[4], lon_b[4])
    far = lon[5] + beyond(lon_a[5], lon_b[5])
    speed = jnp.where(is_east, lon[0], beyond(lon_a[0], lon_b[0]))
    packed[0] = speed * far * (by * lon[3] * beyond(lon_a[3], lon_b[3]))
    even = even_lat()
    exists = b_exists()
    mine, theirs = halves()
    for first, there_a, there_b in ((mine, from_a2, from_b2), (theirs, from_a, from_b)):
        at = pl.ds(first, HALF)
        part = first // HALF
        for side in range(2):
            north = side == 0
            use_a = even if north else jnp.logical_not(even)
            wet_here = edge_row(w, north, 0, first, HALF)
            wet_there = jnp.where(use_a, there_a[3], there_b[3] * exists)
            near = edge_row(t, north, 0, first, HALF) * wet_here
            inner = edge_row(t, north, 1, first, HALF) * edge_row(w, north, 1, first, HALF)
            far = jnp.where(use_a, from_a2[6 + part], from_b2[6 + part]) + (7.0 * near - inner)
            if north:
                speed = edge_row(v, True, 0, first, HALF)
            else:
                speed = jnp.where(use_a, there_a[1], there_b[1])
            lines[side, at, :] = speed * far * (by * wet_here * wet_there)
            lines[2 + side, at, :] = jnp.where(use_a, from_a2[4 + part], from_b2[4 + part] * exists)
    spread = spread_of(packed, lines)
    at_east, at_west, at_north, at_south = row_masks()
    lon_up = lambda x: pltpu.roll(x, NC - 1, 1)
    lat_up = lambda x: pltpu.roll(x, NR - 1, 0)

    def body(k, carry):
        at = level(k)
        tt = t[at, :]
        wet = w[at, :].astype(jnp.float32)
        wt = tt * wet
        side = pltpu.roll(packed[1], NC - 1 - 2 * k, 1)
        north = jnp.broadcast_to(lines[2, pl.ds(k, 1), :], (NR, NC))
        south = jnp.broadcast_to(lines[3, pl.ds(k, 1), :], (NR, NC))
        t_e = jnp.where(at_east, side, lon_up(wt))
        t_w = jnp.where(at_west, side, pltpu.roll(wt, 1, 1))
        t_n = jnp.where(at_north, north, lat_up(wt))
        t_s = jnp.where(at_south, south, pltpu.roll(wt, 1, 0))
        part = by * wet
        flux_e = u[at, :] * (7.0 * (wt + t_e) - (t_w + lon_up(t_e))) * (part * lon_up(wet))
        flux_n = v[at, :] * (7.0 * (wt + t_n) - (t_s + lat_up(t_n))) * (part * lat_up(wet))
        t_out[at, :] = wet * (tt - spread(k, flux_e, flux_n, 0))
        return carry

    write_out(body, ((t_out, t_hbm),), sems, 8)


def local(tracer, east_vel, north_vel, viscosity, land_sea, thickness, surface, surface_diag, precond_kernel):
    flat = (NZ * NR, NC)
    u, v, vi, w, t = (x.reshape(flat) for x in (east_vel, north_vel, viscosity, land_sea, tracer))
    block = NZ * NR * NC * 4
    field = pltpu.VMEM(flat, jnp.float32)
    wets = pltpu.VMEM(flat, jnp.int32)
    dma = pltpu.SemaphoreType.DMA
    rows = (4, HALF, NC)
    late = (8, HALF, NC)
    lon, a, b, a2, b2, inner, th = call(
        fetch_kernel,
        [(6, NR, NC), rows, rows, late, late, (2, NR, NC), (NZ + 8, NC)],
        [HBM] * 6,
        50 * NZ * NR * NC,
        5 * block,
        [field] * 3 + [wets, field, pltpu.SMEM((NZ,), jnp.float32), dma((CHUNKS, 5)), dma],
        vmem=FETCH_VMEM,
    )(thickness, u, v, vi, w, t)
    from_b = lax.ppermute(b, LAT, SWAP_B)
    from_a = lax.ppermute(a, LAT, SWAP_A)
    lon_b = lax.ppermute(lon, LON, SWAP_B)
    lon_a = lax.ppermute(lon, LON, SWAP_A)
    (msg,) = call(join_kernel, [(MSG, NC)], [VM] * 11, 10**6, 10**6)(
        inner, lon, lon_a, lon_b, a2, from_a, b2, from_b, th, surface, surface_diag
    )
    msg_b = lax.ppermute(msg, LON, SWAP_B)
    msg_a = lax.ppermute(msg, LON, SWAP_A)
    wide = (NR, 2 * NC)
    rest, dg, edge, side_a, side_b = call(
        side_kernel, [wide, wide, (8, 2 * NC), wide, wide], [VM] * 3, 10**6, 10**5
    )(msg, msg_a, msg_b)
    got_b = lax.ppermute(side_b, LAT, SWAP_B)
    got_a = lax.ppermute(side_a, LAT, SWAP_A)
    (taps,) = call(taps_kernel, [(32, 2 * NC)], [SM], 10**4, 10**4)(precond_kernel)
    def velocity(early, edges, written):
        return call(
            functools.partial(velocity_kernel, early),
            [flat] * 2,
            [VM] * 9 + [HBM] * len(written),
            30 * NZ * NR * NC,
            3 * block,
            [field] * 2
            + [pltpu.VMEM((2, NR, NC), jnp.float32), pltpu.VMEM((4, NZ, NC), jnp.float32), dma((CHUNKS, 2))],
            HBM,
            aliases={9 + i: i for i in range(len(written))},
        )(u, v, vi, w, lon, lon_a, lon_b, *edges, *written)

    u_half, v_half = velocity(True, (from_a, from_b), ())
    got_a, got_b, u_half, v_half = lax.optimization_barrier((got_a, got_b, u_half, v_half))
    vecs, dots = call(
        solve_kernel,
        [(3, NR, NC), (32, 8, NC)],
        [VM] * 6,
        10**6,
        10**5,
        [pltpu.VMEM((3, NR, NC), jnp.float32), dma],
        [HBM, VM],
    )(taps, rest, dg, edge, got_a, got_b)
    dots, a2, b2 = lax.optimization_barrier((dots, a2, b2))
    from_b2 = lax.ppermute(b2, LAT, SWAP_B)
    from_a2 = lax.ppermute(a2, LAT, SWAP_A)
    dots = lax.all_to_all(dots, ("x", "y", "c"), 0, 0)
    lat = (from_a, from_a2, from_b, from_b2)
    u_new, v_new = velocity(False, (from_a2, from_b2), (u_half, v_half))
    t_new = call(
        tracer_kernel,
        [flat],
        [VM] * 11,
        60 * NZ * NR * NC,
        5 * block,
        [field, pltpu.VMEM((2, NR, NC), jnp.float32), pltpu.VMEM((4, NZ, NC), jnp.float32), dma((CHUNKS, 1))],
        HBM,
    )(t, u, v, w, lon, lon_a, lon_b, *lat)[0]
    (dots,) = call(
        relay_kernel,
        [(8, 1, NC)],
        [HBM],
        10**4,
        10**4,
        [pltpu.VMEM((32, 8, NC), jnp.float32), pltpu.VMEM((8, 1, NC), jnp.float32), dma((2,))],
        HBM,
    )(dots)
    dots = lax.all_to_all(dots, ("zl", "zh"), 0, 0)
    dots, t_new, u_new, v_new = lax.optimization_barrier((dots, t_new, u_new, v_new))
    (surface_new,) = call(
        step_kernel,
        [(NR, NC)],
        [HBM] + [VM] * 2,
        10**5,
        10**4,
        [pltpu.VMEM((8, 1, NC), jnp.float32), dma],
    )(dots, vecs, surface)
    shape = (NZ, NR, NC)
    return t_new.reshape(shape), u_new.reshape(shape), v_new.reshape(shape), surface_new


def solution(mesh):
    sizes = dict(mesh.shape)
    assert sizes == {"lon": 16, "lat": 16} and tuple(mesh.axis_names) == ("lon", "lat")
    fine = Mesh(mesh.devices.reshape(2, 4, 2, 4, 4), ("zl", "x", "c", "y", "zh"))
    deep = P(None, LAT, LON)
    flat = P(LAT, LON)
    return jax.shard_map(
        local,
        mesh=fine,
        in_specs=(deep,) * 5 + (P(), flat, flat, P()),
        out_specs=(deep, deep, deep, flat),
        check_vma=False,
    )
```

```python
import functools

import jax
import jax.numpy as jnp
from jax import lax
from jax.experimental import pallas as pl
from jax.experimental.pallas import tpu as pltpu
from jax.sharding import Mesh
from jax.sharding import PartitionSpec as P

DT_ADV = 0.25
DT_VISC = 0.2
TAU = 0.05
SHIFTS = (0.3, 1.3)

LON = ("zl", "x", "c")
LAT = ("y", "zh")
NZ, NR, NC = 64, 16, 128
SWAP_A = [(i, i ^ 1) for i in range(16)]
SWAP_B = [(i, (i + 1) % 16 if i % 2 else (i - 1) % 16) for i in range(16)]

VM = pl.BlockSpec(memory_space=pltpu.VMEM)
SM = pl.BlockSpec(memory_space=pltpu.SMEM)
HBM = pl.BlockSpec(memory_space=pltpu.HBM)
FETCH_VMEM = 53.25


def call(kernel, outs, specs, flops, nbytes, scratch=(), place=VM, vmem=4, aliases=None):
    return pl.pallas_call(
        kernel,
        out_shape=[jax.ShapeDtypeStruct(s, jnp.float32) for s in outs],
        in_specs=specs,
        out_specs=place if isinstance(place, list) else [place] * len(outs),
        scratch_shapes=list(scratch),
        input_output_aliases=aliases or {},
        compiler_params=pltpu.CompilerParams(vmem_limit_bytes=int(vmem * 1024 * 1024)),
        cost_estimate=pl.CostEstimate(flops=flops, bytes_accessed=nbytes, transcendentals=0),
    )


def lane_of(shape):
    return lax.broadcasted_iota(jnp.int32, shape, len(shape) - 1)


def row_of(shape):
    return lax.broadcasted_iota(jnp.int32, shape, len(shape) - 2)


def even_lon():
    return lax.axis_index("c") == 0


def even_lat():
    return lax.axis_index("zh") % 2 == 0


def lat_index():
    return lax.axis_index("y") * 4 + lax.axis_index("zh")


def b_exists():
    lat = lat_index()
    return jnp.where(jnp.logical_or(lat == 0, lat == 15), 0.0, 1.0).astype(jnp.float32)


HALF = NZ // 2
CHUNKS = 4


def halves():
    mine = jnp.where(even_lat(), 0, HALF)
    return pl.multiple_of(mine, HALF), pl.multiple_of(HALF - mine, HALF)


def edge_row(ref, north, inwards, first, count):
    if isinstance(north, bool):
        row = NR - 1 - inwards if north else inwards
    else:
        row = jnp.where(north, NR - 1 - inwards, inwards)
    return ref[pl.ds(first * NR + row, count, stride=NR), :].astype(jnp.float32)


def pipeline(copies, body, acc, unroll):
    per = NZ // CHUNKS

    def start(c, carry):
        for copy in copies(c):
            copy.start()
        return carry

    def chunk(c, carry):
        for copy in copies(c):
            copy.wait()
        return lax.fori_loop(0, per, lambda i, x: body(c * per + i, x), carry, unroll=unroll)

    lax.fori_loop(0, CHUNKS, start, 0)
    return lax.fori_loop(0, CHUNKS, chunk, acc)


def chunk_copies(pairs, sems):
    span = NZ * NR // CHUNKS

    def copies(c):
        at = pl.ds(pl.multiple_of(c * span, span), span)
        return [
            pltpu.make_async_copy(src.at[at], dst.at[at], sems.at[c, i])
            for i, (src, dst) in enumerate(pairs)
        ]

    return copies


def level(k):
    return pl.ds(pl.multiple_of(k * NR, NR), NR)


def fetch_kernel(u, v, vi, land, lon_out, a_out, b_out, other_a, other_b, uo, vo, vio, lo, sems):
    pair = lane_of((NR, NC)) // 2

    def body(k, acc):
        at = level(k)
        values = (uo[at, :], vo[at, :], vio[at, :], lo[at, :].astype(jnp.float32))
        mine = pair == k
        return tuple(
            jnp.where(mine, pltpu.roll(x, 2 * k + 1, 1), old) for x, old in zip(values, acc)
        )

    copies = chunk_copies(((u, uo), (v, vo), (vi, vio), (land, lo)), sems)
    acc = pipeline(copies, body, (jnp.zeros((NR, NC), jnp.float32),) * 4, 8)
    for i in range(4):
        lon_out[i] = acc[i]
    even = even_lat()
    mine, theirs = halves()
    for north, first, rest in ((even, a_out, other_a), (jnp.logical_not(even), b_out, other_b)):
        for i, ref in enumerate((uo, vo, vio, lo)):
            first[i] = edge_row(ref, north, 0, mine, HALF)
            rest[i] = edge_row(ref, north, 0, theirs, HALF)


def inner_kernel(thick, u, v, vi, w, out, th_out):
    lane, row = lane_of((NR, NC)), row_of((NR, NC))
    pair = lane[:1] // 2
    up = lambda x: pltpu.roll(x, NC - 1, 1)
    north_of = lambda x: pltpu.roll(x, NR - 1, 0)

    def body(k, acc):
        at = level(k)
        wet, uu, vv, visc = w[at, :].astype(jnp.float32), u[at, :], v[at, :], vi[at, :]
        th = jnp.full((1, NC), thick[k], jnp.float32)
        th_out[pl.ds(k, 1), :] = th
        own = wet * th
        half = 0.5 * own
        east = (visc + up(visc)) * (half * up(wet))
        north = (visc + north_of(visc)) * (half * north_of(wet))
        return (
            acc[0] + own * uu,
            acc[1] + east * (up(uu) - uu),
            acc[2] + north * (north_of(uu) - uu),
            acc[3] + own * vv,
            acc[4] + east * (up(vv) - vv),
            acc[5] + north * (north_of(vv) - vv),
            jnp.where(pair == k, th, acc[6]),
        )

    zero = jnp.zeros((NR, NC), jnp.float32)
    acc = lax.fori_loop(0, NZ, body, (zero,) * 6 + (zero[:1],), unroll=4)
    th_out[NZ:, :] = jnp.broadcast_to(acc[6], (8, NC))
    for i in range(2):
        east = jnp.where(lane == NC - 1, 0.0, acc[3 * i + 1])
        north = jnp.where(row == NR - 1, 0.0, acc[3 * i + 2])
        out[i] = acc[3 * i] + DT_VISC * (
            east - pltpu.roll(east, 1, 1) + north - pltpu.roll(north, 1, 0)
        )


def late_kernel(t, w, other_a, other_b, lon_out, a_out, b_out):
    lane = lane_of((NR, NC))
    pair = lane // 2
    half_lane = lane < NC // 2

    def body(k, acc):
        at = level(k)
        first = t[at, :] * w[at, :].astype(jnp.float32)
        inner = jnp.where(half_lane, pltpu.roll(first, NC - 1, 1), pltpu.roll(first, 1, 1))
        mine = pair == k
        return tuple(
            jnp.where(mine, pltpu.roll(x, 2 * k + 1, 1), old)
            for x, old in zip((first, 7.0 * first - inner), acc)
        )

    acc = lax.fori_loop(0, NZ, body, (jnp.zeros((NR, NC), jnp.float32),) * 2, unroll=8)
    lon_out[0] = acc[0]
    lon_out[1] = acc[1]
    even = even_lat()
    for north, src, dst in ((even, other_a, a_out), (jnp.logical_not(even), other_b, b_out)):
        dst[:4] = src[...]
        for i in range(2):
            near, inner = (
                edge_row(t, north, n, i * HALF, HALF) * edge_row(w, north, n, i * HALF, HALF)
                for n in range(2)
            )
            dst[4 + i] = near
            dst[6 + i] = 7.0 * near - inner


def taps_kernel(pc, out):
    for i in range(25):
        out[i : i + 1, :] = jnp.full((1, 2 * NC), pc[i // 5, i % 5], jnp.float32)


def lon_sides(first, second):
    even = even_lon()
    return jnp.where(even, first, second), jnp.where(even, second, first)


def beyond(from_a, from_b):
    east, west = lon_sides(from_a, from_b)
    is_east = lane_of((NR, NC)) % 2 == 0
    return jnp.where(is_east, pltpu.roll(east, NC - 1, 1), pltpu.roll(west, 1, 1))


def face_in(own, other):
    face = 0.5 * (own[2] + other[2]) * (own[3] * other[3])
    return face * (other[0] - own[0]), face * (other[1] - own[1])


MSG = 72


def join_kernel(inner, lon, lon_a, lon_b, a2, from_a, b2, from_b, th, sf, dg, out):
    lane = lane_of((NR, NC))
    own = [lon[i] for i in range(4)]
    other = [beyond(lon_a[i], lon_b[i]) for i in range(4)]
    is_east = lane % 2 == 0
    for i, grad in enumerate(face_in(own, other)):
        grad = grad * th[NZ : NZ + 1, :]
        east = jnp.sum(jnp.where(is_east, grad, 0.0), axis=1, keepdims=True)
        west = jnp.sum(jnp.where(is_east, 0.0, grad), axis=1, keepdims=True)
        add = jnp.where(lane == NC - 1, east, 0.0) + jnp.where(lane == 0, west, 0.0)
        out[NR * i : NR * (i + 1), :] = inner[i] + DT_VISC * add
    _, theirs = halves()
    weight = DT_VISC * th[pl.ds(theirs, HALF), :]
    lat_a = face_in([a2[i] for i in range(4)], [from_a[i] for i in range(4)])
    weight_b = weight * b_exists()
    lat_b = face_in([b2[i] for i in range(4)], [from_b[i] for i in range(4)])
    sums = [jnp.sum(x * weight, axis=0, keepdims=True) for x in lat_a]
    sums += [jnp.sum(x * weight_b, axis=0, keepdims=True) for x in lat_b]
    out[2 * NR : 2 * NR + 8, :] = jnp.concatenate(sums + [jnp.zeros((4, NC), jnp.float32)], axis=0)
    out[40:56, :] = sf[...]
    out[56:72, :] = dg[...]


def side_kernel(msg, msg_a, msg_b, rest_out, diag_out, edge_out, a_out, b_out):
    def widen(own, first, second):
        east, west = lon_sides(first, second)
        halo = jnp.where(lane_of(own.shape) < NC // 2, east, west)
        return jnp.concatenate([own, halo], axis=1)

    part = lambda lo, hi: widen(msg[lo:hi, :], msg_a[lo:hi, :], msg_b[lo:hi, :])
    te, tn, faces = part(0, NR), part(NR, 2 * NR), part(2 * NR, 2 * NR + 8)
    sf, dg = part(40, 56), part(56, 72)
    row = row_of((NR, 2 * NC))
    even = even_lat()
    north_u, north_v = (jnp.where(even, faces[i : i + 1], faces[i + 2 : i + 3]) for i in range(2))
    south_u, south_v = (jnp.where(even, faces[i + 2 : i + 3], faces[i : i + 1]) for i in range(2))
    at_north, at_south = row == NR - 1, row == 0
    te = te + jnp.where(at_north, north_u, 0.0) + jnp.where(at_south, south_u, 0.0)
    tn = tn + jnp.where(at_north, north_v, 0.0) + jnp.where(at_south, south_v, 0.0)
    east = lambda x: pltpu.roll(x, 2 * NC - 1, 1)
    west = lambda x: pltpu.roll(x, 1, 1)
    north = lambda x: jnp.where(at_north, 0.0, pltpu.roll(x, NR - 1, 0))
    south = lambda x: jnp.where(at_south, 0.0, pltpu.roll(x, 1, 0))
    across = lambda fu, fv: TAU * (fu - west(fu) + fv)
    rest = sf - TAU * (te - west(te) + tn - south(tn))
    rest = rest - ((4.0 + dg) * sf - (east(sf) + west(sf) + north(sf) + south(sf)))
    rest = rest - jnp.where(at_south, TAU * south_v, 0.0)
    rest_out[...] = rest
    diag_out[...] = dg
    first = TAU * tn[NR - 1 :] + sf[NR - 1 :] + across(north_u, north_v)
    second = -TAU * north_v
    to_south = sf[:1] + across(south_u, south_v)
    zero = jnp.zeros((5, 2 * NC), jnp.float32)
    edge_out[...] = jnp.concatenate([first, second, to_south, zero], axis=0)
    msg_north = jnp.concatenate([rest[8:], dg[11:], first, second, zero[:1]], axis=0)
    msg_south = jnp.concatenate([rest[:9], dg[:6], to_south], axis=0)
    a_out[...] = jnp.where(even, msg_north, msg_south)
    b_out[...] = jnp.where(even, msg_south, msg_north)


def solve_kernel(pc, rest, dg, edge, from_a, from_b, v_hbm, dots_out, v_out, sem):
    rows, wide = 2 * NR, 2 * NC
    even = even_lat()
    exists = b_exists()
    msg_a = from_a[...]
    msg_b = from_b[...] * exists
    north = jnp.where(even, msg_a, msg_b)
    south = jnp.where(even, msg_b, msg_a)
    zeros = lambda n: jnp.zeros((n, wide), jnp.float32)
    row = row_of((rows + 8, wide))
    lat = lat_index()
    low = jnp.where(lat == 0, 8, 0)
    high = jnp.where(lat == 15, 8 + NR, rows + 8)
    inside = jnp.where(jnp.logical_and(row >= low, row < high), 1.0, 0.0).astype(jnp.float32)
    below = jnp.concatenate([south[:7], south[7:8] + edge[2:3]], axis=0)
    above = jnp.concatenate(
        [north[:1] + edge[0:1], north[1:2] + edge[1:2], north[2:9], zeros(7)], axis=0
    )
    own = rest[...] + jnp.concatenate([south[13:15], zeros(13), north[15:]], axis=0)
    res = jnp.concatenate([below, own, above], axis=0) * inside
    inside = inside[:rows]
    diag = 4.0 + jnp.concatenate([zeros(3), south[8:13], dg[...], north[9:15], zeros(2)], axis=0)

    def lon_shift(x, n):
        return x if n == 0 else pltpu.roll(x, (-n) % wide, 1)

    def lat_shift(x, n):
        return x if n == 0 else pltpu.roll(x, (-n) % x.shape[0], 0)

    def operate(x):
        near = lon_shift(x, 1) + lon_shift(x, -1) + lat_shift(x, 1) + lat_shift(x, -1)
        return diag * x - near

    def tap(a, b):
        at = 5 * (a + 2) + b + 2
        return pc[at : at + 1, :]

    def precondition(x):
        moved = [lon_shift(x, b) for b in range(-2, 3)]
        total = None
        for a in range(-2, 3):
            line = tap(a, -2) * moved[0]
            for b in range(1, 5):
                line = line + tap(a, b - 2) * moved[b]
            line = lat_shift(line, a)[:rows]
            total = line if total is None else total + line
        return total * inside

    scale = 1.0 / (5.0 * tap(0, 0))
    p0 = res
    v0 = precondition(p0)
    a0 = operate(v0)
    p1 = (a0 * scale - SHIFTS[0] * p0[:rows]) * inside
    v1 = precondition(p1)
    a1 = operate(v1)
    p2 = (a1 * scale - SHIFTS[1] * p1) * inside
    v2 = precondition(p2)
    mine = lambda x: x[8 : 8 + NR, :NC]
    half_a2 = mine(diag * v2 - 2.0 * (lon_shift(v2, 1) + lat_shift(v2, 1)))
    v0, v1, v2, a0, a1, r = (mine(x) for x in (v0, v1, v2, a0, a1, p0))
    v_out[0] = v0
    v_out[1] = v1
    v_out[2] = v2
    pairs = ((v0, a0), (v0, a1), (v2, a0), (v1, a1), (v2, a1), (v2, half_a2), (v0, r), (v1, r), (v2, r))
    copy = pltpu.make_async_copy(v_out, v_hbm, sem)
    copy.start()
    lane = lane_of((1, NC))
    line = jnp.zeros((1, NC), jnp.float32)
    for i, (x, y) in enumerate(pairs):
        total = jnp.sum(jnp.sum(x * y, axis=0, keepdims=True), axis=1, keepdims=True)
        line = line + jnp.where(lane == i, total, 0.0)
    dots_out[...] = jnp.broadcast_to(line[None], dots_out.shape)
    copy.wait()


def relay_kernel(got, out):
    out[...] = jnp.broadcast_to(jnp.sum(got[...], axis=0, keepdims=True)[:, :1], out.shape)


def step_kernel(got, v, sf, out):
    line = jnp.sum(got[...], axis=0)
    lane = lane_of((1, NC))
    h00, h01, h02, h11, h12, h22, g0, g1, g2 = (
        jnp.sum(jnp.where(lane == i, line, 0.0), axis=1, keepdims=True) for i in range(9)
    )
    l1 = h01 / h00
    l2 = h02 / h00
    d1 = h11 - l1 * h01
    e12 = h12 - l1 * h02
    l3 = e12 / d1
    d2 = h22 - l2 * h02 - l3 * e12
    y1 = g1 - l1 * g0
    y2 = g2 - l2 * g0 - l3 * y1
    c2 = y2 / d2
    c1 = y1 / d1 - l3 * c2
    c0 = g0 / h00 - l1 * c1 - l2 * c2
    out[...] = sf[...] + c0 * v[0] + c1 * v[1] + c2 * v[2]


def row_masks():
    lane, row = lane_of((NR, NC)), row_of((NR, NC))
    return lane == NC - 1, lane == 0, row == NR - 1, row == 0


def spread_of(packed, lines):
    at_east, at_west, at_north, at_south = row_masks()

    def spread(k, flux_e, flux_n, i):
        side = pltpu.roll(packed[i], NC - 1 - 2 * k, 1)
        north = jnp.broadcast_to(lines[2 * i, pl.ds(k, 1), :], (NR, NC))
        south = jnp.broadcast_to(lines[2 * i + 1, pl.ds(k, 1), :], (NR, NC))
        flux_e = jnp.where(at_east, side, flux_e)
        flux_n = jnp.where(at_north, north, flux_n)
        back_e = jnp.where(at_west, side, pltpu.roll(flux_e, 1, 1))
        back_n = jnp.where(at_south, south, pltpu.roll(flux_n, 1, 0))
        return flux_e - back_e + (flux_n - back_n)

    return spread


def write_out(body, pairs, sems, unroll, first=0, count=NZ):
    per = NZ // CHUNKS
    all_copies = chunk_copies(pairs, sems)
    copies = lambda c: all_copies(first // per + c)

    def chunk(c, carry):
        lax.fori_loop(0, per, lambda i, x: body(first + c * per + i, x), 0, unroll=unroll)
        for copy in copies(c):
            copy.start()
        return carry

    def finish(c, carry):
        for copy in copies(c):
            copy.wait()
        return carry

    lax.fori_loop(0, count // per, chunk, 0)
    lax.fori_loop(0, count // per, finish, 0)


def velocity_kernel(early, u, v, vi, w, lon, lon_a, lon_b, from_a, from_b, *rest):
    u_hbm, v_hbm, u_out, v_out, packed, lines, sems = rest[0 if early else 2 :]
    is_east = lane_of((NR, NC)) % 2 == 0
    own = [lon[i] for i in range(4)]
    other = [beyond(lon_a[i], lon_b[i]) for i in range(4)]
    for i, grad in enumerate(face_in(own, other)):
        packed[i] = DT_VISC * jnp.where(is_east, grad, -grad)
    even = even_lat()
    exists = b_exists()
    mine, theirs = halves()
    first = theirs if early else mine
    at = pl.ds(first, HALF)
    for side in range(2):
        use_a = even if side == 0 else jnp.logical_not(even)
        here = [edge_row(ref, side == 0, 0, first, HALF) for ref in (u, v, vi, w)]
        there = [jnp.where(use_a, from_a[i], from_b[i] * exists) for i in range(4)]
        sign = DT_VISC if side == 0 else -DT_VISC
        for i, grad in enumerate(face_in(here, there)):
            lines[2 * i + side, at, :] = sign * grad
    spread = spread_of(packed, lines)
    lon_up = lambda x: pltpu.roll(x, NC - 1, 1)
    lat_up = lambda x: pltpu.roll(x, NR - 1, 0)

    def body(k, carry):
        at = level(k)
        uu, vv, visc = u[at, :], v[at, :], vi[at, :]
        wet = w[at, :].astype(jnp.float32)
        half = wet * (0.5 * DT_VISC)
        face_e = (visc + lon_up(visc)) * (half * lon_up(wet))
        face_n = (visc + lat_up(visc)) * (half * lat_up(wet))
        u_out[at, :] = wet * (uu + spread(k, face_e * (lon_up(uu) - uu), face_n * (lat_up(uu) - uu), 0))
        v_out[at, :] = wet * (vv + spread(k, face_e * (lon_up(vv) - vv), face_n * (lat_up(vv) - vv), 1))
        return carry

    write_out(body, ((u_out, u_hbm), (v_out, v_hbm)), sems, 8, first, HALF)


def tracer_kernel(
    t, u, v, w, lon, lon_a, lon_b, lon2, lon2_a, lon2_b, from_a, from_a2, from_b, from_b2,
    t_hbm, t_out, packed, lines, sems,
):
    is_east = lane_of((NR, NC)) % 2 == 0
    by = DT_ADV / 12.0
    packed[1] = beyond(lon2_a[0], lon2_b[0])
    far = lon2[1] + beyond(lon2_a[1], lon2_b[1])
    speed = jnp.where(is_east, lon[0], beyond(lon_a[0], lon_b[0]))
    packed[0] = speed * far * (by * lon[3] * beyond(lon_a[3], lon_b[3]))
    even = even_lat()
    exists = b_exists()
    mine, theirs = halves()
    for first, there_a, there_b in ((mine, from_a2, from_b2), (theirs, from_a, from_b)):
        at = pl.ds(first, HALF)
        part = first // HALF
        for side in range(2):
            north = side == 0
            use_a = even if north else jnp.logical_not(even)
            wet_here = edge_row(w, north, 0, first, HALF)
            wet_there = jnp.where(use_a, there_a[3], there_b[3] * exists)
            near = edge_row(t, north, 0, first, HALF) * wet_here
            inner = edge_row(t, north, 1, first, HALF) * edge_row(w, north, 1, first, HALF)
            far = jnp.where(use_a, from_a2[6 + part], from_b2[6 + part]) + (7.0 * near - inner)
            if north:
                speed = edge_row(v, True, 0, first, HALF)
            else:
                speed = jnp.where(use_a, there_a[1], there_b[1])
            lines[side, at, :] = speed * far * (by * wet_here * wet_there)
            lines[2 + side, at, :] = jnp.where(use_a, from_a2[4 + part], from_b2[4 + part] * exists)
    spread = spread_of(packed, lines)
    at_east, at_west, at_north, at_south = row_masks()
    lon_up = lambda x: pltpu.roll(x, NC - 1, 1)
    lat_up = lambda x: pltpu.roll(x, NR - 1, 0)

    def body(k, carry):
        at = level(k)
        tt = t[at, :]
        wet = w[at, :].astype(jnp.float32)
        wt = tt * wet
        side = pltpu.roll(packed[1], NC - 1 - 2 * k, 1)
        north = jnp.broadcast_to(lines[2, pl.ds(k, 1), :], (NR, NC))
        south = jnp.broadcast_to(lines[3, pl.ds(k, 1), :], (NR, NC))
        t_e = jnp.where(at_east, side, lon_up(wt))
        t_w = jnp.where(at_west, side, pltpu.roll(wt, 1, 1))
        t_n = jnp.where(at_north, north, lat_up(wt))
        t_s = jnp.where(at_south, south, pltpu.roll(wt, 1, 0))
        part = by * wet
        flux_e = u[at, :] * (7.0 * (wt + t_e) - (t_w + lon_up(t_e))) * (part * lon_up(wet))
        flux_n = v[at, :] * (7.0 * (wt + t_n) - (t_s + lat_up(t_n))) * (part * lat_up(wet))
        t_out[at, :] = wet * (tt - spread(k, flux_e, flux_n, 0))
        return carry

    write_out(body, ((t_out, t_hbm),), sems, 8)


def local(tracer, east_vel, north_vel, viscosity, land_sea, thickness, surface, surface_diag, precond_kernel):
    flat = (NZ * NR, NC)
    u, v, vi, w, t = (x.reshape(flat) for x in (east_vel, north_vel, viscosity, land_sea, tracer))
    block = NZ * NR * NC * 4
    field = pltpu.VMEM(flat, jnp.float32)
    wets = pltpu.VMEM(flat, jnp.int32)
    dma = pltpu.SemaphoreType.DMA
    rows = (4, HALF, NC)
    late = (8, HALF, NC)
    lon, a, b, other_a, other_b = call(
        fetch_kernel,
        [(4, NR, NC), rows, rows, rows, rows],
        [HBM] * 4,
        20 * NZ * NR * NC,
        4 * block,
        [field] * 3 + [wets, dma((CHUNKS, 4))],
        vmem=FETCH_VMEM,
    )(u, v, vi, w)
    from_b = lax.ppermute(b, LAT, SWAP_B)
    from_a = lax.ppermute(a, LAT, SWAP_A)
    lon_b = lax.ppermute(lon, LON, SWAP_B)
    lon_a = lax.ppermute(lon, LON, SWAP_A)
    inner, th = call(
        inner_kernel, [(2, NR, NC), (NZ + 8, NC)], [SM] + [VM] * 4, 40 * NZ * NR * NC, 4 * block
    )(thickness, u, v, vi, w)
    (msg,) = call(join_kernel, [(MSG, NC)], [VM] * 11, 10**6, 10**6)(
        inner, lon, lon_a, lon_b, other_a, from_a, other_b, from_b, th, surface, surface_diag
    )
    msg_b = lax.ppermute(msg, LON, SWAP_B)
    msg_a = lax.ppermute(msg, LON, SWAP_A)
    lon2, a2, b2 = call(
        late_kernel, [(2, NR, NC), late, late], [VM] * 4, 20 * NZ * NR * NC, 2 * block
    )(t, w, other_a, other_b)
    msg_a, msg_b, lon2, a2, b2 = lax.optimization_barrier((msg_a, msg_b, lon2, a2, b2))
    wide = (NR, 2 * NC)
    rest, dg, edge, side_a, side_b = call(
        side_kernel, [wide, wide, (8, 2 * NC), wide, wide], [VM] * 3, 10**6, 10**5
    )(msg, msg_a, msg_b)
    got_b = lax.ppermute(side_b, LAT, SWAP_B)
    got_a = lax.ppermute(side_a, LAT, SWAP_A)
    (taps,) = call(taps_kernel, [(32, 2 * NC)], [SM], 10**4, 10**4)(precond_kernel)
    def velocity(early, edges, written):
        return call(
            functools.partial(velocity_kernel, early),
            [flat] * 2,
            [VM] * 9 + [HBM] * len(written),
            30 * NZ * NR * NC,
            3 * block,
            [field] * 2
            + [pltpu.VMEM((2, NR, NC), jnp.float32), pltpu.VMEM((4, NZ, NC), jnp.float32), dma((CHUNKS, 2))],
            HBM,
            aliases={9 + i: i for i in range(len(written))},
        )(u, v, vi, w, lon, lon_a, lon_b, *edges, *written)

    u_half, v_half = velocity(True, (from_a, from_b), ())
    got_a, got_b, u_half, v_half = lax.optimization_barrier((got_a, got_b, u_half, v_half))
    vecs, dots = call(
        solve_kernel,
        [(3, NR, NC), (32, 8, NC)],
        [VM] * 6,
        10**6,
        10**5,
        [pltpu.VMEM((3, NR, NC), jnp.float32), dma],
        [HBM, VM],
    )(taps, rest, dg, edge, got_a, got_b)
    dots, a2, b2, lon2 = lax.optimization_barrier((dots, a2, b2, lon2))
    from_b2 = lax.ppermute(b2, LAT, SWAP_B)
    from_a2 = lax.ppermute(a2, LAT, SWAP_A)
    lon2_b = lax.ppermute(lon2, LON, SWAP_B)
    lon2_a = lax.ppermute(lon2, LON, SWAP_A)
    dots = lax.all_to_all(dots, ("x", "y", "c"), 0, 0)
    lat = (from_a, from_a2, from_b, from_b2)
    u_new, v_new = velocity(False, (from_a2, from_b2), (u_half, v_half))
    t_new = call(
        tracer_kernel,
        [flat],
        [VM] * 14,
        60 * NZ * NR * NC,
        5 * block,
        [field, pltpu.VMEM((2, NR, NC), jnp.float32), pltpu.VMEM((4, NZ, NC), jnp.float32), dma((CHUNKS, 1))],
        HBM,
    )(t, u, v, w, lon, lon_a, lon_b, lon2, lon2_a, lon2_b, *lat)[0]
    (dots,) = call(relay_kernel, [(8, 1, NC)], [VM], 10**4, 10**4)(dots)
    dots = lax.all_to_all(dots, ("zl", "zh"), 0, 0)
    dots, t_new, u_new, v_new = lax.optimization_barrier((dots, t_new, u_new, v_new))
    (surface_new,) = call(step_kernel, [(NR, NC)], [VM] * 3, 10**5, 10**4)(dots, vecs, surface)
    shape = (NZ, NR, NC)
    return t_new.reshape(shape), u_new.reshape(shape), v_new.reshape(shape), surface_new


def solution(mesh):
    sizes = dict(mesh.shape)
    assert sizes == {"lon": 16, "lat": 16} and tuple(mesh.axis_names) == ("lon", "lat")
    fine = Mesh(mesh.devices.reshape(2, 4, 2, 4, 4), ("zl", "x", "c", "y", "zh"))
    deep = P(None, LAT, LON)
    flat = P(LAT, LON)
    return jax.shard_map(
        local,
        mesh=fine,
        in_specs=(deep,) * 5 + (P(), flat, flat, P()),
        out_specs=(deep, deep, deep, flat),
        check_vma=False,
    )
```

```python
import functools

import jax
import jax.numpy as jnp
from jax import lax
from jax.experimental import pallas as pl
from jax.experimental.pallas import tpu as pltpu
from jax.sharding import Mesh
from jax.sharding import PartitionSpec as P

DT_ADV = 0.25
DT_VISC = 0.2
TAU = 0.05
SHIFTS = (0.3, 1.3)

LON = ("zl", "x", "c")
LAT = ("y", "zh")
NZ, NR, NC = 64, 16, 128
SWAP_A = [(i, i ^ 1) for i in range(16)]
SWAP_B = [(i, (i + 1) % 16 if i % 2 else (i - 1) % 16) for i in range(16)]

VM = pl.BlockSpec(memory_space=pltpu.VMEM)
SM = pl.BlockSpec(memory_space=pltpu.SMEM)
HBM = pl.BlockSpec(memory_space=pltpu.HBM)
FETCH_VMEM = 53.25


def call(kernel, outs, specs, flops, nbytes, scratch=(), place=VM, vmem=4, aliases=None):
    return pl.pallas_call(
        kernel,
        out_shape=[jax.ShapeDtypeStruct(s, jnp.float32) for s in outs],
        in_specs=specs,
        out_specs=place if isinstance(place, list) else [place] * len(outs),
        scratch_shapes=list(scratch),
        input_output_aliases=aliases or {},
        compiler_params=pltpu.CompilerParams(vmem_limit_bytes=int(vmem * 1024 * 1024)),
        cost_estimate=pl.CostEstimate(flops=flops, bytes_accessed=nbytes, transcendentals=0),
    )


def lane_of(shape):
    return lax.broadcasted_iota(jnp.int32, shape, len(shape) - 1)


def row_of(shape):
    return lax.broadcasted_iota(jnp.int32, shape, len(shape) - 2)


def even_lon():
    return lax.axis_index("c") == 0


def even_lat():
    return lax.axis_index("zh") % 2 == 0


def lat_index():
    return lax.axis_index("y") * 4 + lax.axis_index("zh")


def b_exists():
    lat = lat_index()
    return jnp.where(jnp.logical_or(lat == 0, lat == 15), 0.0, 1.0).astype(jnp.float32)


HALF = NZ // 2
CHUNKS = 4


def halves():
    mine = jnp.where(even_lat(), 0, HALF)
    return pl.multiple_of(mine, HALF), pl.multiple_of(HALF - mine, HALF)


def edge_row(ref, north, inwards, first, count):
    if isinstance(north, bool):
        row = NR - 1 - inwards if north else inwards
    else:
        row = jnp.where(north, NR - 1 - inwards, inwards)
    return ref[pl.ds(first * NR + row, count, stride=NR), :].astype(jnp.float32)


def pipeline(copies, body, acc, unroll):
    per = NZ // CHUNKS

    def start(c, carry):
        for copy in copies(c):
            copy.start()
        return carry

    def chunk(c, carry):
        for copy in copies(c):
            copy.wait()
        return lax.fori_loop(0, per, lambda i, x: body(c * per + i, x), carry, unroll=unroll)

    lax.fori_loop(0, CHUNKS, start, 0)
    return lax.fori_loop(0, CHUNKS, chunk, acc)


def chunk_copies(pairs, sems):
    span = NZ * NR // CHUNKS

    def copies(c):
        at = pl.ds(pl.multiple_of(c * span, span), span)
        return [
            pltpu.make_async_copy(src.at[at], dst.at[at], sems.at[c, i])
            for i, (src, dst) in enumerate(pairs)
        ]

    return copies


def level(k):
    return pl.ds(pl.multiple_of(k * NR, NR), NR)


def squeeze(rows, shift):
    group = lane_of((8, NC)) // 32
    out = None
    for g in range(4):
        part = pltpu.roll(rows[8 * g : 8 * g + 8], (shift + 32 * g) % NC, 1)
        out = part if g == 0 else jnp.where(group == g, part, out)
    return out


def fetch_kernel(u, v, vi, land, lon_out, a_out, b_out, other_a, other_b, corners, uo, vo, vio, lo, sems):
    pair = lane_of((NR, NC)) // 2

    def body(k, acc):
        at = level(k)
        values = (uo[at, :], vo[at, :], vio[at, :], lo[at, :].astype(jnp.float32))
        mine = pair == k
        return tuple(
            jnp.where(mine, pltpu.roll(x, 2 * k + 1, 1), old) for x, old in zip(values, acc)
        )

    copies = chunk_copies(((u, uo), (v, vo), (vi, vio), (land, lo)), sems)
    acc = pipeline(copies, body, (jnp.zeros((NR, NC), jnp.float32),) * 4, 8)
    for i in range(4):
        lon_out[i] = acc[i]
    even = even_lat()
    mine, theirs = halves()
    for north, first, rest in ((even, a_out, other_a), (jnp.logical_not(even), b_out, other_b)):
        for i, ref in enumerate((uo, vo, vio, lo)):
            first[i] = edge_row(ref, north, 0, mine, HALF)
            rest[i] = edge_row(ref, north, 0, theirs, HALF)
    for n, ref in enumerate((a_out, other_a, b_out, other_b)):
        for i in range(4):
            corners[4 * n + i] = squeeze(ref[i], 16)


AT_CORNER, AT_FIELDS, MSG = 32, 96, 112


def put_side_by_side(first, second, step, high):
    left = lane_of(first.shape) % (2 * step) < step
    high_pair = jnp.where(left, first, pltpu.roll(second, step, 1))
    low_pair = jnp.where(left, pltpu.roll(first, NC - step, 1), second)
    return jnp.where(high, high_pair, low_pair)


def take_across(east, west, which, step, east_first):
    left = lane_of(east.shape) % (2 * step) < step
    place = 0 if east_first else 1
    east = east if which == place else pltpu.roll(east, step if which < place else NC - step, 1)
    west = west if which != place else pltpu.roll(west, NC - step if which else step, 1)
    return jnp.where(left, east, west) if east_first else jnp.where(left, west, east)


def inner_kernel(thick, u, v, vi, w, lon, corners, sf, dg, out, msg_a, msg_b, th_out):
    lane, row = lane_of((NR, NC)), row_of((NR, NC))
    pair = lane[:1] // 2
    up = lambda x: pltpu.roll(x, NC - 1, 1)
    north_of = lambda x: pltpu.roll(x, NR - 1, 0)

    def body(k, acc):
        at = level(k)
        wet, uu, vv, visc = w[at, :].astype(jnp.float32), u[at, :], v[at, :], vi[at, :]
        th = jnp.full((1, NC), thick[k], jnp.float32)
        th_out[pl.ds(k, 1), :] = th
        own = wet * th
        half = 0.5 * own
        east = (visc + up(visc)) * (half * up(wet))
        north = (visc + north_of(visc)) * (half * north_of(wet))
        return (
            acc[0] + own * uu,
            acc[1] + east * (up(uu) - uu),
            acc[2] + north * (north_of(uu) - uu),
            acc[3] + own * vv,
            acc[4] + east * (up(vv) - vv),
            acc[5] + north * (north_of(vv) - vv),
            jnp.where(pair == k, th, acc[6]),
        )

    zero = jnp.zeros((NR, NC), jnp.float32)
    acc = lax.fori_loop(0, NZ, body, (zero,) * 6 + (zero[:1],), unroll=4)
    th_out[NZ:, :] = jnp.broadcast_to(acc[6], (8, NC))
    for i in range(2):
        east = jnp.where(lane == NC - 1, 0.0, acc[3 * i + 1])
        north = jnp.where(row == NR - 1, 0.0, acc[3 * i + 2])
        out[i] = acc[3 * i] + DT_VISC * (
            east - pltpu.roll(east, 1, 1) + north - pltpu.roll(north, 1, 0)
        )
    fields = (out[0], out[1], sf[...], dg[...])
    for msg, high in ((msg_a, even_lon()), (msg_b, jnp.logical_not(even_lon()))):
        for i in range(2):
            msg[NR * i : NR * (i + 1), :] = put_side_by_side(lon[2 * i], lon[2 * i + 1], 1, high)
        for n in range(2):
            for i in range(4):
                at = AT_CORNER + 32 * n + 8 * i
                first, second = corners[8 * n + i], corners[8 * n + 4 + i]
                msg[at : at + 8, :] = put_side_by_side(first, second, 16, high)
        line = None
        for f, x in enumerate(fields):
            part = jnp.where(high, pltpu.roll(x, 16 * (f + 1) % NC, 1), pltpu.roll(x, 16 * f, 1) if f else x)
            line = part if f == 0 else jnp.where(lane // 16 == f, part, line)
        msg[AT_FIELDS:, :] = line


def late_kernel(t, w, other_a, other_b, lon_out, a_out, b_out):
    lane = lane_of((NR, NC))
    pair = lane // 2
    half_lane = lane < NC // 2

    def body(k, acc):
        at = level(k)
        first = t[at, :] * w[at, :].astype(jnp.float32)
        inner = jnp.where(half_lane, pltpu.roll(first, NC - 1, 1), pltpu.roll(first, 1, 1))
        mine = pair == k
        return tuple(
            jnp.where(mine, pltpu.roll(x, 2 * k + 1, 1), old)
            for x, old in zip((first, 7.0 * first - inner), acc)
        )

    acc = lax.fori_loop(0, NZ, body, (jnp.zeros((NR, NC), jnp.float32),) * 2, unroll=8)
    lon_out[0] = acc[0]
    lon_out[1] = acc[1]
    even = even_lat()
    for north, src, dst in ((even, other_a, a_out), (jnp.logical_not(even), other_b, b_out)):
        dst[:4] = src[...]
        for i in range(2):
            near, inner = (
                edge_row(t, north, n, i * HALF, HALF) * edge_row(w, north, n, i * HALF, HALF)
                for n in range(2)
            )
            dst[4 + i] = near
            dst[6 + i] = 7.0 * near - inner


def taps_kernel(pc, out):
    for i in range(25):
        out[i : i + 1, :] = jnp.full((1, 2 * NC), pc[i // 5, i % 5], jnp.float32)


def lon_sides(first, second):
    even = even_lon()
    return jnp.where(even, first, second), jnp.where(even, second, first)


def beyond(from_a, from_b):
    east, west = lon_sides(from_a, from_b)
    is_east = lane_of((NR, NC)) % 2 == 0
    return jnp.where(is_east, pltpu.roll(east, NC - 1, 1), pltpu.roll(west, 1, 1))


def edge_across(msg_a, msg_b, i):
    at = slice(NR * (i // 2), NR * (i // 2 + 1))
    return take_across(*lon_sides(msg_a[at, :], msg_b[at, :]), i % 2, 1, True)


def face_in(own, other):
    face = 0.5 * (own[2] + other[2]) * (own[3] * other[3])
    return face * (other[0] - own[0]), face * (other[1] - own[1])


LAT_MSG = 96


def side_kernel(
    inner, lon, sf_own, dg_own, msg_a, msg_b, a2, from_a, b2, from_b, th,
    rest_out, diag_out, edge_out, corner_out, a_out, b_out,
):
    lane = lane_of((NR, NC))
    is_east = lane % 2 == 0
    packed = [lon[i] for i in range(4)]
    other = [edge_across(msg_a, msg_b, i) for i in range(4)]
    far_east, far_west = lon_sides(msg_a[AT_FIELDS:, :], msg_b[AT_FIELDS:, :])

    def widen(own, f):
        east = pltpu.roll(far_east, (NC - 16 * f) % NC, 1) if f else far_east
        west = pltpu.roll(far_west, (NC - 16 - 16 * f) % NC, 1)
        halo = jnp.where(lane < 16, east, jnp.where(lane >= NC - 16, west, 0.0))
        return jnp.concatenate([own, halo], axis=1)

    wide_lane = lane_of((NR, 2 * NC))
    te, tn = widen(inner[0], 0), widen(inner[1], 1)
    sf, dg = widen(sf_own[...], 2), widen(dg_own[...], 3)
    add = []
    for grad in face_in(packed, other):
        grad = grad * (DT_VISC * th[NZ : NZ + 1, :])
        east = jnp.sum(jnp.where(is_east, grad, 0.0), axis=1, keepdims=True)
        west = jnp.sum(jnp.where(is_east, 0.0, grad), axis=1, keepdims=True)
        here = jnp.where(wide_lane == NC - 1, east, 0.0) + jnp.where(wide_lane == 0, west, 0.0)
        there = jnp.where(wide_lane == NC, east, 0.0) + jnp.where(wide_lane == 2 * NC - 1, west, 0.0)
        add.append(here - there)
    te = te + add[0]
    tn = tn + add[1]
    _, theirs = halves()
    weight = DT_VISC * th[pl.ds(theirs, HALF), :]
    lat_a = face_in([a2[i] for i in range(4)], [from_a[i] for i in range(4)])
    weight_b = weight * b_exists()
    lat_b = face_in([b2[i] for i in range(4)], [from_b[i] for i in range(4)])
    faces = [jnp.sum(x * weight, axis=0, keepdims=True) for x in lat_a]
    faces += [jnp.sum(x * weight_b, axis=0, keepdims=True) for x in lat_b]
    faces = [jnp.concatenate([x, jnp.zeros((1, NC), jnp.float32)], axis=1) for x in faces]
    for n in range(2):
        for i in range(4):
            at = AT_CORNER + 32 * n + 8 * i
            sides = lon_sides(msg_a[at : at + 8, :], msg_b[at : at + 8, :])
            for h in range(2):
                to = 64 * n + 32 * h + 8 * i
                corner_out[to : to + 8, :] = take_across(*sides, h, 16, False)
    row = row_of((NR, 2 * NC))
    even = even_lat()
    north_u, north_v = (jnp.where(even, faces[i], faces[i + 2]) for i in range(2))
    south_u, south_v = (jnp.where(even, faces[i + 2], faces[i]) for i in range(2))
    at_north, at_south = row == NR - 1, row == 0
    te = te + jnp.where(at_north, north_u, 0.0) + jnp.where(at_south, south_u, 0.0)
    tn = tn + jnp.where(at_north, north_v, 0.0) + jnp.where(at_south, south_v, 0.0)
    east = lambda x: pltpu.roll(x, 2 * NC - 1, 1)
    west = lambda x: pltpu.roll(x, 1, 1)
    north = lambda x: jnp.where(at_north, 0.0, pltpu.roll(x, NR - 1, 0))
    south = lambda x: jnp.where(at_south, 0.0, pltpu.roll(x, 1, 0))
    across = lambda fu, fv: TAU * (fu - west(fu) + fv)
    rest = sf - TAU * (te - west(te) + tn - south(tn))
    rest = rest - ((4.0 + dg) * sf - (east(sf) + west(sf) + north(sf) + south(sf)))
    rest = rest - jnp.where(at_south, TAU * south_v, 0.0)
    rest_out[...] = rest
    diag_out[...] = dg
    first = TAU * tn[NR - 1 :] + sf[NR - 1 :] + across(north_u, north_v)
    second = -TAU * north_v
    to_south = sf[:1] + across(south_u, south_v)
    zero = jnp.zeros((5, 2 * NC), jnp.float32)
    edge_out[...] = jnp.concatenate([first, second, to_south, zero], axis=0)
    msg_north = jnp.concatenate([rest[8:], dg[11:], first, second, zero[:1]], axis=0)
    msg_south = jnp.concatenate([rest[:9], dg[:6], to_south], axis=0)
    for n, (out, lines) in enumerate(
        (
            (a_out, jnp.where(even, msg_north, msg_south)),
            (b_out, jnp.where(even, msg_south, msg_north)),
        )
    ):
        out[:NR, :] = lines[:, :NC]
        out[NR : 2 * NR, :] = lines[:, NC:]
        out[2 * NR :, :] = corner_out[64 * n : 64 * (n + 1), :]


def solve_kernel(pc, th, corner, rest, dg, edge, from_a, from_b, v_hbm, dots_out, v_out, sem):
    rows, wide = 2 * NR, 2 * NC
    even = even_lat()
    exists = b_exists()
    msg_a = jnp.concatenate([from_a[:NR, :], from_a[NR : 2 * NR, :]], axis=1)
    msg_b = jnp.concatenate([from_b[:NR, :], from_b[NR : 2 * NR, :]], axis=1) * exists
    north = jnp.where(even, msg_a, msg_b)
    south = jnp.where(even, msg_b, msg_a)
    zeros = lambda n: jnp.zeros((n, wide), jnp.float32)
    row = row_of((rows + 8, wide))
    lat = lat_index()
    low = jnp.where(lat == 0, 8, 0)
    high = jnp.where(lat == 15, 8 + NR, rows + 8)
    inside = jnp.where(jnp.logical_and(row >= low, row < high), 1.0, 0.0).astype(jnp.float32)
    below = jnp.concatenate([south[:7], south[7:8] + edge[2:3]], axis=0)
    above = jnp.concatenate(
        [north[:1] + edge[0:1], north[1:2] + edge[1:2], north[2:9], zeros(7)], axis=0
    )
    own = rest[...] + jnp.concatenate([south[13:15], zeros(13), north[15:]], axis=0)
    res = jnp.concatenate([below, own, above], axis=0)
    group = lane_of((8, NC)) // 32
    weights = []
    for first in halves():
        line = None
        for g in range(4):
            part = th[pl.ds(pl.multiple_of(first + 8 * g, 8), 8), :]
            line = part if g == 0 else jnp.where(group == g, part, line)
        weights.append(DT_VISC * line)
    sums = []
    for n, got in enumerate((from_a, from_b)):
        total = None
        for h in range(2):
            here = [corner[64 * n + 32 * h + 8 * i : 64 * n + 32 * h + 8 * (i + 1), :] for i in range(4)]
            at = 2 * NR + 32 * (1 - h)
            there = [got[at + 8 * i : at + 8 * (i + 1), :] for i in range(4)]
            part = [x * weights[h] for x in face_in(here, there)]
            total = part if h == 0 else [x + y for x, y in zip(total, part)]
        for x in total:
            x = jnp.sum(x, axis=0, keepdims=True)
            x = x + pltpu.roll(x, 32, 1)
            x = x + pltpu.roll(x, 64, 1)
            edge_lane = lane_of((1, NC))
            near = jnp.logical_or(edge_lane < 16, edge_lane >= NC - 16)
            x = jnp.where(near, pltpu.roll(x, NC - 16, 1), 0.0)
            sums.append(jnp.concatenate([jnp.zeros((1, NC), jnp.float32), x], axis=1))
    sums[2] = sums[2] * exists
    sums[3] = sums[3] * exists
    north_u, north_v = (jnp.where(even, sums[i], sums[i + 2]) for i in range(2))
    south_u, south_v = (jnp.where(even, sums[i + 2], sums[i]) for i in range(2))
    across = lambda fu, fv: TAU * (fu - pltpu.roll(fu, 1, 1) + fv)
    for at, line in (
        (7 + NR, -across(north_u, north_v)),
        (8 + NR, across(north_u, north_v) + TAU * north_v),
        (9 + NR, -TAU * north_v),
        (7, across(south_u, south_v)),
        (8, -across(south_u, south_v) - TAU * south_v),
        (9, TAU * south_v),
    ):
        res = res + jnp.where(row == at, line, 0.0)
    res = res * inside
    inside = inside[:rows]
    diag = 4.0 + jnp.concatenate([zeros(3), south[8:13], dg[...], north[9:15], zeros(2)], axis=0)

    def lon_shift(x, n):
        return x if n == 0 else pltpu.roll(x, (-n) % wide, 1)

    def lat_shift(x, n):
        return x if n == 0 else pltpu.roll(x, (-n) % x.shape[0], 0)

    def operate(x):
        near = lon_shift(x, 1) + lon_shift(x, -1) + lat_shift(x, 1) + lat_shift(x, -1)
        return diag * x - near

    def tap(a, b):
        at = 5 * (a + 2) + b + 2
        return pc[at : at + 1, :]

    def precondition(x):
        moved = [lon_shift(x, b) for b in range(-2, 3)]
        total = None
        for a in range(-2, 3):
            line = tap(a, -2) * moved[0]
            for b in range(1, 5):
                line = line + tap(a, b - 2) * moved[b]
            line = lat_shift(line, a)[:rows]
            total = line if total is None else total + line
        return total * inside

    scale = 1.0 / (5.0 * tap(0, 0))
    p0 = res
    v0 = precondition(p0)
    a0 = operate(v0)
    p1 = (a0 * scale - SHIFTS[0] * p0[:rows]) * inside
    v1 = precondition(p1)
    a1 = operate(v1)
    p2 = (a1 * scale - SHIFTS[1] * p1) * inside
    v2 = precondition(p2)
    mine = lambda x: x[8 : 8 + NR, :NC]
    half_a2 = mine(diag * v2 - 2.0 * (lon_shift(v2, 1) + lat_shift(v2, 1)))
    v0, v1, v2, a0, a1, r = (mine(x) for x in (v0, v1, v2, a0, a1, p0))
    v_out[0] = v0
    v_out[1] = v1
    v_out[2] = v2
    pairs = ((v0, a0), (v0, a1), (v2, a0), (v1, a1), (v2, a1), (v2, half_a2), (v0, r), (v1, r), (v2, r))
    copy = pltpu.make_async_copy(v_out, v_hbm, sem)
    copy.start()
    lane = lane_of((1, NC))
    line = jnp.zeros((1, NC), jnp.float32)
    for i, (x, y) in enumerate(pairs):
        total = jnp.sum(jnp.sum(x * y, axis=0, keepdims=True), axis=1, keepdims=True)
        line = line + jnp.where(lane == i, total, 0.0)
    dots_out[...] = jnp.broadcast_to(line[None], dots_out.shape)
    copy.wait()


def relay_kernel(got, out):
    out[...] = jnp.broadcast_to(jnp.sum(got[...], axis=0, keepdims=True)[:, :1], out.shape)


def step_kernel(got, v, sf, out):
    line = jnp.sum(got[...], axis=0)
    lane = lane_of((1, NC))
    h00, h01, h02, h11, h12, h22, g0, g1, g2 = (
        jnp.sum(jnp.where(lane == i, line, 0.0), axis=1, keepdims=True) for i in range(9)
    )
    l1 = h01 / h00
    l2 = h02 / h00
    d1 = h11 - l1 * h01
    e12 = h12 - l1 * h02
    l3 = e12 / d1
    d2 = h22 - l2 * h02 - l3 * e12
    y1 = g1 - l1 * g0
    y2 = g2 - l2 * g0 - l3 * y1
    c2 = y2 / d2
    c1 = y1 / d1 - l3 * c2
    c0 = g0 / h00 - l1 * c1 - l2 * c2
    out[...] = sf[...] + c0 * v[0] + c1 * v[1] + c2 * v[2]


def row_masks():
    lane, row = lane_of((NR, NC)), row_of((NR, NC))
    return lane == NC - 1, lane == 0, row == NR - 1, row == 0


def spread_of(packed, lines):
    at_east, at_west, at_north, at_south = row_masks()

    def spread(k, flux_e, flux_n, i):
        side = pltpu.roll(packed[i], NC - 1 - 2 * k, 1)
        north = jnp.broadcast_to(lines[2 * i, pl.ds(k, 1), :], (NR, NC))
        south = jnp.broadcast_to(lines[2 * i + 1, pl.ds(k, 1), :], (NR, NC))
        flux_e = jnp.where(at_east, side, flux_e)
        flux_n = jnp.where(at_north, north, flux_n)
        back_e = jnp.where(at_west, side, pltpu.roll(flux_e, 1, 1))
        back_n = jnp.where(at_south, south, pltpu.roll(flux_n, 1, 0))
        return flux_e - back_e + (flux_n - back_n)

    return spread


def write_out(body, pairs, sems, unroll, first=0, count=NZ):
    per = NZ // CHUNKS
    all_copies = chunk_copies(pairs, sems)
    copies = lambda c: all_copies(first // per + c)

    def chunk(c, carry):
        lax.fori_loop(0, per, lambda i, x: body(first + c * per + i, x), 0, unroll=unroll)
        for copy in copies(c):
            copy.start()
        return carry

    def finish(c, carry):
        for copy in copies(c):
            copy.wait()
        return carry

    lax.fori_loop(0, count // per, chunk, 0)
    lax.fori_loop(0, count // per, finish, 0)


def velocity_kernel(early, u, v, vi, w, lon, msg_a, msg_b, from_a, from_b, *rest):
    u_hbm, v_hbm, u_out, v_out, packed, lines, sems = rest[0 if early else 2 :]
    is_east = lane_of((NR, NC)) % 2 == 0
    own = [lon[i] for i in range(4)]
    other = [edge_across(msg_a, msg_b, i) for i in range(4)]
    for i, grad in enumerate(face_in(own, other)):
        packed[i] = DT_VISC * jnp.where(is_east, grad, -grad)
    even = even_lat()
    exists = b_exists()
    mine, theirs = halves()
    first = theirs if early else mine
    at = pl.ds(first, HALF)
    for side in range(2):
        use_a = even if side == 0 else jnp.logical_not(even)
        here = [edge_row(ref, side == 0, 0, first, HALF) for ref in (u, v, vi, w)]
        there = [jnp.where(use_a, from_a[i], from_b[i] * exists) for i in range(4)]
        sign = DT_VISC if side == 0 else -DT_VISC
        for i, grad in enumerate(face_in(here, there)):
            lines[2 * i + side, at, :] = sign * grad
    spread = spread_of(packed, lines)
    lon_up = lambda x: pltpu.roll(x, NC - 1, 1)
    lat_up = lambda x: pltpu.roll(x, NR - 1, 0)

    def body(k, carry):
        at = level(k)
        uu, vv, visc = u[at, :], v[at, :], vi[at, :]
        wet = w[at, :].astype(jnp.float32)
        half = wet * (0.5 * DT_VISC)
        face_e = (visc + lon_up(visc)) * (half * lon_up(wet))
        face_n = (visc + lat_up(visc)) * (half * lat_up(wet))
        u_out[at, :] = wet * (uu + spread(k, face_e * (lon_up(uu) - uu), face_n * (lat_up(uu) - uu), 0))
        v_out[at, :] = wet * (vv + spread(k, face_e * (lon_up(vv) - vv), face_n * (lat_up(vv) - vv), 1))
        return carry

    write_out(body, ((u_out, u_hbm), (v_out, v_hbm)), sems, 8, first, HALF)


def tracer_kernel(
    t, u, v, w, lon, msg_a, msg_b, lon2, lon2_a, lon2_b, from_a, from_a2, from_b, from_b2,
    t_hbm, t_out, packed, lines, sems,
):
    is_east = lane_of((NR, NC)) % 2 == 0
    by = DT_ADV / 12.0
    packed[1] = beyond(lon2_a[0], lon2_b[0])
    far = lon2[1] + beyond(lon2_a[1], lon2_b[1])
    speed = jnp.where(is_east, lon[0], edge_across(msg_a, msg_b, 0))
    wets = edge_across(msg_a, msg_b, 3) * lon[3]
    packed[0] = speed * far * (by * wets)
    even = even_lat()
    exists = b_exists()
    mine, theirs = halves()
    for first, there_a, there_b in ((mine, from_a2, from_b2), (theirs, from_a, from_b)):
        at = pl.ds(first, HALF)
        part = first // HALF
        for side in range(2):
            north = side == 0
            use_a = even if north else jnp.logical_not(even)
            wet_here = edge_row(w, north, 0, first, HALF)
            wet_there = jnp.where(use_a, there_a[3], there_b[3] * exists)
            near = edge_row(t, north, 0, first, HALF) * wet_here
            inner = edge_row(t, north, 1, first, HALF) * edge_row(w, north, 1, first, HALF)
            far = jnp.where(use_a, from_a2[6 + part], from_b2[6 + part]) + (7.0 * near - inner)
            if north:
                speed = edge_row(v, True, 0, first, HALF)
            else:
                speed = jnp.where(use_a, there_a[1], there_b[1])
            lines[side, at, :] = speed * far * (by * wet_here * wet_there)
            lines[2 + side, at, :] = jnp.where(use_a, from_a2[4 + part], from_b2[4 + part] * exists)
    spread = spread_of(packed, lines)
    at_east, at_west, at_north, at_south = row_masks()
    lon_up = lambda x: pltpu.roll(x, NC - 1, 1)
    lat_up = lambda x: pltpu.roll(x, NR - 1, 0)

    def body(k, carry):
        at = level(k)
        tt = t[at, :]
        wet = w[at, :].astype(jnp.float32)
        wt = tt * wet
        side = pltpu.roll(packed[1], NC - 1 - 2 * k, 1)
        north = jnp.broadcast_to(lines[2, pl.ds(k, 1), :], (NR, NC))
        south = jnp.broadcast_to(lines[3, pl.ds(k, 1), :], (NR, NC))
        t_e = jnp.where(at_east, side, lon_up(wt))
        t_w = jnp.where(at_west, side, pltpu.roll(wt, 1, 1))
        t_n = jnp.where(at_north, north, lat_up(wt))
        t_s = jnp.where(at_south, south, pltpu.roll(wt, 1, 0))
        part = by * wet
        flux_e = u[at, :] * (7.0 * (wt + t_e) - (t_w + lon_up(t_e))) * (part * lon_up(wet))
        flux_n = v[at, :] * (7.0 * (wt + t_n) - (t_s + lat_up(t_n))) * (part * lat_up(wet))
        t_out[at, :] = wet * (tt - spread(k, flux_e, flux_n, 0))
        return carry

    write_out(body, ((t_out, t_hbm),), sems, 8)


def local(tracer, east_vel, north_vel, viscosity, land_sea, thickness, surface, surface_diag, precond_kernel):
    flat = (NZ * NR, NC)
    u, v, vi, w, t = (x.reshape(flat) for x in (east_vel, north_vel, viscosity, land_sea, tracer))
    block = NZ * NR * NC * 4
    field = pltpu.VMEM(flat, jnp.float32)
    wets = pltpu.VMEM(flat, jnp.int32)
    dma = pltpu.SemaphoreType.DMA
    rows = (4, HALF, NC)
    late = (8, HALF, NC)
    lon, a, b, other_a, other_b, corners = call(
        fetch_kernel,
        [(4, NR, NC), rows, rows, rows, rows, (16, 8, NC)],
        [HBM] * 4,
        20 * NZ * NR * NC,
        4 * block,
        [field] * 3 + [wets, dma((CHUNKS, 4))],
        vmem=FETCH_VMEM,
    )(u, v, vi, w)
    from_b = lax.ppermute(b, LAT, SWAP_B)
    from_a = lax.ppermute(a, LAT, SWAP_A)
    inner, to_a, to_b, th = call(
        inner_kernel,
        [(2, NR, NC), (MSG, NC), (MSG, NC), (NZ + 8, NC)],
        [SM] + [VM] * 8,
        40 * NZ * NR * NC,
        4 * block,
    )(thickness, u, v, vi, w, lon, corners, surface, surface_diag)
    msg_b = lax.ppermute(to_b, LON, SWAP_B)
    msg_a = lax.ppermute(to_a, LON, SWAP_A)
    lon2, a2, b2 = call(
        late_kernel, [(2, NR, NC), late, late], [VM] * 4, 20 * NZ * NR * NC, 2 * block
    )(t, w, other_a, other_b)
    msg_a, msg_b, lon2, a2, b2 = lax.optimization_barrier((msg_a, msg_b, lon2, a2, b2))
    wide = (NR, 2 * NC)
    rest, dg, edge, corner, side_a, side_b = call(
        side_kernel,
        [wide, wide, (8, 2 * NC), (128, NC), (LAT_MSG, NC), (LAT_MSG, NC)],
        [VM] * 11,
        10**6,
        10**5,
    )(inner, lon, surface, surface_diag, msg_a, msg_b, other_a, from_a, other_b, from_b, th)
    got_b = lax.ppermute(side_b, LAT, SWAP_B)
    got_a = lax.ppermute(side_a, LAT, SWAP_A)
    (taps,) = call(taps_kernel, [(32, 2 * NC)], [SM], 10**4, 10**4)(precond_kernel)
    def velocity(early, edges, written):
        return call(
            functools.partial(velocity_kernel, early),
            [flat] * 2,
            [VM] * 9 + [HBM] * len(written),
            30 * NZ * NR * NC,
            3 * block,
            [field] * 2
            + [pltpu.VMEM((2, NR, NC), jnp.float32), pltpu.VMEM((4, NZ, NC), jnp.float32), dma((CHUNKS, 2))],
            HBM,
            aliases={9 + i: i for i in range(len(written))},
        )(u, v, vi, w, lon, msg_a, msg_b, *edges, *written)

    u_half, v_half = velocity(True, (from_a, from_b), ())
    got_a, got_b, u_half, v_half = lax.optimization_barrier((got_a, got_b, u_half, v_half))
    vecs, dots = call(
        solve_kernel,
        [(3, NR, NC), (32, 8, NC)],
        [VM] * 8,
        10**6,
        10**5,
        [pltpu.VMEM((3, NR, NC), jnp.float32), dma],
        [HBM, VM],
    )(taps, th, corner, rest, dg, edge, got_a, got_b)
    dots, a2, b2, lon2 = lax.optimization_barrier((dots, a2, b2, lon2))
    from_b2 = lax.ppermute(b2, LAT, SWAP_B)
    from_a2 = lax.ppermute(a2, LAT, SWAP_A)
    lon2_b = lax.ppermute(lon2, LON, SWAP_B)
    lon2_a = lax.ppermute(lon2, LON, SWAP_A)
    dots = lax.all_to_all(dots, ("x", "y", "c"), 0, 0)
    lat = (from_a, from_a2, from_b, from_b2)
    u_new, v_new = velocity(False, (from_a2, from_b2), (u_half, v_half))
    t_new = call(
        tracer_kernel,
        [flat],
        [VM] * 14,
        60 * NZ * NR * NC,
        5 * block,
        [field, pltpu.VMEM((2, NR, NC), jnp.float32), pltpu.VMEM((4, NZ, NC), jnp.float32), dma((CHUNKS, 1))],
        HBM,
    )(t, u, v, w, lon, msg_a, msg_b, lon2, lon2_a, lon2_b, *lat)[0]
    (dots,) = call(relay_kernel, [(8, 1, NC)], [VM], 10**4, 10**4)(dots)
    dots = lax.all_to_all(dots, ("zl", "zh"), 0, 0)
    dots, t_new, u_new, v_new = lax.optimization_barrier((dots, t_new, u_new, v_new))
    (surface_new,) = call(step_kernel, [(NR, NC)], [VM] * 3, 10**5, 10**4)(dots, vecs, surface)
    shape = (NZ, NR, NC)
    return t_new.reshape(shape), u_new.reshape(shape), v_new.reshape(shape), surface_new


def solution(mesh):
    sizes = dict(mesh.shape)
    assert sizes == {"lon": 16, "lat": 16} and tuple(mesh.axis_names) == ("lon", "lat")
    fine = Mesh(mesh.devices.reshape(2, 4, 2, 4, 4), ("zl", "x", "c", "y", "zh"))
    deep = P(None, LAT, LON)
    flat = P(LAT, LON)
    return jax.shard_map(
        local,
        mesh=fine,
        in_specs=(deep,) * 5 + (P(), flat, flat, P()),
        out_specs=(deep, deep, deep, flat),
        check_vma=False,
    )
```

```python
import functools

import jax
import jax.numpy as jnp
from jax import lax
from jax.experimental import pallas as pl
from jax.experimental.pallas import tpu as pltpu
from jax.sharding import Mesh
from jax.sharding import PartitionSpec as P

DT_ADV = 0.25
DT_VISC = 0.2
TAU = 0.05
SHIFTS = (0.3, 1.3)

LON = ("zl", "x", "c")
LAT = ("y", "zh")
NZ, NR, NC = 64, 16, 128
SWAP_A = [(i, i ^ 1) for i in range(16)]
SWAP_B = [(i, (i + 1) % 16 if i % 2 else (i - 1) % 16) for i in range(16)]

VM = pl.BlockSpec(memory_space=pltpu.VMEM)
SM = pl.BlockSpec(memory_space=pltpu.SMEM)
HBM = pl.BlockSpec(memory_space=pltpu.HBM)
FETCH_VMEM = 53.25


def call(kernel, outs, specs, flops, nbytes, scratch=(), place=VM, vmem=4, aliases=None):
    return pl.pallas_call(
        kernel,
        out_shape=[jax.ShapeDtypeStruct(s, jnp.float32) for s in outs],
        in_specs=specs,
        out_specs=place if isinstance(place, list) else [place] * len(outs),
        scratch_shapes=list(scratch),
        input_output_aliases=aliases or {},
        compiler_params=pltpu.CompilerParams(vmem_limit_bytes=int(vmem * 1024 * 1024)),
        cost_estimate=pl.CostEstimate(flops=flops, bytes_accessed=nbytes, transcendentals=0),
    )


def lane_of(shape):
    return lax.broadcasted_iota(jnp.int32, shape, len(shape) - 1)


def row_of(shape):
    return lax.broadcasted_iota(jnp.int32, shape, len(shape) - 2)


def even_lon():
    return lax.axis_index("c") == 0


def even_lat():
    return lax.axis_index("zh") % 2 == 0


def lat_index():
    return lax.axis_index("y") * 4 + lax.axis_index("zh")


def b_exists():
    lat = lat_index()
    return jnp.where(jnp.logical_or(lat == 0, lat == 15), 0.0, 1.0).astype(jnp.float32)


HALF = NZ // 2
CHUNKS = 4


def halves():
    mine = jnp.where(even_lat(), 0, HALF)
    return pl.multiple_of(mine, HALF), pl.multiple_of(HALF - mine, HALF)


def edge_row(ref, north, inwards, first, count):
    if isinstance(north, bool):
        row = NR - 1 - inwards if north else inwards
    else:
        row = jnp.where(north, NR - 1 - inwards, inwards)
    return ref[pl.ds(first * NR + row, count, stride=NR), :].astype(jnp.float32)


def pipeline(copies, body, acc, unroll):
    per = NZ // CHUNKS

    def start(c, carry):
        for copy in copies(c):
            copy.start()
        return carry

    def chunk(c, carry):
        for copy in copies(c):
            copy.wait()
        return lax.fori_loop(0, per, lambda i, x: body(c * per + i, x), carry, unroll=unroll)

    lax.fori_loop(0, CHUNKS, start, 0)
    return lax.fori_loop(0, CHUNKS, chunk, acc)


def chunk_copies(pairs, sems):
    span = NZ * NR // CHUNKS

    def copies(c):
        at = pl.ds(pl.multiple_of(c * span, span), span)
        return [
            pltpu.make_async_copy(src.at[at], dst.at[at], sems.at[c, i])
            for i, (src, dst) in enumerate(pairs)
        ]

    return copies


def level(k):
    return pl.ds(pl.multiple_of(k * NR, NR), NR)


def squeeze(rows, shift):
    group = lane_of((8, NC)) // 32
    out = None
    for g in range(4):
        part = pltpu.roll(rows[8 * g : 8 * g + 8], (shift + 32 * g) % NC, 1)
        out = part if g == 0 else jnp.where(group == g, part, out)
    return out


def fetch_kernel(u, v, vi, land, lon_out, a_out, b_out, corners, uo, vo, vio, lo, sems):
    pair = lane_of((NR, NC)) // 2

    def body(k, acc):
        at = level(k)
        values = (uo[at, :], vo[at, :], vio[at, :], lo[at, :].astype(jnp.float32))
        mine = pair == k
        return tuple(
            jnp.where(mine, pltpu.roll(x, 2 * k + 1, 1), old) for x, old in zip(values, acc)
        )

    copies = chunk_copies(((u, uo), (v, vo), (vi, vio), (land, lo)), sems)
    acc = pipeline(copies, body, (jnp.zeros((NR, NC), jnp.float32),) * 4, 8)
    for i in range(4):
        lon_out[i] = acc[i]
    even = even_lat()
    mine, theirs = halves()
    for n, (north, out) in enumerate(((even, a_out), (jnp.logical_not(even), b_out))):
        for i, ref in enumerate((uo, vo, vio, lo)):
            out[i] = edge_row(ref, north, 0, mine, HALF)
            corners[8 * n + i] = squeeze(out[i], 16)
            corners[8 * n + 4 + i] = squeeze(edge_row(ref, north, 0, theirs, HALF), 16)


AT_CORNER, AT_FIELDS, MSG = 32, 96, 112


def put_side_by_side(first, second, step, high):
    left = lane_of(first.shape) % (2 * step) < step
    high_pair = jnp.where(left, first, pltpu.roll(second, step, 1))
    low_pair = jnp.where(left, pltpu.roll(first, NC - step, 1), second)
    return jnp.where(high, high_pair, low_pair)


def take_across(east, west, which, step, east_first):
    left = lane_of(east.shape) % (2 * step) < step
    place = 0 if east_first else 1
    east = east if which == place else pltpu.roll(east, step if which < place else NC - step, 1)
    west = west if which != place else pltpu.roll(west, NC - step if which else step, 1)
    return jnp.where(left, east, west) if east_first else jnp.where(left, west, east)


def inner_kernel(thick, u, v, vi, w, lon, corners, sf, dg, out, msg_a, msg_b, th_out):
    lane, row = lane_of((NR, NC)), row_of((NR, NC))
    pair = lane[:1] // 2
    up = lambda x: pltpu.roll(x, NC - 1, 1)
    north_of = lambda x: pltpu.roll(x, NR - 1, 0)

    def body(k, acc):
        at = level(k)
        wet, uu, vv, visc = w[at, :].astype(jnp.float32), u[at, :], v[at, :], vi[at, :]
        th = jnp.full((1, NC), thick[k], jnp.float32)
        th_out[pl.ds(k, 1), :] = th
        own = wet * th
        half = 0.5 * own
        east = (visc + up(visc)) * (half * up(wet))
        north = (visc + north_of(visc)) * (half * north_of(wet))
        return (
            acc[0] + own * uu,
            acc[1] + east * (up(uu) - uu),
            acc[2] + north * (north_of(uu) - uu),
            acc[3] + own * vv,
            acc[4] + east * (up(vv) - vv),
            acc[5] + north * (north_of(vv) - vv),
            jnp.where(pair == k, th, acc[6]),
        )

    zero = jnp.zeros((NR, NC), jnp.float32)
    acc = lax.fori_loop(0, NZ, body, (zero,) * 6 + (zero[:1],), unroll=4)
    th_out[NZ:, :] = jnp.broadcast_to(acc[6], (8, NC))
    for i in range(2):
        east = jnp.where(lane == NC - 1, 0.0, acc[3 * i + 1])
        north = jnp.where(row == NR - 1, 0.0, acc[3 * i + 2])
        out[i] = acc[3 * i] + DT_VISC * (
            east - pltpu.roll(east, 1, 1) + north - pltpu.roll(north, 1, 0)
        )
    fields = (out[0], out[1], sf[...], dg[...])
    for msg, high in ((msg_a, even_lon()), (msg_b, jnp.logical_not(even_lon()))):
        for i in range(2):
            msg[NR * i : NR * (i + 1), :] = put_side_by_side(lon[2 * i], lon[2 * i + 1], 1, high)
        for n in range(2):
            for i in range(4):
                at = AT_CORNER + 32 * n + 8 * i
                first, second = corners[8 * n + i], corners[8 * n + 4 + i]
                msg[at : at + 8, :] = put_side_by_side(first, second, 16, high)
        line = None
        for f, x in enumerate(fields):
            part = jnp.where(high, pltpu.roll(x, 16 * (f + 1) % NC, 1), pltpu.roll(x, 16 * f, 1) if f else x)
            line = part if f == 0 else jnp.where(lane // 16 == f, part, line)
        msg[AT_FIELDS:, :] = line


def late_kernel(t, u, v, vi, w, lon_out, a_out, b_out):
    lane = lane_of((NR, NC))
    pair = lane // 2
    half_lane = lane < NC // 2

    def body(k, acc):
        at = level(k)
        first = t[at, :] * w[at, :].astype(jnp.float32)
        inner = jnp.where(half_lane, pltpu.roll(first, NC - 1, 1), pltpu.roll(first, 1, 1))
        mine = pair == k
        return tuple(
            jnp.where(mine, pltpu.roll(x, 2 * k + 1, 1), old)
            for x, old in zip((first, 7.0 * first - inner), acc)
        )

    acc = lax.fori_loop(0, NZ, body, (jnp.zeros((NR, NC), jnp.float32),) * 2, unroll=8)
    lon_out[0] = acc[0]
    lon_out[1] = acc[1]
    even = even_lat()
    _, theirs = halves()
    for north, dst in ((even, a_out), (jnp.logical_not(even), b_out)):
        for i, ref in enumerate((u, v, vi, w)):
            dst[i] = edge_row(ref, north, 0, theirs, HALF)
        for i in range(2):
            near, inner = (
                edge_row(t, north, n, i * HALF, HALF) * edge_row(w, north, n, i * HALF, HALF)
                for n in range(2)
            )
            dst[4 + i] = near
            dst[6 + i] = 7.0 * near - inner


def taps_kernel(pc, out):
    for i in range(25):
        out[i : i + 1, :] = jnp.full((1, 2 * NC), pc[i // 5, i % 5], jnp.float32)


def lon_sides(first, second):
    even = even_lon()
    return jnp.where(even, first, second), jnp.where(even, second, first)


def beyond(from_a, from_b):
    east, west = lon_sides(from_a, from_b)
    is_east = lane_of((NR, NC)) % 2 == 0
    return jnp.where(is_east, pltpu.roll(east, NC - 1, 1), pltpu.roll(west, 1, 1))


def edge_across(msg_a, msg_b, i):
    at = slice(NR * (i // 2), NR * (i // 2 + 1))
    return take_across(*lon_sides(msg_a[at, :], msg_b[at, :]), i % 2, 1, True)


def face_in(own, other):
    face = 0.5 * (own[2] + other[2]) * (own[3] * other[3])
    return face * (other[0] - own[0]), face * (other[1] - own[1])


LAT_MSG = 96


def side_kernel(
    inner, lon, sf_own, dg_own, msg_a, msg_b, u, v, vi, w, from_a, from_b, th,
    rest_out, diag_out, edge_out, corner_out, a_out, b_out,
):
    lane = lane_of((NR, NC))
    is_east = lane % 2 == 0
    packed = [lon[i] for i in range(4)]
    other = [edge_across(msg_a, msg_b, i) for i in range(4)]
    far_east, far_west = lon_sides(msg_a[AT_FIELDS:, :], msg_b[AT_FIELDS:, :])

    def widen(own, f):
        east = pltpu.roll(far_east, (NC - 16 * f) % NC, 1) if f else far_east
        west = pltpu.roll(far_west, (NC - 16 - 16 * f) % NC, 1)
        halo = jnp.where(lane < 16, east, jnp.where(lane >= NC - 16, west, 0.0))
        return jnp.concatenate([own, halo], axis=1)

    wide_lane = lane_of((NR, 2 * NC))
    te, tn = widen(inner[0], 0), widen(inner[1], 1)
    sf, dg = widen(sf_own[...], 2), widen(dg_own[...], 3)
    add = []
    for grad in face_in(packed, other):
        grad = grad * (DT_VISC * th[NZ : NZ + 1, :])
        east = jnp.sum(jnp.where(is_east, grad, 0.0), axis=1, keepdims=True)
        west = jnp.sum(jnp.where(is_east, 0.0, grad), axis=1, keepdims=True)
        here = jnp.where(wide_lane == NC - 1, east, 0.0) + jnp.where(wide_lane == 0, west, 0.0)
        there = jnp.where(wide_lane == NC, east, 0.0) + jnp.where(wide_lane == 2 * NC - 1, west, 0.0)
        add.append(here - there)
    te = te + add[0]
    tn = tn + add[1]
    _, theirs = halves()
    weight = DT_VISC * th[pl.ds(theirs, HALF), :]
    even = even_lat()
    rows_of = lambda north: [edge_row(ref, north, 0, theirs, HALF) for ref in (u, v, vi, w)]
    lat_a = face_in(rows_of(even), [from_a[i] for i in range(4)])
    weight_b = weight * b_exists()
    lat_b = face_in(rows_of(jnp.logical_not(even)), [from_b[i] for i in range(4)])
    faces = [jnp.sum(x * weight, axis=0, keepdims=True) for x in lat_a]
    faces += [jnp.sum(x * weight_b, axis=0, keepdims=True) for x in lat_b]
    faces = [jnp.concatenate([x, jnp.zeros((1, NC), jnp.float32)], axis=1) for x in faces]
    for n in range(2):
        for i in range(4):
            at = AT_CORNER + 32 * n + 8 * i
            sides = lon_sides(msg_a[at : at + 8, :], msg_b[at : at + 8, :])
            for h in range(2):
                to = 64 * n + 32 * h + 8 * i
                corner_out[to : to + 8, :] = take_across(*sides, h, 16, False)
    row = row_of((NR, 2 * NC))
    even = even_lat()
    north_u, north_v = (jnp.where(even, faces[i], faces[i + 2]) for i in range(2))
    south_u, south_v = (jnp.where(even, faces[i + 2], faces[i]) for i in range(2))
    at_north, at_south = row == NR - 1, row == 0
    te = te + jnp.where(at_north, north_u, 0.0) + jnp.where(at_south, south_u, 0.0)
    tn = tn + jnp.where(at_north, north_v, 0.0) + jnp.where(at_south, south_v, 0.0)
    east = lambda x: pltpu.roll(x, 2 * NC - 1, 1)
    west = lambda x: pltpu.roll(x, 1, 1)
    north = lambda x: jnp.where(at_north, 0.0, pltpu.roll(x, NR - 1, 0))
    south = lambda x: jnp.where(at_south, 0.0, pltpu.roll(x, 1, 0))
    across = lambda fu, fv: TAU * (fu - west(fu) + fv)
    rest = sf - TAU * (te - west(te) + tn - south(tn))
    rest = rest - ((4.0 + dg) * sf - (east(sf) + west(sf) + north(sf) + south(sf)))
    rest = rest - jnp.where(at_south, TAU * south_v, 0.0)
    rest_out[...] = rest
    diag_out[...] = dg
    first = TAU * tn[NR - 1 :] + sf[NR - 1 :] + across(north_u, north_v)
    second = -TAU * north_v
    to_south = sf[:1] + across(south_u, south_v)
    zero = jnp.zeros((5, 2 * NC), jnp.float32)
    edge_out[...] = jnp.concatenate([first, second, to_south, zero], axis=0)
    msg_north = jnp.concatenate([rest[8:], dg[11:], first, second, zero[:1]], axis=0)
    msg_south = jnp.concatenate([rest[:9], dg[:6], to_south], axis=0)
    for n, (out, lines) in enumerate(
        (
            (a_out, jnp.where(even, msg_north, msg_south)),
            (b_out, jnp.where(even, msg_south, msg_north)),
        )
    ):
        out[:NR, :] = lines[:, :NC]
        out[NR : 2 * NR, :] = lines[:, NC:]
        out[2 * NR :, :] = corner_out[64 * n : 64 * (n + 1), :]


def solve_kernel(pc, th, corner, rest, dg, edge, from_a, from_b, v_hbm, dots_out, v_out, sem):
    rows, wide = 2 * NR, 2 * NC
    even = even_lat()
    exists = b_exists()
    msg_a = jnp.concatenate([from_a[:NR, :], from_a[NR : 2 * NR, :]], axis=1)
    msg_b = jnp.concatenate([from_b[:NR, :], from_b[NR : 2 * NR, :]], axis=1) * exists
    north = jnp.where(even, msg_a, msg_b)
    south = jnp.where(even, msg_b, msg_a)
    zeros = lambda n: jnp.zeros((n, wide), jnp.float32)
    row = row_of((rows + 8, wide))
    lat = lat_index()
    low = jnp.where(lat == 0, 8, 0)
    high = jnp.where(lat == 15, 8 + NR, rows + 8)
    inside = jnp.where(jnp.logical_and(row >= low, row < high), 1.0, 0.0).astype(jnp.float32)
    below = jnp.concatenate([south[:7], south[7:8] + edge[2:3]], axis=0)
    above = jnp.concatenate(
        [north[:1] + edge[0:1], north[1:2] + edge[1:2], north[2:9], zeros(7)], axis=0
    )
    own = rest[...] + jnp.concatenate([south[13:15], zeros(13), north[15:]], axis=0)
    res = jnp.concatenate([below, own, above], axis=0)
    group = lane_of((8, NC)) // 32
    weights = []
    for first in halves():
        line = None
        for g in range(4):
            part = th[pl.ds(pl.multiple_of(first + 8 * g, 8), 8), :]
            line = part if g == 0 else jnp.where(group == g, part, line)
        weights.append(DT_VISC * line)
    sums = []
    for n, got in enumerate((from_a, from_b)):
        total = None
        for h in range(2):
            here = [corner[64 * n + 32 * h + 8 * i : 64 * n + 32 * h + 8 * (i + 1), :] for i in range(4)]
            at = 2 * NR + 32 * (1 - h)
            there = [got[at + 8 * i : at + 8 * (i + 1), :] for i in range(4)]
            part = [x * weights[h] for x in face_in(here, there)]
            total = part if h == 0 else [x + y for x, y in zip(total, part)]
        for x in total:
            x = jnp.sum(x, axis=0, keepdims=True)
            x = x + pltpu.roll(x, 32, 1)
            x = x + pltpu.roll(x, 64, 1)
            edge_lane = lane_of((1, NC))
            near = jnp.logical_or(edge_lane < 16, edge_lane >= NC - 16)
            x = jnp.where(near, pltpu.roll(x, NC - 16, 1), 0.0)
            sums.append(jnp.concatenate([jnp.zeros((1, NC), jnp.float32), x], axis=1))
    sums[2] = sums[2] * exists
    sums[3] = sums[3] * exists
    north_u, north_v = (jnp.where(even, sums[i], sums[i + 2]) for i in range(2))
    south_u, south_v = (jnp.where(even, sums[i + 2], sums[i]) for i in range(2))
    across = lambda fu, fv: TAU * (fu - pltpu.roll(fu, 1, 1) + fv)
    for at, line in (
        (7 + NR, -across(north_u, north_v)),
        (8 + NR, across(north_u, north_v) + TAU * north_v),
        (9 + NR, -TAU * north_v),
        (7, across(south_u, south_v)),
        (8, -across(south_u, south_v) - TAU * south_v),
        (9, TAU * south_v),
    ):
        res = res + jnp.where(row == at, line, 0.0)
    res = res * inside
    inside = inside[:rows]
    diag = 4.0 + jnp.concatenate([zeros(3), south[8:13], dg[...], north[9:15], zeros(2)], axis=0)

    def lon_shift(x, n):
        return x if n == 0 else pltpu.roll(x, (-n) % wide, 1)

    def lat_shift(x, n):
        return x if n == 0 else pltpu.roll(x, (-n) % x.shape[0], 0)

    def operate(x):
        near = lon_shift(x, 1) + lon_shift(x, -1) + lat_shift(x, 1) + lat_shift(x, -1)
        return diag * x - near

    def tap(a, b):
        at = 5 * (a + 2) + b + 2
        return pc[at : at + 1, :]

    def precondition(x):
        moved = [lon_shift(x, b) for b in range(-2, 3)]
        total = None
        for a in range(-2, 3):
            line = tap(a, -2) * moved[0]
            for b in range(1, 5):
                line = line + tap(a, b - 2) * moved[b]
            line = lat_shift(line, a)[:rows]
            total = line if total is None else total + line
        return total * inside

    scale = 1.0 / (5.0 * tap(0, 0))
    p0 = res
    v0 = precondition(p0)
    a0 = operate(v0)
    p1 = (a0 * scale - SHIFTS[0] * p0[:rows]) * inside
    v1 = precondition(p1)
    a1 = operate(v1)
    p2 = (a1 * scale - SHIFTS[1] * p1) * inside
    v2 = precondition(p2)
    mine = lambda x: x[8 : 8 + NR, :NC]
    half_a2 = mine(diag * v2 - 2.0 * (lon_shift(v2, 1) + lat_shift(v2, 1)))
    v0, v1, v2, a0, a1, r = (mine(x) for x in (v0, v1, v2, a0, a1, p0))
    v_out[0] = v0
    v_out[1] = v1
    v_out[2] = v2
    pairs = ((v0, a0), (v0, a1), (v2, a0), (v1, a1), (v2, a1), (v2, half_a2), (v0, r), (v1, r), (v2, r))
    copy = pltpu.make_async_copy(v_out, v_hbm, sem)
    copy.start()
    lane = lane_of((1, NC))
    line = jnp.zeros((1, NC), jnp.float32)
    for i, (x, y) in enumerate(pairs):
        total = jnp.sum(jnp.sum(x * y, axis=0, keepdims=True), axis=1, keepdims=True)
        line = line + jnp.where(lane == i, total, 0.0)
    dots_out[...] = jnp.broadcast_to(line[None], dots_out.shape)
    copy.wait()


def relay_kernel(got, out):
    out[...] = jnp.broadcast_to(jnp.sum(got[...], axis=0, keepdims=True)[:, :1], out.shape)


def step_kernel(got, v, sf, out):
    line = jnp.sum(got[...], axis=0)
    lane = lane_of((1, NC))
    h00, h01, h02, h11, h12, h22, g0, g1, g2 = (
        jnp.sum(jnp.where(lane == i, line, 0.0), axis=1, keepdims=True) for i in range(9)
    )
    l1 = h01 / h00
    l2 = h02 / h00
    d1 = h11 - l1 * h01
    e12 = h12 - l1 * h02
    l3 = e12 / d1
    d2 = h22 - l2 * h02 - l3 * e12
    y1 = g1 - l1 * g0
    y2 = g2 - l2 * g0 - l3 * y1
    c2 = y2 / d2
    c1 = y1 / d1 - l3 * c2
    c0 = g0 / h00 - l1 * c1 - l2 * c2
    out[...] = sf[...] + c0 * v[0] + c1 * v[1] + c2 * v[2]


def row_masks():
    lane, row = lane_of((NR, NC)), row_of((NR, NC))
    return lane == NC - 1, lane == 0, row == NR - 1, row == 0


def spread_of(packed, lines):
    at_east, at_west, at_north, at_south = row_masks()

    def spread(k, flux_e, flux_n, i):
        side = pltpu.roll(packed[i], NC - 1 - 2 * k, 1)
        north = jnp.broadcast_to(lines[2 * i, pl.ds(k, 1), :], (NR, NC))
        south = jnp.broadcast_to(lines[2 * i + 1, pl.ds(k, 1), :], (NR, NC))
        flux_e = jnp.where(at_east, side, flux_e)
        flux_n = jnp.where(at_north, north, flux_n)
        back_e = jnp.where(at_west, side, pltpu.roll(flux_e, 1, 1))
        back_n = jnp.where(at_south, south, pltpu.roll(flux_n, 1, 0))
        return flux_e - back_e + (flux_n - back_n)

    return spread


def write_out(body, pairs, sems, unroll, first=0, count=NZ):
    per = NZ // CHUNKS
    all_copies = chunk_copies(pairs, sems)
    copies = lambda c: all_copies(first // per + c)

    def chunk(c, carry):
        lax.fori_loop(0, per, lambda i, x: body(first + c * per + i, x), 0, unroll=unroll)
        for copy in copies(c):
            copy.start()
        return carry

    def finish(c, carry):
        for copy in copies(c):
            copy.wait()
        return carry

    lax.fori_loop(0, count // per, chunk, 0)
    lax.fori_loop(0, count // per, finish, 0)


def velocity_kernel(early, u, v, vi, w, lon, msg_a, msg_b, from_a, from_b, *rest):
    u_hbm, v_hbm, u_out, v_out, packed, lines, sems = rest[0 if early else 2 :]
    is_east = lane_of((NR, NC)) % 2 == 0
    own = [lon[i] for i in range(4)]
    other = [edge_across(msg_a, msg_b, i) for i in range(4)]
    for i, grad in enumerate(face_in(own, other)):
        packed[i] = DT_VISC * jnp.where(is_east, grad, -grad)
    even = even_lat()
    exists = b_exists()
    mine, theirs = halves()
    first = theirs if early else mine
    at = pl.ds(first, HALF)
    for side in range(2):
        use_a = even if side == 0 else jnp.logical_not(even)
        here = [edge_row(ref, side == 0, 0, first, HALF) for ref in (u, v, vi, w)]
        there = [jnp.where(use_a, from_a[i], from_b[i] * exists) for i in range(4)]
        sign = DT_VISC if side == 0 else -DT_VISC
        for i, grad in enumerate(face_in(here, there)):
            lines[2 * i + side, at, :] = sign * grad
    spread = spread_of(packed, lines)
    lon_up = lambda x: pltpu.roll(x, NC - 1, 1)
    lat_up = lambda x: pltpu.roll(x, NR - 1, 0)

    def body(k, carry):
        at = level(k)
        uu, vv, visc = u[at, :], v[at, :], vi[at, :]
        wet = w[at, :].astype(jnp.float32)
        half = wet * (0.5 * DT_VISC)
        face_e = (visc + lon_up(visc)) * (half * lon_up(wet))
        face_n = (visc + lat_up(visc)) * (half * lat_up(wet))
        u_out[at, :] = wet * (uu + spread(k, face_e * (lon_up(uu) - uu), face_n * (lat_up(uu) - uu), 0))
        v_out[at, :] = wet * (vv + spread(k, face_e * (lon_up(vv) - vv), face_n * (lat_up(vv) - vv), 1))
        return carry

    write_out(body, ((u_out, u_hbm), (v_out, v_hbm)), sems, 8, first, HALF)


def tracer_kernel(
    t, u, v, w, lon, msg_a, msg_b, lon2, lon2_a, lon2_b, from_a, from_a2, from_b, from_b2,
    t_hbm, t_out, packed, lines, sems,
):
    is_east = lane_of((NR, NC)) % 2 == 0
    by = DT_ADV / 12.0
    packed[1] = beyond(lon2_a[0], lon2_b[0])
    far = lon2[1] + beyond(lon2_a[1], lon2_b[1])
    speed = jnp.where(is_east, lon[0], edge_across(msg_a, msg_b, 0))
    wets = edge_across(msg_a, msg_b, 3) * lon[3]
    packed[0] = speed * far * (by * wets)
    even = even_lat()
    exists = b_exists()
    mine, theirs = halves()
    for first, there_a, there_b in ((mine, from_a2, from_b2), (theirs, from_a, from_b)):
        at = pl.ds(first, HALF)
        part = first // HALF
        for side in range(2):
            north = side == 0
            use_a = even if north else jnp.logical_not(even)
            wet_here = edge_row(w, north, 0, first, HALF)
            wet_there = jnp.where(use_a, there_a[3], there_b[3] * exists)
            near = edge_row(t, north, 0, first, HALF) * wet_here
            inner = edge_row(t, north, 1, first, HALF) * edge_row(w, north, 1, first, HALF)
            far = jnp.where(use_a, from_a2[6 + part], from_b2[6 + part]) + (7.0 * near - inner)
            if north:
                speed = edge_row(v, True, 0, first, HALF)
            else:
                speed = jnp.where(use_a, there_a[1], there_b[1])
            lines[side, at, :] = speed * far * (by * wet_here * wet_there)
            lines[2 + side, at, :] = jnp.where(use_a, from_a2[4 + part], from_b2[4 + part] * exists)
    spread = spread_of(packed, lines)
    at_east, at_west, at_north, at_south = row_masks()
    lon_up = lambda x: pltpu.roll(x, NC - 1, 1)
    lat_up = lambda x: pltpu.roll(x, NR - 1, 0)

    def body(k, carry):
        at = level(k)
        tt = t[at, :]
        wet = w[at, :].astype(jnp.float32)
        wt = tt * wet
        side = pltpu.roll(packed[1], NC - 1 - 2 * k, 1)
        north = jnp.broadcast_to(lines[2, pl.ds(k, 1), :], (NR, NC))
        south = jnp.broadcast_to(lines[3, pl.ds(k, 1), :], (NR, NC))
        t_e = jnp.where(at_east, side, lon_up(wt))
        t_w = jnp.where(at_west, side, pltpu.roll(wt, 1, 1))
        t_n = jnp.where(at_north, north, lat_up(wt))
        t_s = jnp.where(at_south, south, pltpu.roll(wt, 1, 0))
        part = by * wet
        flux_e = u[at, :] * (7.0 * (wt + t_e) - (t_w + lon_up(t_e))) * (part * lon_up(wet))
        flux_n = v[at, :] * (7.0 * (wt + t_n) - (t_s + lat_up(t_n))) * (part * lat_up(wet))
        t_out[at, :] = wet * (tt - spread(k, flux_e, flux_n, 0))
        return carry

    write_out(body, ((t_out, t_hbm),), sems, 8)


def local(tracer, east_vel, north_vel, viscosity, land_sea, thickness, surface, surface_diag, precond_kernel):
    flat = (NZ * NR, NC)
    u, v, vi, w, t = (x.reshape(flat) for x in (east_vel, north_vel, viscosity, land_sea, tracer))
    block = NZ * NR * NC * 4
    field = pltpu.VMEM(flat, jnp.float32)
    wets = pltpu.VMEM(flat, jnp.int32)
    dma = pltpu.SemaphoreType.DMA
    rows = (4, HALF, NC)
    late = (8, HALF, NC)
    lon, a, b, corners = call(
        fetch_kernel,
        [(4, NR, NC), rows, rows, (16, 8, NC)],
        [HBM] * 4,
        20 * NZ * NR * NC,
        4 * block,
        [field] * 3 + [wets, dma((CHUNKS, 4))],
        vmem=FETCH_VMEM,
    )(u, v, vi, w)
    from_b = lax.ppermute(b, LAT, SWAP_B)
    from_a = lax.ppermute(a, LAT, SWAP_A)
    inner, to_a, to_b, th = call(
        inner_kernel,
        [(2, NR, NC), (MSG, NC), (MSG, NC), (NZ + 8, NC)],
        [SM] + [VM] * 8,
        40 * NZ * NR * NC,
        4 * block,
    )(thickness, u, v, vi, w, lon, corners, surface, surface_diag)
    msg_b = lax.ppermute(to_b, LON, SWAP_B)
    msg_a = lax.ppermute(to_a, LON, SWAP_A)
    lon2, a2, b2 = call(
        late_kernel, [(2, NR, NC), late, late], [VM] * 5, 20 * NZ * NR * NC, 2 * block
    )(t, u, v, vi, w)
    lon2_b = lax.ppermute(lon2, LON, SWAP_B)
    lon2_a = lax.ppermute(lon2, LON, SWAP_A)
    msg_a, msg_b, a2, b2 = lax.optimization_barrier((msg_a, msg_b, a2, b2))
    wide = (NR, 2 * NC)
    rest, dg, edge, corner, side_a, side_b = call(
        side_kernel,
        [wide, wide, (8, 2 * NC), (128, NC), (LAT_MSG, NC), (LAT_MSG, NC)],
        [VM] * 13,
        10**6,
        10**5,
    )(inner, lon, surface, surface_diag, msg_a, msg_b, u, v, vi, w, from_a, from_b, th)
    got_b = lax.ppermute(side_b, LAT, SWAP_B)
    got_a = lax.ppermute(side_a, LAT, SWAP_A)
    (taps,) = call(taps_kernel, [(32, 2 * NC)], [SM], 10**4, 10**4)(precond_kernel)
    def velocity(early, edges, written):
        return call(
            functools.partial(velocity_kernel, early),
            [flat] * 2,
            [VM] * 9 + [HBM] * len(written),
            30 * NZ * NR * NC,
            3 * block,
            [field] * 2
            + [pltpu.VMEM((2, NR, NC), jnp.float32), pltpu.VMEM((4, NZ, NC), jnp.float32), dma((CHUNKS, 2))],
            HBM,
            aliases={9 + i: i for i in range(len(written))},
        )(u, v, vi, w, lon, msg_a, msg_b, *edges, *written)

    u_half, v_half = velocity(True, (from_a, from_b), ())
    got_a, got_b, u_half, v_half, lon2_a, lon2_b = lax.optimization_barrier(
        (got_a, got_b, u_half, v_half, lon2_a, lon2_b)
    )
    vecs, dots = call(
        solve_kernel,
        [(3, NR, NC), (32, 8, NC)],
        [VM] * 8,
        10**6,
        10**5,
        [pltpu.VMEM((3, NR, NC), jnp.float32), dma],
        [HBM, VM],
    )(taps, th, corner, rest, dg, edge, got_a, got_b)
    dots, a2, b2 = lax.optimization_barrier((dots, a2, b2))
    from_b2 = lax.ppermute(b2, LAT, SWAP_B)
    from_a2 = lax.ppermute(a2, LAT, SWAP_A)
    dots = lax.all_to_all(dots, ("x", "y", "c"), 0, 0)
    lat = (from_a, from_a2, from_b, from_b2)
    u_new, v_new = velocity(False, (from_a2, from_b2), (u_half, v_half))
    t_new = call(
        tracer_kernel,
        [flat],
        [VM] * 14,
        60 * NZ * NR * NC,
        5 * block,
        [field, pltpu.VMEM((2, NR, NC), jnp.float32), pltpu.VMEM((4, NZ, NC), jnp.float32), dma((CHUNKS, 1))],
        HBM,
    )(t, u, v, w, lon, msg_a, msg_b, lon2, lon2_a, lon2_b, *lat)[0]
    (dots,) = call(relay_kernel, [(8, 1, NC)], [VM], 10**4, 10**4)(dots)
    dots = lax.all_to_all(dots, ("zl", "zh"), 0, 0)
    dots, t_new, u_new, v_new = lax.optimization_barrier((dots, t_new, u_new, v_new))
    (surface_new,) = call(step_kernel, [(NR, NC)], [VM] * 3, 10**5, 10**4)(dots, vecs, surface)
    shape = (NZ, NR, NC)
    return t_new.reshape(shape), u_new.reshape(shape), v_new.reshape(shape), surface_new


def solution(mesh):
    sizes = dict(mesh.shape)
    assert sizes == {"lon": 16, "lat": 16} and tuple(mesh.axis_names) == ("lon", "lat")
    fine = Mesh(mesh.devices.reshape(2, 4, 2, 4, 4), ("zl", "x", "c", "y", "zh"))
    deep = P(None, LAT, LON)
    flat = P(LAT, LON)
    return jax.shard_map(
        local,
        mesh=fine,
        in_specs=(deep,) * 5 + (P(), flat, flat, P()),
        out_specs=(deep, deep, deep, flat),
        check_vma=False,
    )
```

```python
import functools

import jax
import jax.numpy as jnp
from jax import lax
from jax.experimental import pallas as pl
from jax.experimental.pallas import tpu as pltpu
from jax.sharding import Mesh
from jax.sharding import PartitionSpec as P

DT_ADV = 0.25
DT_VISC = 0.2
TAU = 0.05
SHIFTS = (0.3, 1.3)

LON = ("zl", "x", "c")
LAT = ("y", "zh")
NZ, NR, NC = 64, 16, 128
SWAP_A = [(i, i ^ 1) for i in range(16)]
SWAP_B = [(i, (i + 1) % 16 if i % 2 else (i - 1) % 16) for i in range(16)]

VM = pl.BlockSpec(memory_space=pltpu.VMEM)
SM = pl.BlockSpec(memory_space=pltpu.SMEM)
HBM = pl.BlockSpec(memory_space=pltpu.HBM)
FETCH_VMEM = 53.25


def call(kernel, outs, specs, flops, nbytes, scratch=(), place=VM, vmem=4, aliases=None):
    return pl.pallas_call(
        kernel,
        out_shape=[jax.ShapeDtypeStruct(s, jnp.float32) for s in outs],
        in_specs=specs,
        out_specs=place if isinstance(place, list) else [place] * len(outs),
        scratch_shapes=list(scratch),
        input_output_aliases=aliases or {},
        compiler_params=pltpu.CompilerParams(vmem_limit_bytes=int(vmem * 1024 * 1024)),
        cost_estimate=pl.CostEstimate(flops=flops, bytes_accessed=nbytes, transcendentals=0),
    )


def lane_of(shape):
    return lax.broadcasted_iota(jnp.int32, shape, len(shape) - 1)


def row_of(shape):
    return lax.broadcasted_iota(jnp.int32, shape, len(shape) - 2)


def even_lon():
    return lax.axis_index("c") == 0


def even_lat():
    return lax.axis_index("zh") % 2 == 0


def lat_index():
    return lax.axis_index("y") * 4 + lax.axis_index("zh")


def b_exists():
    lat = lat_index()
    return jnp.where(jnp.logical_or(lat == 0, lat == 15), 0.0, 1.0).astype(jnp.float32)


HALF = NZ // 2
CHUNKS = 4


def halves():
    mine = jnp.where(even_lat(), 0, HALF)
    return pl.multiple_of(mine, HALF), pl.multiple_of(HALF - mine, HALF)


def edge_row(ref, north, inwards, first, count):
    if isinstance(north, bool):
        row = NR - 1 - inwards if north else inwards
    else:
        row = jnp.where(north, NR - 1 - inwards, inwards)
    return ref[pl.ds(first * NR + row, count, stride=NR), :].astype(jnp.float32)


def pipeline(copies, body, acc, unroll):
    per = NZ // CHUNKS

    def start(c, carry):
        for copy in copies(c):
            copy.start()
        return carry

    def chunk(c, carry):
        for copy in copies(c):
            copy.wait()
        return lax.fori_loop(0, per, lambda i, x: body(c * per + i, x), carry, unroll=unroll)

    lax.fori_loop(0, CHUNKS, start, 0)
    return lax.fori_loop(0, CHUNKS, chunk, acc)


def chunk_copies(pairs, sems):
    span = NZ * NR // CHUNKS

    def copies(c):
        at = pl.ds(pl.multiple_of(c * span, span), span)
        return [
            pltpu.make_async_copy(src.at[at], dst.at[at], sems.at[c, i])
            for i, (src, dst) in enumerate(pairs)
        ]

    return copies


def level(k):
    return pl.ds(pl.multiple_of(k * NR, NR), NR)


def squeeze(rows, shift):
    group = lane_of((8, NC)) // 32
    out = None
    for g in range(4):
        part = pltpu.roll(rows[8 * g : 8 * g + 8], (shift + 32 * g) % NC, 1)
        out = part if g == 0 else jnp.where(group == g, part, out)
    return out


def fetch_kernel(u, v, vi, land, lon_out, a_out, b_out, other_a, other_b, corners, uo, vo, vio, lo, sems):
    pair = lane_of((NR, NC)) // 2

    def body(k, acc):
        at = level(k)
        values = (uo[at, :], vo[at, :], vio[at, :], lo[at, :].astype(jnp.float32))
        mine = pair == k
        return tuple(
            jnp.where(mine, pltpu.roll(x, 2 * k + 1, 1), old) for x, old in zip(values, acc)
        )

    copies = chunk_copies(((u, uo), (v, vo), (vi, vio), (land, lo)), sems)
    acc = pipeline(copies, body, (jnp.zeros((NR, NC), jnp.float32),) * 4, 8)
    for i in range(4):
        lon_out[i] = acc[i]
    even = even_lat()
    mine, theirs = halves()
    for north, first, rest in ((even, a_out, other_a), (jnp.logical_not(even), b_out, other_b)):
        for i, ref in enumerate((uo, vo, vio, lo)):
            first[i] = edge_row(ref, north, 0, mine, HALF)
            rest[i] = edge_row(ref, north, 0, theirs, HALF)
    for n, ref in enumerate((a_out, other_a, b_out, other_b)):
        for i in range(4):
            corners[4 * n + i] = squeeze(ref[i], 16)


AT_CORNER, AT_FIELDS, MSG = 32, 96, 112


def put_side_by_side(first, second, step, high):
    left = lane_of(first.shape) % (2 * step) < step
    high_pair = jnp.where(left, first, pltpu.roll(second, step, 1))
    low_pair = jnp.where(left, pltpu.roll(first, NC - step, 1), second)
    return jnp.where(high, high_pair, low_pair)


def take_across(east, west, which, step, east_first):
    left = lane_of(east.shape) % (2 * step) < step
    place = 0 if east_first else 1
    east = east if which == place else pltpu.roll(east, step if which < place else NC - step, 1)
    west = west if which != place else pltpu.roll(west, NC - step if which else step, 1)
    return jnp.where(left, east, west) if east_first else jnp.where(left, west, east)


def inner_kernel(thick, u, v, vi, w, lon, corners, sf, dg, out, msg_a, msg_b, th_out):
    lane, row = lane_of((NR, NC)), row_of((NR, NC))
    pair = lane[:1] // 2
    up = lambda x: pltpu.roll(x, NC - 1, 1)
    north_of = lambda x: pltpu.roll(x, NR - 1, 0)

    def body(k, acc):
        at = level(k)
        wet, uu, vv, visc = w[at, :].astype(jnp.float32), u[at, :], v[at, :], vi[at, :]
        th = jnp.full((1, NC), thick[k], jnp.float32)
        th_out[pl.ds(k, 1), :] = th
        own = wet * th
        half = 0.5 * own
        east = (visc + up(visc)) * (half * up(wet))
        north = (visc + north_of(visc)) * (half * north_of(wet))
        return (
            acc[0] + own * uu,
            acc[1] + east * (up(uu) - uu),
            acc[2] + north * (north_of(uu) - uu),
            acc[3] + own * vv,
            acc[4] + east * (up(vv) - vv),
            acc[5] + north * (north_of(vv) - vv),
            jnp.where(pair == k, th, acc[6]),
        )

    zero = jnp.zeros((NR, NC), jnp.float32)
    acc = lax.fori_loop(0, NZ, body, (zero,) * 6 + (zero[:1],), unroll=16)
    th_out[NZ:, :] = jnp.broadcast_to(acc[6], (8, NC))
    for i in range(2):
        east = jnp.where(lane == NC - 1, 0.0, acc[3 * i + 1])
        north = jnp.where(row == NR - 1, 0.0, acc[3 * i + 2])
        out[i] = acc[3 * i] + DT_VISC * (
            east - pltpu.roll(east, 1, 1) + north - pltpu.roll(north, 1, 0)
        )
    fields = (out[0], out[1], sf[...], dg[...])
    for msg, high in ((msg_a, even_lon()), (msg_b, jnp.logical_not(even_lon()))):
        for i in range(2):
            msg[NR * i : NR * (i + 1), :] = put_side_by_side(lon[2 * i], lon[2 * i + 1], 1, high)
        for n in range(2):
            for i in range(4):
                at = AT_CORNER + 32 * n + 8 * i
                first, second = corners[8 * n + i], corners[8 * n + 4 + i]
                msg[at : at + 8, :] = put_side_by_side(first, second, 16, high)
        line = None
        for f, x in enumerate(fields):
            part = jnp.where(high, pltpu.roll(x, 16 * (f + 1) % NC, 1), pltpu.roll(x, 16 * f, 1) if f else x)
            line = part if f == 0 else jnp.where(lane // 16 == f, part, line)
        msg[AT_FIELDS:, :] = line


def late_kernel(t, w, other_a, other_b, lon_out, a_out, b_out):
    lane = lane_of((NR, NC))
    pair = lane // 2
    half_lane = lane < NC // 2

    def body(k, acc):
        at = level(k)
        first = t[at, :] * w[at, :].astype(jnp.float32)
        inner = jnp.where(half_lane, pltpu.roll(first, NC - 1, 1), pltpu.roll(first, 1, 1))
        mine = pair == k
        return tuple(
            jnp.where(mine, pltpu.roll(x, 2 * k + 1, 1), old)
            for x, old in zip((first, 7.0 * first - inner), acc)
        )

    acc = lax.fori_loop(0, NZ, body, (jnp.zeros((NR, NC), jnp.float32),) * 2, unroll=8)
    lon_out[0] = acc[0]
    lon_out[1] = acc[1]
    even = even_lat()
    for north, src, dst in ((even, other_a, a_out), (jnp.logical_not(even), other_b, b_out)):
        dst[:4] = src[...]
        for i in range(2):
            near, inner = (
                edge_row(t, north, n, i * HALF, HALF) * edge_row(w, north, n, i * HALF, HALF)
                for n in range(2)
            )
            dst[4 + i] = near
            dst[6 + i] = 7.0 * near - inner


def taps_kernel(pc, out):
    for i in range(25):
        out[i : i + 1, :] = jnp.full((1, 2 * NC), pc[i // 5, i % 5], jnp.float32)


def lon_sides(first, second):
    even = even_lon()
    return jnp.where(even, first, second), jnp.where(even, second, first)


def beyond(from_a, from_b):
    east, west = lon_sides(from_a, from_b)
    is_east = lane_of((NR, NC)) % 2 == 0
    return jnp.where(is_east, pltpu.roll(east, NC - 1, 1), pltpu.roll(west, 1, 1))


def edge_across(msg_a, msg_b, i):
    at = slice(NR * (i // 2), NR * (i // 2 + 1))
    return take_across(*lon_sides(msg_a[at, :], msg_b[at, :]), i % 2, 1, True)


def face_in(own, other):
    face = 0.5 * (own[2] + other[2]) * (own[3] * other[3])
    return face * (other[0] - own[0]), face * (other[1] - own[1])


LAT_MSG = 96


def side_kernel(
    inner, lon, sf_own, dg_own, msg_a, msg_b, a2, from_a, b2, from_b, th,
    rest_out, diag_out, edge_out, corner_out, a_out, b_out,
):
    lane = lane_of((NR, NC))
    is_east = lane % 2 == 0
    packed = [lon[i] for i in range(4)]
    other = [edge_across(msg_a, msg_b, i) for i in range(4)]
    far_east, far_west = lon_sides(msg_a[AT_FIELDS:, :], msg_b[AT_FIELDS:, :])

    def widen(own, f):
        east = pltpu.roll(far_east, (NC - 16 * f) % NC, 1) if f else far_east
        west = pltpu.roll(far_west, (NC - 16 - 16 * f) % NC, 1)
        halo = jnp.where(lane < 16, east, jnp.where(lane >= NC - 16, west, 0.0))
        return jnp.concatenate([own, halo], axis=1)

    wide_lane = lane_of((NR, 2 * NC))
    te, tn = widen(inner[0], 0), widen(inner[1], 1)
    sf, dg = widen(sf_own[...], 2), widen(dg_own[...], 3)
    add = []
    for grad in face_in(packed, other):
        grad = grad * (DT_VISC * th[NZ : NZ + 1, :])
        east = jnp.sum(jnp.where(is_east, grad, 0.0), axis=1, keepdims=True)
        west = jnp.sum(jnp.where(is_east, 0.0, grad), axis=1, keepdims=True)
        here = jnp.where(wide_lane == NC - 1, east, 0.0) + jnp.where(wide_lane == 0, west, 0.0)
        there = jnp.where(wide_lane == NC, east, 0.0) + jnp.where(wide_lane == 2 * NC - 1, west, 0.0)
        add.append(here - there)
    te = te + add[0]
    tn = tn + add[1]
    _, theirs = halves()
    weight = DT_VISC * th[pl.ds(theirs, HALF), :]
    lat_a = face_in([a2[i] for i in range(4)], [from_a[i] for i in range(4)])
    weight_b = weight * b_exists()
    lat_b = face_in([b2[i] for i in range(4)], [from_b[i] for i in range(4)])
    faces = [jnp.sum(x * weight, axis=0, keepdims=True) for x in lat_a]
    faces += [jnp.sum(x * weight_b, axis=0, keepdims=True) for x in lat_b]
    faces = [jnp.concatenate([x, jnp.zeros((1, NC), jnp.float32)], axis=1) for x in faces]
    for n in range(2):
        for i in range(4):
            at = AT_CORNER + 32 * n + 8 * i
            sides = lon_sides(msg_a[at : at + 8, :], msg_b[at : at + 8, :])
            for h in range(2):
                to = 64 * n + 32 * h + 8 * i
                corner_out[to : to + 8, :] = take_across(*sides, h, 16, False)
    row = row_of((NR, 2 * NC))
    even = even_lat()
    north_u, north_v = (jnp.where(even, faces[i], faces[i + 2]) for i in range(2))
    south_u, south_v = (jnp.where(even, faces[i + 2], faces[i]) for i in range(2))
    at_north, at_south = row == NR - 1, row == 0
    te = te + jnp.where(at_north, north_u, 0.0) + jnp.where(at_south, south_u, 0.0)
    tn = tn + jnp.where(at_north, north_v, 0.0) + jnp.where(at_south, south_v, 0.0)
    east = lambda x: pltpu.roll(x, 2 * NC - 1, 1)
    west = lambda x: pltpu.roll(x, 1, 1)
    north = lambda x: jnp.where(at_north, 0.0, pltpu.roll(x, NR - 1, 0))
    south = lambda x: jnp.where(at_south, 0.0, pltpu.roll(x, 1, 0))
    across = lambda fu, fv: TAU * (fu - west(fu) + fv)
    rest = sf - TAU * (te - west(te) + tn - south(tn))
    rest = rest - ((4.0 + dg) * sf - (east(sf) + west(sf) + north(sf) + south(sf)))
    rest = rest - jnp.where(at_south, TAU * south_v, 0.0)
    rest_out[...] = rest
    diag_out[...] = dg
    first = TAU * tn[NR - 1 :] + sf[NR - 1 :] + across(north_u, north_v)
    second = -TAU * north_v
    to_south = sf[:1] + across(south_u, south_v)
    zero = jnp.zeros((5, 2 * NC), jnp.float32)
    edge_out[...] = jnp.concatenate([first, second, to_south, zero], axis=0)
    msg_north = jnp.concatenate([rest[8:], dg[11:], first, second, zero[:1]], axis=0)
    msg_south = jnp.concatenate([rest[:9], dg[:6], to_south], axis=0)
    for n, (out, lines) in enumerate(
        (
            (a_out, jnp.where(even, msg_north, msg_south)),
            (b_out, jnp.where(even, msg_south, msg_north)),
        )
    ):
        out[:NR, :] = lines[:, :NC]
        out[NR : 2 * NR, :] = lines[:, NC:]
        out[2 * NR :, :] = corner_out[64 * n : 64 * (n + 1), :]


def solve_kernel(pc, th, corner, rest, dg, edge, from_a, from_b, v_hbm, dots_out, v_out, sem):
    rows, wide = 2 * NR, 2 * NC
    even = even_lat()
    exists = b_exists()
    msg_a = jnp.concatenate([from_a[:NR, :], from_a[NR : 2 * NR, :]], axis=1)
    msg_b = jnp.concatenate([from_b[:NR, :], from_b[NR : 2 * NR, :]], axis=1) * exists
    north = jnp.where(even, msg_a, msg_b)
    south = jnp.where(even, msg_b, msg_a)
    zeros = lambda n: jnp.zeros((n, wide), jnp.float32)
    row = row_of((rows + 8, wide))
    lat = lat_index()
    low = jnp.where(lat == 0, 8, 0)
    high = jnp.where(lat == 15, 8 + NR, rows + 8)
    inside = jnp.where(jnp.logical_and(row >= low, row < high), 1.0, 0.0).astype(jnp.float32)
    below = jnp.concatenate([south[:7], south[7:8] + edge[2:3]], axis=0)
    above = jnp.concatenate(
        [north[:1] + edge[0:1], north[1:2] + edge[1:2], north[2:9], zeros(7)], axis=0
    )
    own = rest[...] + jnp.concatenate([south[13:15], zeros(13), north[15:]], axis=0)
    res = jnp.concatenate([below, own, above], axis=0)
    group = lane_of((8, NC)) // 32
    weights = []
    for first in halves():
        line = None
        for g in range(4):
            part = th[pl.ds(pl.multiple_of(first + 8 * g, 8), 8), :]
            line = part if g == 0 else jnp.where(group == g, part, line)
        weights.append(DT_VISC * line)
    sums = []
    for n, got in enumerate((from_a, from_b)):
        total = None
        for h in range(2):
            here = [corner[64 * n + 32 * h + 8 * i : 64 * n + 32 * h + 8 * (i + 1), :] for i in range(4)]
            at = 2 * NR + 32 * (1 - h)
            there = [got[at + 8 * i : at + 8 * (i + 1), :] for i in range(4)]
            part = [x * weights[h] for x in face_in(here, there)]
            total = part if h == 0 else [x + y for x, y in zip(total, part)]
        for x in total:
            x = jnp.sum(x, axis=0, keepdims=True)
            x = x + pltpu.roll(x, 32, 1)
            x = x + pltpu.roll(x, 64, 1)
            edge_lane = lane_of((1, NC))
            near = jnp.logical_or(edge_lane < 16, edge_lane >= NC - 16)
            x = jnp.where(near, pltpu.roll(x, NC - 16, 1), 0.0)
            sums.append(jnp.concatenate([jnp.zeros((1, NC), jnp.float32), x], axis=1))
    sums[2] = sums[2] * exists
    sums[3] = sums[3] * exists
    north_u, north_v = (jnp.where(even, sums[i], sums[i + 2]) for i in range(2))
    south_u, south_v = (jnp.where(even, sums[i + 2], sums[i]) for i in range(2))
    across = lambda fu, fv: TAU * (fu - pltpu.roll(fu, 1, 1) + fv)
    for at, line in (
        (7 + NR, -across(north_u, north_v)),
        (8 + NR, across(north_u, north_v) + TAU * north_v),
        (9 + NR, -TAU * north_v),
        (7, across(south_u, south_v)),
        (8, -across(south_u, south_v) - TAU * south_v),
        (9, TAU * south_v),
    ):
        res = res + jnp.where(row == at, line, 0.0)
    res = res * inside
    inside = inside[:rows]
    diag = 4.0 + jnp.concatenate([zeros(3), south[8:13], dg[...], north[9:15], zeros(2)], axis=0)

    def lon_shift(x, n):
        return x if n == 0 else pltpu.roll(x, (-n) % wide, 1)

    def lat_shift(x, n):
        return x if n == 0 else pltpu.roll(x, (-n) % x.shape[0], 0)

    def operate(x):
        near = lon_shift(x, 1) + lon_shift(x, -1) + lat_shift(x, 1) + lat_shift(x, -1)
        return diag * x - near

    def tap(a, b):
        at = 5 * (a + 2) + b + 2
        return pc[at : at + 1, :]

    def precondition(x):
        moved = [lon_shift(x, b) for b in range(-2, 3)]
        total = None
        for a in range(-2, 3):
            line = tap(a, -2) * moved[0]
            for b in range(1, 5):
                line = line + tap(a, b - 2) * moved[b]
            line = lat_shift(line, a)[:rows]
            total = line if total is None else total + line
        return total * inside

    scale = 1.0 / (5.0 * tap(0, 0))
    p0 = res
    v0 = precondition(p0)
    a0 = operate(v0)
    p1 = (a0 * scale - SHIFTS[0] * p0[:rows]) * inside
    v1 = precondition(p1)
    a1 = operate(v1)
    p2 = (a1 * scale - SHIFTS[1] * p1) * inside
    v2 = precondition(p2)
    mine = lambda x: x[8 : 8 + NR, :NC]
    half_a2 = mine(diag * v2 - 2.0 * (lon_shift(v2, 1) + lat_shift(v2, 1)))
    v0, v1, v2, a0, a1, r = (mine(x) for x in (v0, v1, v2, a0, a1, p0))
    v_out[0] = v0
    v_out[1] = v1
    v_out[2] = v2
    pairs = ((v0, a0), (v0, a1), (v2, a0), (v1, a1), (v2, a1), (v2, half_a2), (v0, r), (v1, r), (v2, r))
    copy = pltpu.make_async_copy(v_out, v_hbm, sem)
    copy.start()
    lane = lane_of((1, NC))
    line = jnp.zeros((1, NC), jnp.float32)
    for i, (x, y) in enumerate(pairs):
        total = jnp.sum(jnp.sum(x * y, axis=0, keepdims=True), axis=1, keepdims=True)
        line = line + jnp.where(lane == i, total, 0.0)
    dots_out[...] = jnp.broadcast_to(line[None], dots_out.shape)
    copy.wait()


def relay_kernel(got, out):
    out[...] = jnp.broadcast_to(jnp.sum(got[...], axis=0, keepdims=True)[:, :1], out.shape)


def step_kernel(got, v, sf, out):
    line = jnp.sum(got[...], axis=0)
    lane = lane_of((1, NC))
    h00, h01, h02, h11, h12, h22, g0, g1, g2 = (
        jnp.sum(jnp.where(lane == i, line, 0.0), axis=1, keepdims=True) for i in range(9)
    )
    l1 = h01 / h00
    l2 = h02 / h00
    d1 = h11 - l1 * h01
    e12 = h12 - l1 * h02
    l3 = e12 / d1
    d2 = h22 - l2 * h02 - l3 * e12
    y1 = g1 - l1 * g0
    y2 = g2 - l2 * g0 - l3 * y1
    c2 = y2 / d2
    c1 = y1 / d1 - l3 * c2
    c0 = g0 / h00 - l1 * c1 - l2 * c2
    out[...] = sf[...] + c0 * v[0] + c1 * v[1] + c2 * v[2]


def row_masks():
    lane, row = lane_of((NR, NC)), row_of((NR, NC))
    return lane == NC - 1, lane == 0, row == NR - 1, row == 0


def spread_of(packed, lines):
    at_east, at_west, at_north, at_south = row_masks()

    def spread(k, flux_e, flux_n, i):
        side = pltpu.roll(packed[i], NC - 1 - 2 * k, 1)
        north = jnp.broadcast_to(lines[2 * i, pl.ds(k, 1), :], (NR, NC))
        south = jnp.broadcast_to(lines[2 * i + 1, pl.ds(k, 1), :], (NR, NC))
        flux_e = jnp.where(at_east, side, flux_e)
        flux_n = jnp.where(at_north, north, flux_n)
        back_e = jnp.where(at_west, side, pltpu.roll(flux_e, 1, 1))
        back_n = jnp.where(at_south, south, pltpu.roll(flux_n, 1, 0))
        return flux_e - back_e + (flux_n - back_n)

    return spread


def write_out(body, pairs, sems, unroll, first=0, count=NZ):
    per = NZ // CHUNKS
    all_copies = chunk_copies(pairs, sems)
    copies = lambda c: all_copies(first // per + c)

    def chunk(c, carry):
        lax.fori_loop(0, per, lambda i, x: body(first + c * per + i, x), 0, unroll=unroll)
        for copy in copies(c):
            copy.start()
        return carry

    def finish(c, carry):
        for copy in copies(c):
            copy.wait()
        return carry

    lax.fori_loop(0, count // per, chunk, 0)
    lax.fori_loop(0, count // per, finish, 0)


def velocity_kernel(early, u, v, vi, w, lon, msg_a, msg_b, from_a, from_b, *rest):
    u_hbm, v_hbm, u_out, v_out, packed, lines, sems = rest[0 if early else 2 :]
    is_east = lane_of((NR, NC)) % 2 == 0
    own = [lon[i] for i in range(4)]
    other = [edge_across(msg_a, msg_b, i) for i in range(4)]
    for i, grad in enumerate(face_in(own, other)):
        packed[i] = DT_VISC * jnp.where(is_east, grad, -grad)
    even = even_lat()
    exists = b_exists()
    mine, theirs = halves()
    first = theirs if early else mine
    at = pl.ds(first, HALF)
    for side in range(2):
        use_a = even if side == 0 else jnp.logical_not(even)
        here = [edge_row(ref, side == 0, 0, first, HALF) for ref in (u, v, vi, w)]
        there = [jnp.where(use_a, from_a[i], from_b[i] * exists) for i in range(4)]
        sign = DT_VISC if side == 0 else -DT_VISC
        for i, grad in enumerate(face_in(here, there)):
            lines[2 * i + side, at, :] = sign * grad
    spread = spread_of(packed, lines)
    lon_up = lambda x: pltpu.roll(x, NC - 1, 1)
    lat_up = lambda x: pltpu.roll(x, NR - 1, 0)

    def body(k, carry):
        at = level(k)
        uu, vv, visc = u[at, :], v[at, :], vi[at, :]
        wet = w[at, :].astype(jnp.float32)
        half = wet * (0.5 * DT_VISC)
        face_e = (visc + lon_up(visc)) * (half * lon_up(wet))
        face_n = (visc + lat_up(visc)) * (half * lat_up(wet))
        u_out[at, :] = wet * (uu + spread(k, face_e * (lon_up(uu) - uu), face_n * (lat_up(uu) - uu), 0))
        v_out[at, :] = wet * (vv + spread(k, face_e * (lon_up(vv) - vv), face_n * (lat_up(vv) - vv), 1))
        return carry

    write_out(body, ((u_out, u_hbm), (v_out, v_hbm)), sems, 8, first, HALF)


def tracer_kernel(
    t, u, v, w, lon, msg_a, msg_b, lon2, lon2_a, lon2_b, from_a, from_a2, from_b, from_b2,
    t_hbm, t_out, packed, lines, sems,
):
    is_east = lane_of((NR, NC)) % 2 == 0
    by = DT_ADV / 12.0
    packed[1] = beyond(lon2_a[0], lon2_b[0])
    far = lon2[1] + beyond(lon2_a[1], lon2_b[1])
    speed = jnp.where(is_east, lon[0], edge_across(msg_a, msg_b, 0))
    wets = edge_across(msg_a, msg_b, 3) * lon[3]
    packed[0] = speed * far * (by * wets)
    even = even_lat()
    exists = b_exists()
    mine, theirs = halves()
    for first, there_a, there_b in ((mine, from_a2, from_b2), (theirs, from_a, from_b)):
        at = pl.ds(first, HALF)
        part = first // HALF
        for side in range(2):
            north = side == 0
            use_a = even if north else jnp.logical_not(even)
            wet_here = edge_row(w, north, 0, first, HALF)
            wet_there = jnp.where(use_a, there_a[3], there_b[3] * exists)
            near = edge_row(t, north, 0, first, HALF) * wet_here
            inner = edge_row(t, north, 1, first, HALF) * edge_row(w, north, 1, first, HALF)
            far = jnp.where(use_a, from_a2[6 + part], from_b2[6 + part]) + (7.0 * near - inner)
            if north:
                speed = edge_row(v, True, 0, first, HALF)
            else:
                speed = jnp.where(use_a, there_a[1], there_b[1])
            lines[side, at, :] = speed * far * (by * wet_here * wet_there)
            lines[2 + side, at, :] = jnp.where(use_a, from_a2[4 + part], from_b2[4 + part] * exists)
    spread = spread_of(packed, lines)
    at_east, at_west, at_north, at_south = row_masks()
    lon_up = lambda x: pltpu.roll(x, NC - 1, 1)
    lat_up = lambda x: pltpu.roll(x, NR - 1, 0)

    def body(k, carry):
        at = level(k)
        tt = t[at, :]
        wet = w[at, :].astype(jnp.float32)
        wt = tt * wet
        side = pltpu.roll(packed[1], NC - 1 - 2 * k, 1)
        north = jnp.broadcast_to(lines[2, pl.ds(k, 1), :], (NR, NC))
        south = jnp.broadcast_to(lines[3, pl.ds(k, 1), :], (NR, NC))
        t_e = jnp.where(at_east, side, lon_up(wt))
        t_w = jnp.where(at_west, side, pltpu.roll(wt, 1, 1))
        t_n = jnp.where(at_north, north, lat_up(wt))
        t_s = jnp.where(at_south, south, pltpu.roll(wt, 1, 0))
        part = by * wet
        flux_e = u[at, :] * (7.0 * (wt + t_e) - (t_w + lon_up(t_e))) * (part * lon_up(wet))
        flux_n = v[at, :] * (7.0 * (wt + t_n) - (t_s + lat_up(t_n))) * (part * lat_up(wet))
        t_out[at, :] = wet * (tt - spread(k, flux_e, flux_n, 0))
        return carry

    write_out(body, ((t_out, t_hbm),), sems, 8)


def local(tracer, east_vel, north_vel, viscosity, land_sea, thickness, surface, surface_diag, precond_kernel):
    flat = (NZ * NR, NC)
    u, v, vi, w, t = (x.reshape(flat) for x in (east_vel, north_vel, viscosity, land_sea, tracer))
    block = NZ * NR * NC * 4
    field = pltpu.VMEM(flat, jnp.float32)
    wets = pltpu.VMEM(flat, jnp.int32)
    dma = pltpu.SemaphoreType.DMA
    rows = (4, HALF, NC)
    late = (8, HALF, NC)
    lon, a, b, other_a, other_b, corners = call(
        fetch_kernel,
        [(4, NR, NC), rows, rows, rows, rows, (16, 8, NC)],
        [HBM] * 4,
        20 * NZ * NR * NC,
        4 * block,
        [field] * 3 + [wets, dma((CHUNKS, 4))],
        vmem=FETCH_VMEM,
    )(u, v, vi, w)
    from_b = lax.ppermute(b, LAT, SWAP_B)
    from_a = lax.ppermute(a, LAT, SWAP_A)
    inner, to_a, to_b, th = call(
        inner_kernel,
        [(2, NR, NC), (MSG, NC), (MSG, NC), (NZ + 8, NC)],
        [SM] + [VM] * 8,
        40 * NZ * NR * NC,
        4 * block,
    )(thickness, u, v, vi, w, lon, corners, surface, surface_diag)
    msg_b = lax.ppermute(to_b, LON, SWAP_B)
    msg_a = lax.ppermute(to_a, LON, SWAP_A)
    lon2, a2, b2 = call(
        late_kernel, [(2, NR, NC), late, late], [VM] * 4, 20 * NZ * NR * NC, 2 * block
    )(t, w, other_a, other_b)
    msg_a, msg_b, lon2, a2, b2 = lax.optimization_barrier((msg_a, msg_b, lon2, a2, b2))
    wide = (NR, 2 * NC)
    rest, dg, edge, corner, side_a, side_b = call(
        side_kernel,
        [wide, wide, (8, 2 * NC), (128, NC), (LAT_MSG, NC), (LAT_MSG, NC)],
        [VM] * 11,
        10**6,
        10**5,
    )(inner, lon, surface, surface_diag, msg_a, msg_b, other_a, from_a, other_b, from_b, th)
    got_b = lax.ppermute(side_b, LAT, SWAP_B)
    got_a = lax.ppermute(side_a, LAT, SWAP_A)
    (taps,) = call(taps_kernel, [(32, 2 * NC)], [SM], 10**4, 10**4)(precond_kernel)
    def velocity(early, edges, written):
        return call(
            functools.partial(velocity_kernel, early),
            [flat] * 2,
            [VM] * 9 + [HBM] * len(written),
            30 * NZ * NR * NC,
            3 * block,
            [field] * 2
            + [pltpu.VMEM((2, NR, NC), jnp.float32), pltpu.VMEM((4, NZ, NC), jnp.float32), dma((CHUNKS, 2))],
            HBM,
            aliases={9 + i: i for i in range(len(written))},
        )(u, v, vi, w, lon, msg_a, msg_b, *edges, *written)

    u_half, v_half = velocity(True, (from_a, from_b), ())
    got_a, got_b, u_half, v_half = lax.optimization_barrier((got_a, got_b, u_half, v_half))
    vecs, dots = call(
        solve_kernel,
        [(3, NR, NC), (32, 8, NC)],
        [VM] * 8,
        10**6,
        10**5,
        [pltpu.VMEM((3, NR, NC), jnp.float32), dma],
        [HBM, VM],
    )(taps, th, corner, rest, dg, edge, got_a, got_b)
    dots, a2, b2, lon2 = lax.optimization_barrier((dots, a2, b2, lon2))
    from_b2 = lax.ppermute(b2, LAT, SWAP_B)
    from_a2 = lax.ppermute(a2, LAT, SWAP_A)
    lon2_b = lax.ppermute(lon2, LON, SWAP_B)
    lon2_a = lax.ppermute(lon2, LON, SWAP_A)
    dots = lax.all_to_all(dots, ("x", "y", "c"), 0, 0)
    lat = (from_a, from_a2, from_b, from_b2)
    u_new, v_new = velocity(False, (from_a2, from_b2), (u_half, v_half))
    t_new = call(
        tracer_kernel,
        [flat],
        [VM] * 14,
        60 * NZ * NR * NC,
        5 * block,
        [field, pltpu.VMEM((2, NR, NC), jnp.float32), pltpu.VMEM((4, NZ, NC), jnp.float32), dma((CHUNKS, 1))],
        HBM,
    )(t, u, v, w, lon, msg_a, msg_b, lon2, lon2_a, lon2_b, *lat)[0]
    (dots,) = call(relay_kernel, [(8, 1, NC)], [VM], 10**4, 10**4)(dots)
    dots = lax.all_to_all(dots, ("zl", "zh"), 0, 0)
    dots, t_new, u_new, v_new = lax.optimization_barrier((dots, t_new, u_new, v_new))
    (surface_new,) = call(step_kernel, [(NR, NC)], [VM] * 3, 10**5, 10**4)(dots, vecs, surface)
    shape = (NZ, NR, NC)
    return t_new.reshape(shape), u_new.reshape(shape), v_new.reshape(shape), surface_new


def solution(mesh):
    sizes = dict(mesh.shape)
    assert sizes == {"lon": 16, "lat": 16} and tuple(mesh.axis_names) == ("lon", "lat")
    fine = Mesh(mesh.devices.reshape(2, 4, 2, 4, 4), ("zl", "x", "c", "y", "zh"))
    deep = P(None, LAT, LON)
    flat = P(LAT, LON)
    return jax.shard_map(
        local,
        mesh=fine,
        in_specs=(deep,) * 5 + (P(), flat, flat, P()),
        out_specs=(deep, deep, deep, flat),
        check_vma=False,
    )
```

```python
import functools

import jax
import jax.numpy as jnp
from jax import lax
from jax.experimental import pallas as pl
from jax.experimental.pallas import tpu as pltpu
from jax.sharding import Mesh
from jax.sharding import PartitionSpec as P

DT_ADV = 0.25
DT_VISC = 0.2
TAU = 0.05
SHIFTS = (0.3, 1.3)

LON = ("zl", "x", "c")
LAT = ("y", "zh")
NZ, NR, NC = 64, 16, 128
SWAP_A = [(i, i ^ 1) for i in range(16)]
SWAP_B = [(i, (i + 1) % 16 if i % 2 else (i - 1) % 16) for i in range(16)]

VM = pl.BlockSpec(memory_space=pltpu.VMEM)
SM = pl.BlockSpec(memory_space=pltpu.SMEM)
HBM = pl.BlockSpec(memory_space=pltpu.HBM)
FETCH_VMEM = 53.25


def call(kernel, outs, specs, flops, nbytes, scratch=(), place=VM, vmem=4, aliases=None):
    return pl.pallas_call(
        kernel,
        out_shape=[jax.ShapeDtypeStruct(s, jnp.float32) for s in outs],
        in_specs=specs,
        out_specs=place if isinstance(place, list) else [place] * len(outs),
        scratch_shapes=list(scratch),
        input_output_aliases=aliases or {},
        compiler_params=pltpu.CompilerParams(vmem_limit_bytes=int(vmem * 1024 * 1024)),
        cost_estimate=pl.CostEstimate(flops=flops, bytes_accessed=nbytes, transcendentals=0),
    )


def lane_of(shape):
    return lax.broadcasted_iota(jnp.int32, shape, len(shape) - 1)


def row_of(shape):
    return lax.broadcasted_iota(jnp.int32, shape, len(shape) - 2)


def even_lon():
    return lax.axis_index("c") == 0


def even_lat():
    return lax.axis_index("zh") % 2 == 0


def lat_index():
    return lax.axis_index("y") * 4 + lax.axis_index("zh")


def b_exists():
    lat = lat_index()
    return jnp.where(jnp.logical_or(lat == 0, lat == 15), 0.0, 1.0).astype(jnp.float32)


HALF = NZ // 2
CHUNKS = 4


def halves():
    mine = jnp.where(even_lat(), 0, HALF)
    return pl.multiple_of(mine, HALF), pl.multiple_of(HALF - mine, HALF)


def edge_row(ref, north, inwards, first, count):
    if isinstance(north, bool):
        row = NR - 1 - inwards if north else inwards
    else:
        row = jnp.where(north, NR - 1 - inwards, inwards)
    return ref[pl.ds(first * NR + row, count, stride=NR), :].astype(jnp.float32)


def pipeline(copies, body, acc, unroll):
    per = NZ // CHUNKS

    def start(c, carry):
        for copy in copies(c):
            copy.start()
        return carry

    def chunk(c, carry):
        for copy in copies(c):
            copy.wait()
        return lax.fori_loop(0, per, lambda i, x: body(c * per + i, x), carry, unroll=unroll)

    lax.fori_loop(0, CHUNKS, start, 0)
    return lax.fori_loop(0, CHUNKS, chunk, acc)


def chunk_copies(pairs, sems):
    span = NZ * NR // CHUNKS

    def copies(c):
        at = pl.ds(pl.multiple_of(c * span, span), span)
        return [
            pltpu.make_async_copy(src.at[at], dst.at[at], sems.at[c, i])
            for i, (src, dst) in enumerate(pairs)
        ]

    return copies


def level(k):
    return pl.ds(pl.multiple_of(k * NR, NR), NR)


def squeeze(rows, shift):
    group = lane_of((8, NC)) // 32
    out = None
    for g in range(4):
        part = pltpu.roll(rows[8 * g : 8 * g + 8], (shift + 32 * g) % NC, 1)
        out = part if g == 0 else jnp.where(group == g, part, out)
    return out


def fetch_kernel(u, v, vi, land, lon_out, a_out, b_out, other_a, other_b, corners, uo, vo, vio, lo, sems):
    pair = lane_of((NR, NC)) // 2

    def body(k, acc):
        at = level(k)
        values = (uo[at, :], vo[at, :], vio[at, :], lo[at, :].astype(jnp.float32))
        mine = pair == k
        return tuple(
            jnp.where(mine, pltpu.roll(x, 2 * k + 1, 1), old) for x, old in zip(values, acc)
        )

    copies = chunk_copies(((u, uo), (v, vo), (vi, vio), (land, lo)), sems)
    acc = pipeline(copies, body, (jnp.zeros((NR, NC), jnp.float32),) * 4, 8)
    for i in range(4):
        lon_out[i] = acc[i]
    even = even_lat()
    mine, theirs = halves()
    for north, first, rest in ((even, a_out, other_a), (jnp.logical_not(even), b_out, other_b)):
        for i, ref in enumerate((uo, vo, vio, lo)):
            first[i] = edge_row(ref, north, 0, mine, HALF)
            rest[i] = edge_row(ref, north, 0, theirs, HALF)
    for n, ref in enumerate((a_out, other_a, b_out, other_b)):
        for i in range(4):
            corners[4 * n + i] = squeeze(ref[i], 16)


AT_CORNER, AT_FIELDS, MSG = 32, 96, 112


def put_side_by_side(first, second, step, high):
    left = lane_of(first.shape) % (2 * step) < step
    high_pair = jnp.where(left, first, pltpu.roll(second, step, 1))
    low_pair = jnp.where(left, pltpu.roll(first, NC - step, 1), second)
    return jnp.where(high, high_pair, low_pair)


def take_across(east, west, which, step, east_first):
    left = lane_of(east.shape) % (2 * step) < step
    place = 0 if east_first else 1
    east = east if which == place else pltpu.roll(east, step if which < place else NC - step, 1)
    west = west if which != place else pltpu.roll(west, NC - step if which else step, 1)
    return jnp.where(left, east, west) if east_first else jnp.where(left, west, east)


def inner_kernel(thick, u, v, vi, w, lon, corners, sf, dg, out, msg_a, msg_b, th_out):
    lane, row = lane_of((NR, NC)), row_of((NR, NC))
    pair = lane[:1] // 2
    up = lambda x: pltpu.roll(x, NC - 1, 1)
    north_of = lambda x: pltpu.roll(x, NR - 1, 0)

    def body(k, acc):
        at = level(k)
        wet, uu, vv, visc = w[at, :].astype(jnp.float32), u[at, :], v[at, :], vi[at, :]
        th = jnp.full((1, NC), thick[k], jnp.float32)
        th_out[pl.ds(k, 1), :] = th
        own = wet * th
        half = 0.5 * own
        east = (visc + up(visc)) * (half * up(wet))
        north = (visc + north_of(visc)) * (half * north_of(wet))
        return (
            acc[0] + own * uu,
            acc[1] + east * (up(uu) - uu),
            acc[2] + north * (north_of(uu) - uu),
            acc[3] + own * vv,
            acc[4] + east * (up(vv) - vv),
            acc[5] + north * (north_of(vv) - vv),
            jnp.where(pair == k, th, acc[6]),
        )

    zero = jnp.zeros((NR, NC), jnp.float32)
    acc = lax.fori_loop(0, NZ, body, (zero,) * 6 + (zero[:1],), unroll=16)
    th_out[NZ:, :] = jnp.broadcast_to(acc[6], (8, NC))
    for i in range(2):
        east = jnp.where(lane == NC - 1, 0.0, acc[3 * i + 1])
        north = jnp.where(row == NR - 1, 0.0, acc[3 * i + 2])
        out[i] = acc[3 * i] + DT_VISC * (
            east - pltpu.roll(east, 1, 1) + north - pltpu.roll(north, 1, 0)
        )
    fields = (out[0], out[1], sf[...], dg[...])
    for msg, high in ((msg_a, even_lon()), (msg_b, jnp.logical_not(even_lon()))):
        for i in range(2):
            msg[NR * i : NR * (i + 1), :] = put_side_by_side(lon[2 * i], lon[2 * i + 1], 1, high)
        for n in range(2):
            for i in range(4):
                at = AT_CORNER + 32 * n + 8 * i
                first, second = corners[8 * n + i], corners[8 * n + 4 + i]
                msg[at : at + 8, :] = put_side_by_side(first, second, 16, high)
        line = None
        for f, x in enumerate(fields):
            part = jnp.where(high, pltpu.roll(x, 16 * (f + 1) % NC, 1), pltpu.roll(x, 16 * f, 1) if f else x)
            line = part if f == 0 else jnp.where(lane // 16 == f, part, line)
        msg[AT_FIELDS:, :] = line


def late_kernel(t, w, other_a, other_b, lon_out, a_out, b_out):
    lane = lane_of((NR, NC))
    pair = lane // 2
    half_lane = lane < NC // 2

    def body(k, acc):
        at = level(k)
        first = t[at, :] * w[at, :].astype(jnp.float32)
        inner = jnp.where(half_lane, pltpu.roll(first, NC - 1, 1), pltpu.roll(first, 1, 1))
        mine = pair == k
        return tuple(
            jnp.where(mine, pltpu.roll(x, 2 * k + 1, 1), old)
            for x, old in zip((first, 7.0 * first - inner), acc)
        )

    acc = lax.fori_loop(0, NZ, body, (jnp.zeros((NR, NC), jnp.float32),) * 2, unroll=8)
    lon_out[0] = acc[0]
    lon_out[1] = acc[1]
    even = even_lat()
    for north, src, dst in ((even, other_a, a_out), (jnp.logical_not(even), other_b, b_out)):
        dst[:4] = src[...]
        for i in range(2):
            near, inner = (
                edge_row(t, north, n, i * HALF, HALF) * edge_row(w, north, n, i * HALF, HALF)
                for n in range(2)
            )
            dst[4 + i] = near
            dst[6 + i] = 7.0 * near - inner


def taps_kernel(pc, out):
    for i in range(25):
        out[i : i + 1, :] = jnp.full((1, 2 * NC), pc[i // 5, i % 5], jnp.float32)


def lon_sides(first, second):
    even = even_lon()
    return jnp.where(even, first, second), jnp.where(even, second, first)


def beyond(from_a, from_b):
    east, west = lon_sides(from_a, from_b)
    is_east = lane_of((NR, NC)) % 2 == 0
    return jnp.where(is_east, pltpu.roll(east, NC - 1, 1), pltpu.roll(west, 1, 1))


def edge_across(msg_a, msg_b, i):
    at = slice(NR * (i // 2), NR * (i // 2 + 1))
    return take_across(*lon_sides(msg_a[at, :], msg_b[at, :]), i % 2, 1, True)


def face_in(own, other):
    face = 0.5 * (own[2] + other[2]) * (own[3] * other[3])
    return face * (other[0] - own[0]), face * (other[1] - own[1])


LAT_MSG = 96


def side_kernel(
    inner, lon, sf_own, dg_own, msg_a, msg_b, a2, from_a, b2, from_b, th,
    rest_out, diag_out, edge_out, corner_out, a_out, b_out,
):
    lane = lane_of((NR, NC))
    is_east = lane % 2 == 0
    packed = [lon[i] for i in range(4)]
    other = [edge_across(msg_a, msg_b, i) for i in range(4)]
    far_east, far_west = lon_sides(msg_a[AT_FIELDS:, :], msg_b[AT_FIELDS:, :])

    def widen(own, f):
        east = pltpu.roll(far_east, (NC - 16 * f) % NC, 1) if f else far_east
        west = pltpu.roll(far_west, (NC - 16 - 16 * f) % NC, 1)
        halo = jnp.where(lane < 16, east, jnp.where(lane >= NC - 16, west, 0.0))
        return jnp.concatenate([own, halo], axis=1)

    wide_lane = lane_of((NR, 2 * NC))
    te, tn = widen(inner[0], 0), widen(inner[1], 1)
    sf, dg = widen(sf_own[...], 2), widen(dg_own[...], 3)
    add = []
    for grad in face_in(packed, other):
        grad = grad * (DT_VISC * th[NZ : NZ + 1, :])
        east = jnp.sum(jnp.where(is_east, grad, 0.0), axis=1, keepdims=True)
        west = jnp.sum(jnp.where(is_east, 0.0, grad), axis=1, keepdims=True)
        here = jnp.where(wide_lane == NC - 1, east, 0.0) + jnp.where(wide_lane == 0, west, 0.0)
        there = jnp.where(wide_lane == NC, east, 0.0) + jnp.where(wide_lane == 2 * NC - 1, west, 0.0)
        add.append(here - there)
    te = te + add[0]
    tn = tn + add[1]
    _, theirs = halves()
    weight = DT_VISC * th[pl.ds(theirs, HALF), :]
    lat_a = face_in([a2[i] for i in range(4)], [from_a[i] for i in range(4)])
    weight_b = weight * b_exists()
    lat_b = face_in([b2[i] for i in range(4)], [from_b[i] for i in range(4)])
    faces = [jnp.sum(x * weight, axis=0, keepdims=True) for x in lat_a]
    faces += [jnp.sum(x * weight_b, axis=0, keepdims=True) for x in lat_b]
    faces = [jnp.concatenate([x, jnp.zeros((1, NC), jnp.float32)], axis=1) for x in faces]
    for n in range(2):
        for i in range(4):
            at = AT_CORNER + 32 * n + 8 * i
            sides = lon_sides(msg_a[at : at + 8, :], msg_b[at : at + 8, :])
            for h in range(2):
                to = 64 * n + 32 * h + 8 * i
                corner_out[to : to + 8, :] = take_across(*sides, h, 16, False)
    row = row_of((NR, 2 * NC))
    even = even_lat()
    north_u, north_v = (jnp.where(even, faces[i], faces[i + 2]) for i in range(2))
    south_u, south_v = (jnp.where(even, faces[i + 2], faces[i]) for i in range(2))
    at_north, at_south = row == NR - 1, row == 0
    te = te + jnp.where(at_north, north_u, 0.0) + jnp.where(at_south, south_u, 0.0)
    tn = tn + jnp.where(at_north, north_v, 0.0) + jnp.where(at_south, south_v, 0.0)
    east = lambda x: pltpu.roll(x, 2 * NC - 1, 1)
    west = lambda x: pltpu.roll(x, 1, 1)
    north = lambda x: jnp.where(at_north, 0.0, pltpu.roll(x, NR - 1, 0))
    south = lambda x: jnp.where(at_south, 0.0, pltpu.roll(x, 1, 0))
    across = lambda fu, fv: TAU * (fu - west(fu) + fv)
    rest = sf - TAU * (te - west(te) + tn - south(tn))
    rest = rest - ((4.0 + dg) * sf - (east(sf) + west(sf) + north(sf) + south(sf)))
    rest = rest - jnp.where(at_south, TAU * south_v, 0.0)
    rest_out[...] = rest
    diag_out[...] = dg
    first = TAU * tn[NR - 1 :] + sf[NR - 1 :] + across(north_u, north_v)
    second = -TAU * north_v
    to_south = sf[:1] + across(south_u, south_v)
    zero = jnp.zeros((5, 2 * NC), jnp.float32)
    edge_out[...] = jnp.concatenate([first, second, to_south, zero], axis=0)
    msg_north = jnp.concatenate([rest[8:], dg[11:], first, second, zero[:1]], axis=0)
    msg_south = jnp.concatenate([rest[:9], dg[:6], to_south], axis=0)
    for n, (out, lines) in enumerate(
        (
            (a_out, jnp.where(even, msg_north, msg_south)),
            (b_out, jnp.where(even, msg_south, msg_north)),
        )
    ):
        out[:NR, :] = lines[:, :NC]
        out[NR : 2 * NR, :] = lines[:, NC:]
        out[2 * NR :, :] = corner_out[64 * n : 64 * (n + 1), :]


def solve_kernel(pc, th, corner, rest, dg, edge, from_a, from_b, v_hbm, dots_out, v_out, sem):
    rows, wide = 2 * NR, 2 * NC
    even = even_lat()
    exists = b_exists()
    msg_a = jnp.concatenate([from_a[:NR, :], from_a[NR : 2 * NR, :]], axis=1)
    msg_b = jnp.concatenate([from_b[:NR, :], from_b[NR : 2 * NR, :]], axis=1) * exists
    north = jnp.where(even, msg_a, msg_b)
    south = jnp.where(even, msg_b, msg_a)
    zeros = lambda n: jnp.zeros((n, wide), jnp.float32)
    row = row_of((rows + 8, wide))
    lat = lat_index()
    low = jnp.where(lat == 0, 8, 0)
    high = jnp.where(lat == 15, 8 + NR, rows + 8)
    inside = jnp.where(jnp.logical_and(row >= low, row < high), 1.0, 0.0).astype(jnp.float32)
    below = jnp.concatenate([south[:7], south[7:8] + edge[2:3]], axis=0)
    above = jnp.concatenate(
        [north[:1] + edge[0:1], north[1:2] + edge[1:2], north[2:9], zeros(7)], axis=0
    )
    own = rest[...] + jnp.concatenate([south[13:15], zeros(13), north[15:]], axis=0)
    res = jnp.concatenate([below, own, above], axis=0)
    group = lane_of((8, NC)) // 32
    weights = []
    for first in halves():
        line = None
        for g in range(4):
            part = th[pl.ds(pl.multiple_of(first + 8 * g, 8), 8), :]
            line = part if g == 0 else jnp.where(group == g, part, line)
        weights.append(DT_VISC * line)
    sums = []
    for n, got in enumerate((from_a, from_b)):
        total = None
        for h in range(2):
            here = [corner[64 * n + 32 * h + 8 * i : 64 * n + 32 * h + 8 * (i + 1), :] for i in range(4)]
            at = 2 * NR + 32 * (1 - h)
            there = [got[at + 8 * i : at + 8 * (i + 1), :] for i in range(4)]
            part = [x * weights[h] for x in face_in(here, there)]
            total = part if h == 0 else [x + y for x, y in zip(total, part)]
        for x in total:
            x = jnp.sum(x, axis=0, keepdims=True)
            x = x + pltpu.roll(x, 32, 1)
            x = x + pltpu.roll(x, 64, 1)
            edge_lane = lane_of((1, NC))
            near = jnp.logical_or(edge_lane < 16, edge_lane >= NC - 16)
            x = jnp.where(near, pltpu.roll(x, NC - 16, 1), 0.0)
            sums.append(jnp.concatenate([jnp.zeros((1, NC), jnp.float32), x], axis=1))
    sums[2] = sums[2] * exists
    sums[3] = sums[3] * exists
    north_u, north_v = (jnp.where(even, sums[i], sums[i + 2]) for i in range(2))
    south_u, south_v = (jnp.where(even, sums[i + 2], sums[i]) for i in range(2))
    across = lambda fu, fv: TAU * (fu - pltpu.roll(fu, 1, 1) + fv)
    for at, line in (
        (7 + NR, -across(north_u, north_v)),
        (8 + NR, across(north_u, north_v) + TAU * north_v),
        (9 + NR, -TAU * north_v),
        (7, across(south_u, south_v)),
        (8, -across(south_u, south_v) - TAU * south_v),
        (9, TAU * south_v),
    ):
        res = res + jnp.where(row == at, line, 0.0)
    res = res * inside
    inside = inside[:rows]
    diag = 4.0 + jnp.concatenate([zeros(3), south[8:13], dg[...], north[9:15], zeros(2)], axis=0)

    def lon_shift(x, n):
        return x if n == 0 else pltpu.roll(x, (-n) % wide, 1)

    def lat_shift(x, n):
        return x if n == 0 else pltpu.roll(x, (-n) % x.shape[0], 0)

    def operate(x):
        near = lon_shift(x, 1) + lon_shift(x, -1) + lat_shift(x, 1) + lat_shift(x, -1)
        return diag * x - near

    def tap(a, b):
        at = 5 * (a + 2) + b + 2
        return pc[at : at + 1, :]

    def precondition(x):
        moved = [lon_shift(x, b) for b in range(-2, 3)]
        total = None
        for a in range(-2, 3):
            line = tap(a, -2) * moved[0]
            for b in range(1, 5):
                line = line + tap(a, b - 2) * moved[b]
            line = lat_shift(line, a)[:rows]
            total = line if total is None else total + line
        return total * inside

    scale = 1.0 / (5.0 * tap(0, 0))
    p0 = res
    v0 = precondition(p0)
    a0 = operate(v0)
    p1 = (a0 * scale - SHIFTS[0] * p0[:rows]) * inside
    v1 = precondition(p1)
    a1 = operate(v1)
    p2 = (a1 * scale - SHIFTS[1] * p1) * inside
    v2 = precondition(p2)
    mine = lambda x: x[8 : 8 + NR, :NC]
    half_a2 = mine(diag * v2 - 2.0 * (lon_shift(v2, 1) + lat_shift(v2, 1)))
    v0, v1, v2, a0, a1, r = (mine(x) for x in (v0, v1, v2, a0, a1, p0))
    v_out[0] = v0
    v_out[1] = v1
    v_out[2] = v2
    pairs = ((v0, a0), (v0, a1), (v2, a0), (v1, a1), (v2, a1), (v2, half_a2), (v0, r), (v1, r), (v2, r))
    copy = pltpu.make_async_copy(v_out, v_hbm, sem)
    copy.start()
    lane = lane_of((1, NC))
    line = jnp.zeros((1, NC), jnp.float32)
    for i, (x, y) in enumerate(pairs):
        total = jnp.sum(jnp.sum(x * y, axis=0, keepdims=True), axis=1, keepdims=True)
        line = line + jnp.where(lane == i, total, 0.0)
    dots_out[...] = jnp.broadcast_to(line[None], dots_out.shape)
    copy.wait()


def relay_kernel(got, out):
    out[...] = jnp.broadcast_to(jnp.sum(got[...], axis=0, keepdims=True)[:, :1], out.shape)


def step_kernel(got, v, sf, out):
    line = jnp.sum(got[...], axis=0)
    lane = lane_of((1, NC))
    h00, h01, h02, h11, h12, h22, g0, g1, g2 = (
        jnp.sum(jnp.where(lane == i, line, 0.0), axis=1, keepdims=True) for i in range(9)
    )
    l1 = h01 / h00
    l2 = h02 / h00
    d1 = h11 - l1 * h01
    e12 = h12 - l1 * h02
    l3 = e12 / d1
    d2 = h22 - l2 * h02 - l3 * e12
    y1 = g1 - l1 * g0
    y2 = g2 - l2 * g0 - l3 * y1
    c2 = y2 / d2
    c1 = y1 / d1 - l3 * c2
    c0 = g0 / h00 - l1 * c1 - l2 * c2
    out[...] = sf[...] + c0 * v[0] + c1 * v[1] + c2 * v[2]


def row_masks():
    lane, row = lane_of((NR, NC)), row_of((NR, NC))
    return lane == NC - 1, lane == 0, row == NR - 1, row == 0


def spread_of(packed, lines):
    at_east, at_west, at_north, at_south = row_masks()

    def spread(k, flux_e, flux_n, i):
        side = pltpu.roll(packed[i], NC - 1 - 2 * k, 1)
        north = jnp.broadcast_to(lines[2 * i, pl.ds(k, 1), :], (NR, NC))
        south = jnp.broadcast_to(lines[2 * i + 1, pl.ds(k, 1), :], (NR, NC))
        flux_e = jnp.where(at_east, side, flux_e)
        flux_n = jnp.where(at_north, north, flux_n)
        back_e = jnp.where(at_west, side, pltpu.roll(flux_e, 1, 1))
        back_n = jnp.where(at_south, south, pltpu.roll(flux_n, 1, 0))
        return flux_e - back_e + (flux_n - back_n)

    return spread


def write_out(body, pairs, sems, unroll, first=0, count=NZ):
    per = NZ // CHUNKS
    all_copies = chunk_copies(pairs, sems)
    copies = lambda c: all_copies(first // per + c)

    def chunk(c, carry):
        lax.fori_loop(0, per, lambda i, x: body(first + c * per + i, x), 0, unroll=unroll)
        for copy in copies(c):
            copy.start()
        return carry

    def finish(c, carry):
        for copy in copies(c):
            copy.wait()
        return carry

    lax.fori_loop(0, count // per, chunk, 0)
    return lambda: lax.fori_loop(0, count // per, finish, 0)


def velocity_kernel(early, u, v, vi, w, lon, msg_a, msg_b, from_a, from_b, *rest):
    u_hbm, v_hbm, u_out, v_out, packed, lines, sems = rest[0 if early else 2 :]
    is_east = lane_of((NR, NC)) % 2 == 0
    own = [lon[i] for i in range(4)]
    other = [edge_across(msg_a, msg_b, i) for i in range(4)]
    for i, grad in enumerate(face_in(own, other)):
        packed[i] = DT_VISC * jnp.where(is_east, grad, -grad)
    even = even_lat()
    exists = b_exists()
    mine, theirs = halves()
    first = theirs if early else mine
    at = pl.ds(first, HALF)
    for side in range(2):
        use_a = even if side == 0 else jnp.logical_not(even)
        here = [edge_row(ref, side == 0, 0, first, HALF) for ref in (u, v, vi, w)]
        there = [jnp.where(use_a, from_a[i], from_b[i] * exists) for i in range(4)]
        sign = DT_VISC if side == 0 else -DT_VISC
        for i, grad in enumerate(face_in(here, there)):
            lines[2 * i + side, at, :] = sign * grad
    spread = spread_of(packed, lines)
    lon_up = lambda x: pltpu.roll(x, NC - 1, 1)
    lat_up = lambda x: pltpu.roll(x, NR - 1, 0)

    def body(k, carry):
        at = level(k)
        uu, vv, visc = u[at, :], v[at, :], vi[at, :]
        wet = w[at, :].astype(jnp.float32)
        half = wet * (0.5 * DT_VISC)
        face_e = (visc + lon_up(visc)) * (half * lon_up(wet))
        face_n = (visc + lat_up(visc)) * (half * lat_up(wet))
        u_out[at, :] = wet * (uu + spread(k, face_e * (lon_up(uu) - uu), face_n * (lat_up(uu) - uu), 0))
        v_out[at, :] = wet * (vv + spread(k, face_e * (lon_up(vv) - vv), face_n * (lat_up(vv) - vv), 1))
        return carry

    finish = write_out(body, ((u_out, u_hbm), (v_out, v_hbm)), sems, 8, first, HALF)
    if not early:
        return finish
    finish()


def tracer_kernel(
    t, u, v, w, lon, msg_a, msg_b, lon2, lon2_a, lon2_b, from_a, from_a2, from_b, from_b2,
    t_hbm, t_out, packed, lines, sems,
):
    is_east = lane_of((NR, NC)) % 2 == 0
    by = DT_ADV / 12.0
    packed[1] = beyond(lon2_a[0], lon2_b[0])
    far = lon2[1] + beyond(lon2_a[1], lon2_b[1])
    speed = jnp.where(is_east, lon[0], edge_across(msg_a, msg_b, 0))
    wets = edge_across(msg_a, msg_b, 3) * lon[3]
    packed[0] = speed * far * (by * wets)
    even = even_lat()
    exists = b_exists()
    mine, theirs = halves()
    for first, there_a, there_b in ((mine, from_a2, from_b2), (theirs, from_a, from_b)):
        at = pl.ds(first, HALF)
        part = first // HALF
        for side in range(2):
            north = side == 0
            use_a = even if north else jnp.logical_not(even)
            wet_here = edge_row(w, north, 0, first, HALF)
            wet_there = jnp.where(use_a, there_a[3], there_b[3] * exists)
            near = edge_row(t, north, 0, first, HALF) * wet_here
            inner = edge_row(t, north, 1, first, HALF) * edge_row(w, north, 1, first, HALF)
            far = jnp.where(use_a, from_a2[6 + part], from_b2[6 + part]) + (7.0 * near - inner)
            if north:
                speed = edge_row(v, True, 0, first, HALF)
            else:
                speed = jnp.where(use_a, there_a[1], there_b[1])
            lines[side, at, :] = speed * far * (by * wet_here * wet_there)
            lines[2 + side, at, :] = jnp.where(use_a, from_a2[4 + part], from_b2[4 + part] * exists)
    spread = spread_of(packed, lines)
    at_east, at_west, at_north, at_south = row_masks()
    lon_up = lambda x: pltpu.roll(x, NC - 1, 1)
    lat_up = lambda x: pltpu.roll(x, NR - 1, 0)

    def body(k, carry):
        at = level(k)
        tt = t[at, :]
        wet = w[at, :].astype(jnp.float32)
        wt = tt * wet
        side = pltpu.roll(packed[1], NC - 1 - 2 * k, 1)
        north = jnp.broadcast_to(lines[2, pl.ds(k, 1), :], (NR, NC))
        south = jnp.broadcast_to(lines[3, pl.ds(k, 1), :], (NR, NC))
        t_e = jnp.where(at_east, side, lon_up(wt))
        t_w = jnp.where(at_west, side, pltpu.roll(wt, 1, 1))
        t_n = jnp.where(at_north, north, lat_up(wt))
        t_s = jnp.where(at_south, south, pltpu.roll(wt, 1, 0))
        part = by * wet
        flux_e = u[at, :] * (7.0 * (wt + t_e) - (t_w + lon_up(t_e))) * (part * lon_up(wet))
        flux_n = v[at, :] * (7.0 * (wt + t_n) - (t_s + lat_up(t_n))) * (part * lat_up(wet))
        t_out[at, :] = wet * (tt - spread(k, flux_e, flux_n, 0))
        return carry

    return write_out(body, ((t_out, t_hbm),), sems, 8)


def last_kernel(
    t, u, v, vi, w, lon, msg_a, msg_b, lon2, lon2_a, lon2_b, from_a, from_a2, from_b, from_b2, u_half, v_half,
    u_hbm, v_hbm, t_hbm, u_out, v_out, packed, lines, sems, t_out, t_packed, t_lines, t_sems,
):
    finish_velocity = velocity_kernel(
        False, u, v, vi, w, lon, msg_a, msg_b, from_a2, from_b2, u_half, v_half,
        u_hbm, v_hbm, u_out, v_out, packed, lines, sems,
    )
    finish_tracer = tracer_kernel(
        t, u, v, w, lon, msg_a, msg_b, lon2, lon2_a, lon2_b, from_a, from_a2, from_b, from_b2,
        t_hbm, t_out, t_packed, t_lines, t_sems,
    )
    finish_velocity()
    finish_tracer()


def local(tracer, east_vel, north_vel, viscosity, land_sea, thickness, surface, surface_diag, precond_kernel):
    flat = (NZ * NR, NC)
    u, v, vi, w, t = (x.reshape(flat) for x in (east_vel, north_vel, viscosity, land_sea, tracer))
    block = NZ * NR * NC * 4
    field = pltpu.VMEM(flat, jnp.float32)
    wets = pltpu.VMEM(flat, jnp.int32)
    dma = pltpu.SemaphoreType.DMA
    rows = (4, HALF, NC)
    late = (8, HALF, NC)
    lon, a, b, other_a, other_b, corners = call(
        fetch_kernel,
        [(4, NR, NC), rows, rows, rows, rows, (16, 8, NC)],
        [HBM] * 4,
        20 * NZ * NR * NC,
        4 * block,
        [field] * 3 + [wets, dma((CHUNKS, 4))],
        vmem=FETCH_VMEM,
    )(u, v, vi, w)
    from_b = lax.ppermute(b, LAT, SWAP_B)
    from_a = lax.ppermute(a, LAT, SWAP_A)
    inner, to_a, to_b, th = call(
        inner_kernel,
        [(2, NR, NC), (MSG, NC), (MSG, NC), (NZ + 8, NC)],
        [SM] + [VM] * 8,
        40 * NZ * NR * NC,
        4 * block,
    )(thickness, u, v, vi, w, lon, corners, surface, surface_diag)
    msg_b = lax.ppermute(to_b, LON, SWAP_B)
    msg_a = lax.ppermute(to_a, LON, SWAP_A)
    lon2, a2, b2 = call(
        late_kernel, [(2, NR, NC), late, late], [VM] * 4, 20 * NZ * NR * NC, 2 * block
    )(t, w, other_a, other_b)
    msg_a, msg_b, lon2, a2, b2 = lax.optimization_barrier((msg_a, msg_b, lon2, a2, b2))
    wide = (NR, 2 * NC)
    rest, dg, edge, corner, side_a, side_b = call(
        side_kernel,
        [wide, wide, (8, 2 * NC), (128, NC), (LAT_MSG, NC), (LAT_MSG, NC)],
        [VM] * 11,
        10**6,
        10**5,
    )(inner, lon, surface, surface_diag, msg_a, msg_b, other_a, from_a, other_b, from_b, th)
    got_b = lax.ppermute(side_b, LAT, SWAP_B)
    got_a = lax.ppermute(side_a, LAT, SWAP_A)
    (taps,) = call(taps_kernel, [(32, 2 * NC)], [SM], 10**4, 10**4)(precond_kernel)
    def velocity(early, edges, written):
        return call(
            functools.partial(velocity_kernel, early),
            [flat] * 2,
            [VM] * 9 + [HBM] * len(written),
            30 * NZ * NR * NC,
            3 * block,
            [field] * 2
            + [pltpu.VMEM((2, NR, NC), jnp.float32), pltpu.VMEM((4, NZ, NC), jnp.float32), dma((CHUNKS, 2))],
            HBM,
            aliases={9 + i: i for i in range(len(written))},
        )(u, v, vi, w, lon, msg_a, msg_b, *edges, *written)

    u_half, v_half = velocity(True, (from_a, from_b), ())
    got_a, got_b, u_half, v_half = lax.optimization_barrier((got_a, got_b, u_half, v_half))
    vecs, dots = call(
        solve_kernel,
        [(3, NR, NC), (32, 8, NC)],
        [VM] * 8,
        10**6,
        10**5,
        [pltpu.VMEM((3, NR, NC), jnp.float32), dma],
        [HBM, VM],
    )(taps, th, corner, rest, dg, edge, got_a, got_b)
    dots, a2, b2, lon2 = lax.optimization_barrier((dots, a2, b2, lon2))
    from_b2 = lax.ppermute(b2, LAT, SWAP_B)
    from_a2 = lax.ppermute(a2, LAT, SWAP_A)
    lon2_b = lax.ppermute(lon2, LON, SWAP_B)
    lon2_a = lax.ppermute(lon2, LON, SWAP_A)
    dots = lax.all_to_all(dots, ("x", "y", "c"), 0, 0)
    small = [pltpu.VMEM((2, NR, NC), jnp.float32), pltpu.VMEM((4, NZ, NC), jnp.float32)]
    u_new, v_new, t_new = call(
        last_kernel,
        [flat] * 3,
        [VM] * 15 + [HBM] * 2,
        90 * NZ * NR * NC,
        7 * block,
        [field] * 2 + small + [dma((CHUNKS, 2)), field] + small + [dma((CHUNKS, 1))],
        HBM,
        aliases={15: 0, 16: 1},
    )(
        t, u, v, vi, w, lon, msg_a, msg_b, lon2, lon2_a, lon2_b,
        from_a, from_a2, from_b, from_b2, u_half, v_half,
    )
    (dots,) = call(relay_kernel, [(8, 1, NC)], [VM], 10**4, 10**4)(dots)
    dots = lax.all_to_all(dots, ("zl", "zh"), 0, 0)
    dots, t_new, u_new, v_new = lax.optimization_barrier((dots, t_new, u_new, v_new))
    (surface_new,) = call(step_kernel, [(NR, NC)], [VM] * 3, 10**5, 10**4)(dots, vecs, surface)
    shape = (NZ, NR, NC)
    return t_new.reshape(shape), u_new.reshape(shape), v_new.reshape(shape), surface_new


def solution(mesh):
    sizes = dict(mesh.shape)
    assert sizes == {"lon": 16, "lat": 16} and tuple(mesh.axis_names) == ("lon", "lat")
    fine = Mesh(mesh.devices.reshape(2, 4, 2, 4, 4), ("zl", "x", "c", "y", "zh"))
    deep = P(None, LAT, LON)
    flat = P(LAT, LON)
    return jax.shard_map(
        local,
        mesh=fine,
        in_specs=(deep,) * 5 + (P(), flat, flat, P()),
        out_specs=(deep, deep, deep, flat),
        check_vma=False,
    )
```
